32 devices in a mesh: scen: 2 (over x), grid: 16 (over z, y, core).
Axes of the slice: x: 2, y: 2, z: 4, core: 2. Of those that a mesh axis runs over, the one named last changes fastest.
Arguments:
- value_next: float32 [256, 64, 1024], P('grid', 'scen'), may hold values from -8 to 8
- scenario_ids: int32 [2], P('scen'), may hold values from 0 to 11
- inflow_table: int32 [12, 3], replicated, may hold values from 0 to 8, as said below
- release_shifts: int32 [16, 3], replicated, may hold values from 0 to 8, as said below
- price: float32 [3], replicated, may hold values from 0.5 to 4
Outputs:
- value_now: float32 [256, 64, 1024], P('grid', 'scen')
The draws below stay inside these ranges and needn't reach their ends.
Inputs may be any that keep to these rules, and one draw needn't show every extreme that they name: `inflow_table`: inflows lie in 0 to 8; each draw holds a 0 and an 8. `release_shifts`: releases lie in 0 to 8; one decision releases 8 from every reservoir and one releases nothing.
All inputs are finite; a program needn't handle non-finite values.
Results may differ from the reference program's by a relative error of at most 0.0003.
Values sent between devices are 32-bit elements; how exact they have to be, the bound alone decides.
No kernel may reach another device: no remote copies, remote signals or barrier semaphores. Data moves between devices by JAX's collectives and lax.ppermute only.
A program may use at most 128 MiB of HBM per device.

```python
import math
import jax
import jax.numpy as jnp
from jax import lax

H = 8
S2 = 1024
S3 = 64
RELEASES = 16
NINFLOW = 12
S1 = 256
SCENARIOS = 2


def draw_inflow_table(key, part):
    table = jax.random.randint(jax.random.fold_in(key, 11), (NINFLOW, 3), 0, H + 1)
    spots = jax.random.randint(jax.random.fold_in(key, 12), (2,), 0, NINFLOW * 3)
    flat = table.reshape(-1)
    flat = flat.at[spots[0]].set(H)
    flat = flat.at[(spots[0] + 1 + spots[1] % (NINFLOW * 3 - 1)) % (NINFLOW * 3)].set(0)
    return flat.reshape(NINFLOW, 3).astype(jnp.int32)


def draw_release_shifts(key, part):
    table = jax.random.randint(jax.random.fold_in(key, 21), (RELEASES, 3), 0, H + 1)
    order = jax.random.permutation(jax.random.fold_in(key, 22), RELEASES)
    table = table.at[order[0]].set(jnp.full((3,), H, jnp.int32))
    table = table.at[order[1]].set(jnp.zeros((3,), jnp.int32))
    return table.astype(jnp.int32)


def block_levels(stream_key, dims, shards, low, high):
    level = 1.0
    for axis_at, shards_of in shards:
        draws = jax.random.uniform(jax.random.fold_in(jax.random.fold_in(stream_key, 6), axis_at), (shards_of,), jnp.float32, low / len(shards), high / len(shards))
        level = level * jnp.repeat(jnp.exp(draws), dims[axis_at] // shards_of).reshape((-1,) + (1,) * (len(dims) - 1 - axis_at))
    return level


def normal_values(own_key, extent, width, limit, shards=(), kind=jnp.bfloat16):
    values = jax.random.normal(own_key, extent, jnp.float32) * width
    if len(shards) > 0:
        values = block_levels(own_key, extent, shards, -0.22, 0.18) * values
    return jnp.clip(values, min=-limit, max=limit).astype(kind)


def setup_inputs(seed: int = 0) -> dict:
    seeds = jax.random.split(jax.random.key(seed), 6)
    return {
        "value_next": normal_values(seeds[0], (S1, S3, S2), 2.0, 8.0, ((0, 16), (1, 2)), jnp.float32),
        "scenario_ids": jax.random.randint(seeds[1], (SCENARIOS,), 0, NINFLOW).astype(jnp.int32),
        "inflow_table": draw_inflow_table(jax.random.fold_in(seeds[5], 71), 0),
        "release_shifts": draw_release_shifts(jax.random.fold_in(seeds[5], 71), 0),
        "price": jnp.clip(jnp.exp(jax.random.uniform(seeds[4], (3,), jnp.float32, math.log(0.5), math.log(4.0))), 0.5, 4.0),
    }


softness = 0.5


def reference(value_next, scenario_ids, inflow_table, release_shifts, price):
    wide_pad = 2 * H
    extended = jnp.pad(value_next, ((H, H), (wide_pad, wide_pad), (wide_pad, wide_pad)), mode="edge")
    height_first = ((jnp.arange(S1) + 1).astype(jnp.float32) / float(S1)).reshape(S1, 1, 1)
    height_third = ((jnp.arange(S3) + 1).astype(jnp.float32) / float(S3)).reshape(1, S3, 1)
    height_second = ((jnp.arange(S2) + 1).astype(jnp.float32) / float(S2)).reshape(1, 1, S2)

    def scenario(running_total, table_row):
        inflow = inflow_table[table_row]

        def add_release(release_index, running):
            release = release_shifts[release_index]
            first_index = (H + inflow[0] - release[0]).astype(jnp.int32)
            third_index = (wide_pad + inflow[2] + release[1] - release[2]).astype(jnp.int32)
            second_index = (wide_pad + inflow[1] + release[0] - release[1]).astype(jnp.int32)
            landed = lax.dynamic_slice(extended, (first_index, third_index, second_index), (S1, S3, S2))
            amount = release.astype(jnp.float32)
            benefit = (price[0] * amount[0] * height_first + price[1] * amount[1] * height_second + price[2] * amount[2] * height_third) / float(H)
            return running + jnp.exp(-(landed - benefit) / softness)

        running = lax.fori_loop(0, RELEASES, add_release, jnp.zeros((S1, S3, S2), jnp.float32))
        return running_total - softness * jnp.log(running), None

    running_total, _ = lax.scan(scenario, jnp.zeros((S1, S3, S2), jnp.float32), scenario_ids)
    average = running_total / float(SCENARIOS)
    return average - jnp.mean(average)
```

```python
import functools

import jax
import jax.numpy as jnp
from jax import lax
from jax.experimental import pallas as pl
from jax.experimental.pallas import tpu as pltpu
from jax.sharding import PartitionSpec as P

H = 8
LOW, HIGH = H, 2 * H
SUB, LANES = 8, 128
softness = 0.5

SHIFT_A, OFFSET, TURN, CUT, SHIFT_C = range(5)
FIRST_ROW, LAST_ROW, FIRST_DEPTH, LAST_DEPTH, ROW0, DEPTH0 = range(6)


class Sizes:
    def __init__(self, rows, depth, width, scenarios, releases):
        self.rows, self.depth, self.width = rows, depth, width
        self.scenarios, self.releases = scenarios, releases
        self.blocks = width // LANES
        self.strips = depth // SUB
        self.lanes_ext = self.blocks + 2
        self.depth_ext = LOW + depth + HIGH
        self.row_size = self.lanes_ext * self.depth_ext


def put(weights, sizes, row, at, values):
    for strip in range(values.shape[0] // SUB):
        levels = slice(strip * SUB, strip * SUB + SUB)
        base = row * sizes.row_size + at + strip * SUB
        for block in range(sizes.blocks):
            e = jnp.exp(values[levels, block * LANES : block * LANES + LANES] * (-1.0 / softness))
            weights[pl.ds(base + (block + 1) * sizes.depth_ext, SUB), :] = e
            if block == 0:
                weights[pl.ds(base, SUB), :] = jnp.broadcast_to(e[:, :1], e.shape)
            if block == sizes.blocks - 1:
                end = base + (sizes.blocks + 1) * sizes.depth_ext
                weights[pl.ds(end, SUB), :] = jnp.broadcast_to(e[:, LANES - 1 :], e.shape)


def put_zeros(weights, sizes, row, at, count):
    zero = jnp.zeros((SUB, LANES), jnp.float32)
    for strip in range(count // SUB):
        for block in range(sizes.lanes_ext):
            weights[pl.ds(row * sizes.row_size + block * sizes.depth_ext + at + strip * SUB, SUB), :] = zero


def put_row(weights, sizes, pos, row, own, low, high):
    if own is None:
        put_zeros(weights, sizes, row, LOW, sizes.depth)
    else:
        put(weights, sizes, row, LOW, own)
    for is_end, at, count, beyond, edge in (
        (pos[FIRST_DEPTH] != 0, 0, LOW, low, None if own is None else own[:1]),
        (pos[LAST_DEPTH] != 0, LOW + sizes.depth, HIGH, high, None if own is None else own[-1:]),
    ):

        @pl.when(is_end)
        def _():
            if edge is None:
                put_zeros(weights, sizes, row, at, count)
            else:
                put(weights, sizes, row, at, jnp.broadcast_to(edge, (count, sizes.width)))

        @pl.when(jnp.logical_not(is_end))
        def _():
            if beyond is None:
                put_zeros(weights, sizes, row, at, count)
            else:
                put(weights, sizes, row, at, beyond())


def fill_gains(gains, sizes, rates):
    lane = lax.broadcasted_iota(jnp.int32, (SUB, LANES), 1)
    for release in range(sizes.releases):
        for block in range(sizes.blocks):
            level = (lane + (block * LANES + 1)).astype(jnp.float32)
            gains[pl.ds((release * sizes.blocks + block) * SUB, SUB), :] = jnp.exp(level * rates[release, 1])


def add_terms(sums, table, rates, pos, weights, gains, sizes, scenario, row, first, count, start, stop, source_row, wanted):
    lane = lax.broadcasted_iota(jnp.int32, (SUB, LANES), 1)
    level = lax.broadcasted_iota(jnp.int32, (SUB, LANES), 0)
    level = (level + (pos[DEPTH0] + first * SUB + 1)).astype(jnp.float32)
    height = (pos[ROW0] + row + 1).astype(jnp.float32)

    def term(release, sums):
        at = scenario * sizes.releases + release
        base = source_row(row + table[at, SHIFT_A]) * sizes.row_size + table[at, OFFSET] + first * SUB
        later = lane < table[at, CUT]
        turn = table[at, TURN]
        out = []
        rate = rates[release, 2]
        flat = rates[release, 0] * height
        factors = [jnp.exp((level + float(strip * SUB)) * rate + flat) for strip in range(count)]
        for block in range(sizes.blocks):
            gain = gains[pl.ds((release * sizes.blocks + block) * SUB, SUB), :]
            for strip in range(count):
                here = weights[pl.ds(base + block * sizes.depth_ext + strip * SUB, SUB), :]
                beyond = weights[pl.ds(base + (block + 1) * sizes.depth_ext + strip * SUB, SUB), :]
                landed = pltpu.roll(jnp.where(later, beyond, here), turn, 1)
                out.append(sums[block * count + strip] + landed * (gain * factors[strip]))
        return tuple(out)

    def step(release, sums):
        if wanted is None:
            return term(release, sums)
        return lax.cond(wanted(table[scenario * sizes.releases + release, SHIFT_C]), lambda s: term(release, s), lambda s: s, sums)

    return lax.fori_loop(start, stop, step, sums)


def load_sums(ref, sizes, scenario, row, first, count):
    return tuple(
        ref[scenario, row, pl.ds(pl.multiple_of((first + strip) * SUB, SUB), SUB), block * LANES : block * LANES + LANES]
        for block in range(sizes.blocks)
        for strip in range(count)
    )


def store_sums(ref, sizes, scenario, row, first, count, sums):
    for block in range(sizes.blocks):
        for strip in range(count):
            ref[
                scenario, row, pl.ds(pl.multiple_of((first + strip) * SUB, SUB), SUB), block * LANES : block * LANES + LANES
            ] = sums[block * count + strip]


def own_range(below, inflow, pos, sizes, scenario, row):
    top = row + inflow[scenario]
    start = jnp.where(pos[LAST_ROW] != 0, 0, below[jnp.clip(top - sizes.rows + 1, 0, H + 1)])
    stop = jnp.where(pos[FIRST_ROW] != 0, sizes.releases, below[jnp.clip(top + 1, 0, H + 1)])
    return start, stop


def own_kernel(sizes, table, rates, below, inflow, pos, values, sums_out, weights, gains):
    fill_gains(gains, sizes, rates)

    def fill(row, _):
        put_row(weights, sizes, pos, row, values[row], None, None)
        return 0

    lax.fori_loop(0, sizes.rows, fill, 0)
    zero = jnp.zeros((SUB, LANES), jnp.float32)

    def work(index, _):
        scenario, row = index // sizes.rows, index % sizes.rows
        start, stop = own_range(below, inflow, pos, sizes, scenario, row)
        sums = tuple(zero for _ in range(sizes.blocks * sizes.strips))
        sums = add_terms(
            sums, table, rates, pos, weights, gains, sizes, scenario, row, 0, sizes.strips, start, stop,
            lambda r: jnp.clip(r, 0, sizes.rows - 1), None,
        )
        store_sums(sums_out, sizes, scenario, row, 0, sizes.strips, sums)
        return 0

    lax.fori_loop(0, sizes.scenarios * sizes.rows, work, 0)


def beyond_levels(pair, pos, low_ref, high_ref, row):
    return lambda: low_ref[row, low_ref.shape[1] - LOW :], lambda: high_ref[row, :HIGH]


def edge_strips(sizes, pos, pair):
    count = min(HIGH // SUB, sizes.strips)
    if pair:
        return jnp.where(pos[FIRST_DEPTH] != 0, sizes.strips - count, 0), count
    return 0, sizes.strips


def reaches(sizes, pos, first, count):
    def test(shift):
        up = jnp.logical_and(pos[LAST_DEPTH] == 0, first * SUB + count * SUB + shift > sizes.depth)
        down = jnp.logical_and(pos[FIRST_DEPTH] == 0, first * SUB + shift < 0)
        return jnp.logical_or(up, down)

    return test


def outside_row(sizes):
    return lambda r: jnp.where(r < 0, r + H, r - sizes.rows + H)


def outside_terms(ref_in, ref_out, table, rates, below, inflow, pos, weights, gains, sizes, first, count, wanted):
    def work(index, _):
        scenario, row = index // sizes.rows, index % sizes.rows
        start, stop = own_range(below, inflow, pos, sizes, scenario, row)

        @pl.when(jnp.logical_or(start > 0, stop < sizes.releases))
        def _():
            sums = load_sums(ref_in, sizes, scenario, row, first, count)
            for lo, hi in ((0, start), (stop, sizes.releases)):
                sums = add_terms(
                    sums, table, rates, pos, weights, gains, sizes, scenario, row, first, count, lo, hi, outside_row(sizes), wanted
                )
            store_sums(ref_out, sizes, scenario, row, first, count, sums)

        return 0

    lax.fori_loop(0, sizes.scenarios * sizes.rows, work, 0)


def edge_kernel(sizes, pair, table, rates, below, inflow, pos, low, high, before, after, sums_in, sums_out, weights, gains):
    fill_gains(gains, sizes, rates)

    def fill_depth(row, _):
        put_row(weights, sizes, pos, row, None, *beyond_levels(pair, pos, low, high, row))
        return 0

    lax.fori_loop(0, sizes.rows, fill_depth, 0)
    first, count = edge_strips(sizes, pos, pair)
    wanted = reaches(sizes, pos, first, count)
    sums_out[...] = sums_in[...]

    def work(index, _):
        scenario, row = index // sizes.rows, index % sizes.rows
        start, stop = own_range(below, inflow, pos, sizes, scenario, row)
        sums = load_sums(sums_out, sizes, scenario, row, first, count)
        sums = add_terms(
            sums, table, rates, pos, weights, gains, sizes, scenario, row, first, count, start, stop,
            lambda r: jnp.clip(r, 0, sizes.rows - 1), wanted,
        )
        store_sums(sums_out, sizes, scenario, row, first, count, sums)
        return 0

    lax.fori_loop(0, sizes.scenarios * sizes.rows, work, 0)

    def fill_rows(row, _):
        put_row(weights, sizes, pos, row, before[row], None, None)
        put_row(weights, sizes, pos, row + H, after[row], None, None)
        return 0

    lax.fori_loop(0, H, fill_rows, 0)
    outside_terms(sums_out, sums_out, table, rates, below, inflow, pos, weights, gains, sizes, 0, sizes.strips, None)


def last_kernel(
    sizes, pair, scale, table, rates, below, inflow, pos, low_before, high_before, low_after, high_after, sums_in, average_out, total_out,
    sums, weights, gains,
):
    fill_gains(gains, sizes, rates)

    def fill_rows(row, _):
        put_row(weights, sizes, pos, row, None, *beyond_levels(pair, pos, low_before, high_before, row))
        put_row(weights, sizes, pos, row + H, None, *beyond_levels(pair, pos, low_after, high_after, row))
        return 0

    lax.fori_loop(0, H, fill_rows, 0)
    first, count = edge_strips(sizes, pos, pair)
    sums[...] = sums_in[...]
    outside_terms(sums, sums, table, rates, below, inflow, pos, weights, gains, sizes, first, count, reaches(sizes, pos, first, count))

    def finish(row, total):
        for strip in range(sizes.strips):
            for block in range(sizes.blocks):
                tile = (row, slice(strip * SUB, strip * SUB + SUB), slice(block * LANES, block * LANES + LANES))
                logs = None
                for scenario in range(0, sizes.scenarios, 2):
                    product = sums[(scenario, *tile)]
                    if scenario + 1 < sizes.scenarios:
                        product = product * sums[(scenario + 1, *tile)]
                    log = jnp.log(product)
                    logs = log if logs is None else logs + log
                average = logs * scale
                average_out[tile] = average
                total = total + average
        return total

    total = lax.fori_loop(0, sizes.rows, finish, jnp.zeros((SUB, LANES), jnp.float32))
    total_out[...] = jnp.sum(total, axis=0, keepdims=True)


def call(kernel, scalars, arrays, outs, scratch, aliases=None):
    smem, vmem = pl.BlockSpec(memory_space=pltpu.SMEM), pl.BlockSpec(memory_space=pltpu.VMEM)
    return pl.pallas_call(
        kernel,
        out_shape=outs,
        in_specs=[smem] * len(scalars) + [vmem] * len(arrays),
        out_specs=jax.tree.map(lambda _: vmem, outs),
        scratch_shapes=scratch,
        input_output_aliases=aliases or {},
        compiler_params=pltpu.CompilerParams(vmem_limit_bytes=56 * 2**20),
    )(*scalars, *arrays)


def from_above(cells, axis, hops=1):
    count = lax.axis_size(axis)
    return lax.ppermute(cells, axis, [(i + hops, i) for i in range(count - hops)])


def from_below(cells, axis, hops=1):
    count = lax.axis_size(axis)
    return lax.ppermute(cells, axis, [(i, i + hops) for i in range(count - hops)])


def on_device(value_next, scenario_ids, inflow_table, release_shifts, price):
    rows, depth, width = value_next.shape
    grid_count, scen_count = lax.axis_size("grid"), lax.axis_size("scen")
    grid, scen = lax.axis_index("grid"), lax.axis_index("scen")
    total_rows, total_depth = rows * grid_count, depth * scen_count
    releases = release_shifts.shape[0]
    pair = scen_count == 2 and depth >= HIGH

    ids = [scenario_ids]
    for hop in range(1, scen_count):
        ids.append(lax.ppermute(scenario_ids, "scen", [(i, (i + hop) % scen_count) for i in range(scen_count)]))
    ids = jnp.concatenate(ids)
    sizes = Sizes(rows, depth, width, ids.shape[0], releases)

    if pair:
        start = jnp.where(scen == 0, depth - HIGH, 0)
        sent = lax.dynamic_slice_in_dim(value_next, start, HIGH, axis=1)
        low = high = lax.ppermute(sent, "scen", [(0, 1), (1, 0)])
    else:
        low, high = [], []
        for hop in range(-(-LOW // depth), 0, -1):
            low.append(from_below(value_next, "scen", hop) if hop < scen_count else jnp.zeros_like(value_next))
        for hop in range(1, -(-HIGH // depth) + 1):
            high.append(from_above(value_next, "scen", hop) if hop < scen_count else jnp.zeros_like(value_next))
        low = jnp.concatenate(low, axis=1)[:, -LOW:]
        high = jnp.concatenate(high, axis=1)[:, :HIGH]
        last = value_next[:, -1:]
        for hop in range(1, -(-HIGH // depth)):
            past = jnp.where(scen + hop == scen_count - 1, 1, 0)
            fill = high[:, hop * depth - 1 : hop * depth]
            keep = lax.broadcasted_iota(jnp.int32, high.shape, 1) < hop * depth
            high = jnp.where(jnp.logical_or(past == 0, keep), high, fill)
        del last
    before = from_below(value_next[rows - H :], "grid")
    after = from_above(value_next[:H], "grid")

    shifts = release_shifts[:, 0]
    order = jnp.arange(releases, dtype=jnp.int32)
    ahead = jnp.logical_or(
        shifts[None, :] < shifts[:, None], jnp.logical_and(shifts[None, :] == shifts[:, None], order[None, :] < order[:, None])
    )
    rank = jnp.sum(ahead.astype(jnp.int32), axis=1)
    moved = (rank[None, :] == order[:, None]).astype(jnp.int32)
    sorted_shifts = jnp.sum(moved[:, :, None] * release_shifts[None, :, :], axis=1)
    below = jnp.sum((shifts[None, :] < jnp.arange(H + 2, dtype=jnp.int32)[:, None]).astype(jnp.int32), axis=1)
    one_hot = (ids[:, None] == jnp.arange(inflow_table.shape[0], dtype=jnp.int32)[None, :]).astype(jnp.int32)
    inflows = jnp.sum(one_hot[:, :, None] * inflow_table[None, :, :], axis=1)
    u1, u2, u3 = (sorted_shifts[None, :, i] for i in range(3))
    i1, i2, i3 = (inflows[:, None, i] for i in range(3))
    shift_b = i2 + u1 - u2
    shift_c = i3 + u2 - u3
    ahead_b = shift_b >= 0
    cut = jnp.where(ahead_b, shift_b, shift_b + LANES)
    table = jnp.stack(
        [i1 - u1, jnp.where(ahead_b, sizes.depth_ext, 0) + LOW + shift_c, (LANES - cut) % LANES, cut, shift_c], axis=-1
    ).reshape(-1, 5)
    spans = jnp.array([total_rows, width, total_depth], jnp.float32)
    rates = sorted_shifts.astype(jnp.float32) * (price / (spans * (H * softness)))[None, :]
    pos = jnp.stack(
        [grid == 0, grid == grid_count - 1, scen == 0, scen == scen_count - 1, grid * rows, scen * depth]
    ).astype(jnp.int32)
    scalars = (table, rates, below, inflows[:, 0], pos)

    sums_shape = jax.ShapeDtypeStruct((sizes.scenarios, rows, depth, width), jnp.float32)
    gains = pltpu.VMEM((releases * sizes.blocks * SUB, LANES), jnp.float32)
    ext = pltpu.VMEM((max(rows, 2 * H) * sizes.row_size, LANES), jnp.float32)
    sums = call(functools.partial(own_kernel, sizes), scalars, (value_next,), sums_shape, [ext, gains])

    sums = call(
        functools.partial(edge_kernel, sizes, pair), scalars, (low, high, before, after, sums), sums_shape, [ext, gains],
        {len(scalars) + 4: 0},
    )

    if pair:
        low_before = high_before = from_below(low[rows - H :], "grid")
        low_after = high_after = from_above(low[:H], "grid")
    else:
        both = jnp.concatenate([low, high], axis=1)
        both_before, both_after = from_below(both[rows - H :], "grid"), from_above(both[:H], "grid")
        low_before, high_before = both_before[:, :LOW], both_before[:, LOW:]
        low_after, high_after = both_after[:, :LOW], both_after[:, LOW:]

    scale = -softness / sizes.scenarios
    average, total = call(
        functools.partial(last_kernel, sizes, pair, scale), scalars, (low_before, high_before, low_after, high_after, sums),
        (jax.ShapeDtypeStruct(value_next.shape, jnp.float32), jax.ShapeDtypeStruct((1, LANES), jnp.float32)),
        [pltpu.VMEM(sums_shape.shape, jnp.float32), pltpu.VMEM((2 * H * sizes.row_size, LANES), jnp.float32), gains],
    )
    devices = grid_count * scen_count
    totals = lax.all_to_all(jnp.broadcast_to(total[None], (devices, 1, LANES)), ("scen", "grid"), 0, 0, tiled=True)
    return average - jnp.sum(totals) / float(total_rows * total_depth * width)


def solution(mesh):
    placed = (P("grid", "scen", None), P("scen"), P(), P(), P())
    return jax.shard_map(
        on_device, mesh=mesh, in_specs=placed, out_specs=P("grid", "scen", None), check_vma=False
    )
```

```python
import functools

import jax
import jax.numpy as jnp
from jax import lax
from jax.experimental import pallas as pl
from jax.experimental.pallas import tpu as pltpu
from jax.sharding import PartitionSpec as P

H = 8
LOW, HIGH = H, 2 * H
SUB, LANES = 8, 128
softness = 0.5

SHIFT_A, OFFSET = range(2)
UNROLL = 2
FIRST_ROW, LAST_ROW, FIRST_DEPTH, LAST_DEPTH = range(4)


class Sizes:
    def __init__(self, rows, depth, width, scenarios, releases):
        self.rows, self.depth, self.width = rows, depth, width
        self.scenarios, self.releases = scenarios, releases
        self.listed = releases + UNROLL - 1
        self.planes = width // LANES
        self.group = LANES // self.planes
        self.strips = depth // SUB
        self.planes_ext = LOW + self.planes + HIGH
        self.depth_ext = LOW + depth + HIGH
        self.row_size = self.planes_ext * self.depth_ext

    def place(self, lane):
        return lane % self.planes * self.group + lane // self.planes

    def lane(self, place):
        return place % self.group * self.planes + place // self.group


def transpose(blocks):
    lane = lax.broadcasted_iota(jnp.int32, (SUB, LANES), 1)
    blocks = list(blocks)
    step = 1
    while step < len(blocks):
        odd = (lane // step) % 2 == 1
        for i in range(len(blocks)):
            if i // step % 2 == 0:
                first, second = blocks[i], blocks[i + step]
                blocks[i] = jnp.where(odd, pltpu.roll(second, step, 1), first)
                blocks[i + step] = jnp.where(odd, second, pltpu.roll(first, LANES - step, 1))
        step *= 2
    return blocks


def put(weights, sizes, row, at, values):
    lane = lax.broadcasted_iota(jnp.int32, (SUB, LANES), 1)
    for strip in range(values.shape[0] // SUB):
        levels = slice(strip * SUB, strip * SUB + SUB)
        base = row * sizes.row_size + at + strip * SUB
        planes = transpose(
            jnp.exp(values[levels, block * LANES : block * LANES + LANES] * (-1.0 / softness)) for block in range(sizes.planes)
        )

        def store(beyond, moved):
            for plane in range(sizes.planes):
                to = LOW + beyond * sizes.planes + plane
                if 0 <= to < sizes.planes_ext:
                    weights[pl.ds(base + to * sizes.depth_ext, SUB), :] = moved[plane]

        store(0, planes)
        for up in (False, True):
            turn = LANES - 1 if up else 1
            next_lane = [pltpu.roll(plane, turn, 1) for plane in planes]
            last = LANES - 1 if up else 0
            for beyond in range(1, -(-(HIGH if up else LOW) // sizes.planes) + 1):
                wrap = beyond * sizes.planes
                wrapped = lane < wrap if up else lane >= LANES - wrap
                moved = [
                    pltpu.roll(jnp.where(wrapped, there, plane), LANES - wrap if up else wrap, 1)
                    for plane, there in zip(planes, next_lane, strict=True)
                ]
                place = sizes.place(lane)
                past = place + beyond > last if up else place < beyond
                end = jnp.broadcast_to(planes[-1 if up else 0][:, last : last + 1], (SUB, LANES))
                store(beyond if up else -beyond, [jnp.where(past, end, plane) for plane in moved])


def repeat(weights, sizes, row, source, at, count):
    for plane in range(sizes.planes_ext):
        base = row * sizes.row_size + plane * sizes.depth_ext
        level = jnp.broadcast_to(weights[pl.ds(base + source, 1), :], (SUB, LANES))
        for strip in range(count // SUB):
            weights[pl.ds(base + at + strip * SUB, SUB), :] = level


def put_zeros(weights, sizes, row, at, count):
    zero = jnp.zeros((SUB, LANES), jnp.float32)
    for strip in range(count // SUB):
        for plane in range(sizes.planes_ext):
            weights[pl.ds(row * sizes.row_size + plane * sizes.depth_ext + at + strip * SUB, SUB), :] = zero


def put_row(weights, sizes, pos, row, own, low, high):
    if own is None:
        put_zeros(weights, sizes, row, LOW, sizes.depth)
    else:
        put(weights, sizes, row, LOW, own)
    for is_end, at, count, beyond, edge in (
        (pos[FIRST_DEPTH] != 0, 0, LOW, low, LOW),
        (pos[LAST_DEPTH] != 0, LOW + sizes.depth, HIGH, high, LOW + sizes.depth - 1),
    ):

        @pl.when(is_end)
        def _():
            if own is None:
                put_zeros(weights, sizes, row, at, count)
            else:
                repeat(weights, sizes, row, edge, at, count)

        @pl.when(jnp.logical_not(is_end))
        def _():
            if beyond is None:
                put_zeros(weights, sizes, row, at, count)
            else:
                put(weights, sizes, row, at, beyond())


def add_term(sums, table, heights, gains, depths, weights, sizes, scenario, row, first, count, release, source_row):
    at = scenario * sizes.listed + release
    base = source_row(row + table[at, SHIFT_A]) * sizes.row_size + table[at, OFFSET] + first * SUB
    height = heights[at, row]
    out = []
    factors = [
        depths[pl.ds(pl.multiple_of(release * sizes.depth + (first + strip) * SUB, SUB), SUB), :] * height for strip in range(count)
    ]
    for plane in range(sizes.planes):
        gain = gains[pl.ds(pl.multiple_of((release * sizes.planes + plane) * SUB, SUB), SUB), :]
        for strip in range(count):
            landed = weights[pl.ds(base + plane * sizes.depth_ext + strip * SUB, SUB), :]
            out.append(sums[plane * count + strip] + landed * (gain * factors[strip]))
    return out


def own_row(sizes):
    return lambda r: jnp.clip(r, 0, sizes.rows - 1)


def outside_row(sizes):
    return lambda r: jnp.clip(jnp.where(r < 0, r + H, r - sizes.rows + H), 0, 2 * H - 1)


def load_sums(ref, sizes, scenario, row, first, count):
    return tuple(
        ref[scenario, row, plane, pl.ds(pl.multiple_of((first + strip) * SUB, SUB), SUB), :]
        for plane in range(sizes.planes)
        for strip in range(count)
    )


def store_sums(ref, sizes, scenario, row, first, count, sums):
    for plane in range(sizes.planes):
        for strip in range(count):
            ref[scenario, row, plane, pl.ds(pl.multiple_of((first + strip) * SUB, SUB), SUB), :] = sums[plane * count + strip]


def own_range(below, inflow, pos, sizes, scenario, row):
    top = row + inflow[scenario]
    start = jnp.where(pos[LAST_ROW] != 0, 0, below[jnp.clip(top - sizes.rows + 1, 0, H + 1)])
    stop = jnp.where(pos[FIRST_ROW] != 0, sizes.releases, below[jnp.clip(top + 1, 0, H + 1)])
    return start, stop


def own_terms(load, store, table, heights, gains, depths, weights, sizes, first, count):
    def work(index, _):
        scenario, row = index // sizes.rows, index % sizes.rows
        sums = load(scenario, row, first, count)
        for release in range(sizes.releases):
            sums = add_term(sums, table, heights, gains, depths, weights, sizes, scenario, row, first, count, release, own_row(sizes))
        store(scenario, row, first, count, sums)
        return 0

    lax.fori_loop(0, sizes.scenarios * sizes.rows, work, 0)


def own_kernel(sizes, table, heights, below, inflow, pos, gains, depths, values, sums_out, weights):
    def fill(row, _):
        put_row(weights, sizes, pos, row, values[row], None, None)
        return 0

    lax.fori_loop(0, sizes.rows, fill, 0)
    zero = jnp.zeros((SUB, LANES), jnp.float32)

    def load(scenario, row, first, count):
        return [zero] * (sizes.planes * count)

    step = min(sizes.strips, 4)
    for first in range(0, sizes.strips, step):
        own_terms(
            load, functools.partial(store_sums, sums_out, sizes), table, heights, gains, depths, weights, sizes, first,
            min(step, sizes.strips - first),
        )


def beyond_levels(pair, pos, low_ref, high_ref, row):
    return lambda: low_ref[row, low_ref.shape[1] - LOW :], lambda: high_ref[row, :HIGH]


def edge_strips(sizes, pos, pair):
    count = min(HIGH // SUB, sizes.strips)
    if pair:
        return jnp.where(pos[FIRST_DEPTH] != 0, sizes.strips - count, 0), count
    return 0, sizes.strips


def outside_terms(ref_in, ref_out, table, heights, below, inflow, pos, gains, depths, weights, sizes, first, count):
    def work(index, _):
        scenario, row = index // sizes.rows, index % sizes.rows
        top = row + inflow[scenario]
        start = jnp.where(pos[LAST_ROW] != 0, 0, below[jnp.clip(top - sizes.rows + 1, 0, H + 1)])
        stop = jnp.where(pos[FIRST_ROW] != 0, sizes.releases, below[jnp.clip(top + 1, 0, H + 1)])

        def some(lo, hi):
            @pl.when(lo < hi)
            def _():
                def step(index, sums):
                    for k in range(UNROLL):
                        sums = add_term(
                            sums, table, heights, gains, depths, weights, sizes, scenario, row, first, count, lo + index * UNROLL + k,
                            outside_row(sizes),
                        )
                    return tuple(sums)

                sums = lax.fori_loop(0, (hi - lo + UNROLL - 1) // UNROLL, step, load_sums(ref_in, sizes, scenario, row, first, count))
                store_sums(ref_out, sizes, scenario, row, first, count, sums)

        some(0, start)
        some(stop, sizes.releases)
        return 0

    lax.fori_loop(0, sizes.scenarios * sizes.rows, work, 0)


def edge_kernel(
    sizes, pair, table, heights, outside, below, inflow, pos, gains, depths, low, high, before, after, sums_in, sums_out, weights
):
    def fill_depth(row, _):
        put_row(weights, sizes, pos, row, None, *beyond_levels(pair, pos, low, high, row))
        return 0

    lax.fori_loop(0, sizes.rows, fill_depth, 0)
    first, count = edge_strips(sizes, pos, pair)
    sums_out[...] = sums_in[...]
    own_terms(
        functools.partial(load_sums, sums_out, sizes), functools.partial(store_sums, sums_out, sizes), table, heights, gains, depths,
        weights, sizes, first, count,
    )

    def fill_rows(row, _):
        put_row(weights, sizes, pos, row, before[row], None, None)
        put_row(weights, sizes, pos, row + H, after[row], None, None)
        return 0

    lax.fori_loop(0, H, fill_rows, 0)
    step = min(sizes.strips, 4)
    for first in range(0, sizes.strips, step):
        outside_terms(
            sums_out, sums_out, table, outside, below, inflow, pos, gains, depths, weights, sizes, first, min(step, sizes.strips - first)
        )


def last_kernel(
    sizes, pair, scale, table, outside, below, inflow, pos, gains, depths, low_before, high_before, low_after, high_after, sums_in,
    average_out, total_out, sums, weights,
):
    def fill_rows(row, _):
        put_row(weights, sizes, pos, row, None, *beyond_levels(pair, pos, low_before, high_before, row))
        put_row(weights, sizes, pos, row + H, None, *beyond_levels(pair, pos, low_after, high_after, row))
        return 0

    lax.fori_loop(0, H, fill_rows, 0)
    first, count = edge_strips(sizes, pos, pair)
    sums[...] = sums_in[...]
    outside_terms(sums, sums, table, outside, below, inflow, pos, gains, depths, weights, sizes, first, count)

    def finish(row, total):
        for strip in range(sizes.strips):
            levels = slice(strip * SUB, strip * SUB + SUB)
            averages = []
            for plane in range(sizes.planes):
                logs = None
                for scenario in range(0, sizes.scenarios, 2):
                    product = sums[scenario, row, plane, levels, :]
                    if scenario + 1 < sizes.scenarios:
                        product = product * sums[scenario + 1, row, plane, levels, :]
                    log = jnp.log(product)
                    logs = log if logs is None else logs + log
                averages.append(logs * scale)
                total = total + averages[-1]
            for block, average in enumerate(transpose(averages)):
                average_out[row, levels, block * LANES : block * LANES + LANES] = average
        return total

    total = lax.fori_loop(0, sizes.rows, finish, jnp.zeros((SUB, LANES), jnp.float32))
    total_out[...] = jnp.sum(total, axis=0, keepdims=True)


def call(kernel, scalars, arrays, outs, scratch, aliases=None):
    smem, vmem = pl.BlockSpec(memory_space=pltpu.SMEM), pl.BlockSpec(memory_space=pltpu.VMEM)
    return pl.pallas_call(
        kernel,
        out_shape=outs,
        in_specs=[smem] * len(scalars) + [vmem] * len(arrays),
        out_specs=jax.tree.map(lambda _: vmem, outs),
        scratch_shapes=scratch,
        input_output_aliases=aliases or {},
        compiler_params=pltpu.CompilerParams(vmem_limit_bytes=32 * 2**20),
    )(*scalars, *arrays)


def from_above(cells, axis, hops=1):
    count = lax.axis_size(axis)
    return lax.ppermute(cells, axis, [(i + hops, i) for i in range(count - hops)])


def from_below(cells, axis, hops=1):
    count = lax.axis_size(axis)
    return lax.ppermute(cells, axis, [(i, i + hops) for i in range(count - hops)])


def on_device(value_next, scenario_ids, inflow_table, release_shifts, price):
    rows, depth, width = value_next.shape
    grid_count, scen_count = lax.axis_size("grid"), lax.axis_size("scen")
    grid, scen = lax.axis_index("grid"), lax.axis_index("scen")
    total_rows, total_depth = rows * grid_count, depth * scen_count
    releases = release_shifts.shape[0]
    pair = scen_count == 2 and depth >= HIGH

    ids = [scenario_ids]
    for hop in range(1, scen_count):
        ids.append(lax.ppermute(scenario_ids, "scen", [(i, (i + hop) % scen_count) for i in range(scen_count)]))
    ids = jnp.concatenate(ids)
    sizes = Sizes(rows, depth, width, ids.shape[0], releases)

    if pair:
        start = jnp.where(scen == 0, depth - HIGH, 0)
        sent = lax.dynamic_slice_in_dim(value_next, start, HIGH, axis=1)
        low = high = lax.ppermute(sent, "scen", [(0, 1), (1, 0)])
    else:
        low, high = [], []
        for hop in range(-(-LOW // depth), 0, -1):
            low.append(from_below(value_next, "scen", hop) if hop < scen_count else jnp.zeros_like(value_next))
        for hop in range(1, -(-HIGH // depth) + 1):
            high.append(from_above(value_next, "scen", hop) if hop < scen_count else jnp.zeros_like(value_next))
        low = jnp.concatenate(low, axis=1)[:, -LOW:]
        high = jnp.concatenate(high, axis=1)[:, :HIGH]
        last = value_next[:, -1:]
        for hop in range(1, -(-HIGH // depth)):
            past = jnp.where(scen + hop == scen_count - 1, 1, 0)
            fill = high[:, hop * depth - 1 : hop * depth]
            keep = lax.broadcasted_iota(jnp.int32, high.shape, 1) < hop * depth
            high = jnp.where(jnp.logical_or(past == 0, keep), high, fill)
        del last
    before = from_below(value_next[rows - H :], "grid")
    after = from_above(value_next[:H], "grid")

    shifts = release_shifts[:, 0]
    order = jnp.arange(releases, dtype=jnp.int32)
    ahead = jnp.logical_or(
        shifts[None, :] < shifts[:, None], jnp.logical_and(shifts[None, :] == shifts[:, None], order[None, :] < order[:, None])
    )
    rank = jnp.sum(ahead.astype(jnp.int32), axis=1)
    moved = (rank[None, :] == order[:, None]).astype(jnp.int32)
    sorted_shifts = jnp.sum(moved[:, :, None] * release_shifts[None, :, :], axis=1)
    below = jnp.sum((shifts[None, :] < jnp.arange(H + 2, dtype=jnp.int32)[:, None]).astype(jnp.int32), axis=1)
    one_hot = (ids[:, None] == jnp.arange(inflow_table.shape[0], dtype=jnp.int32)[None, :]).astype(jnp.int32)
    inflows = jnp.sum(one_hot[:, :, None] * inflow_table[None, :, :], axis=1)
    u1, u2, u3 = (sorted_shifts[None, :, i] for i in range(3))
    i1, i2, i3 = (inflows[:, None, i] for i in range(3))
    shift_b = i2 + u1 - u2
    shift_c = i3 + u2 - u3
    extra = ((0, 0), (0, sizes.listed - releases), (0, 0))
    table = jnp.stack([i1 - u1, (LOW + shift_b) * sizes.depth_ext + LOW + shift_c], axis=-1)
    table = jnp.pad(table, extra).reshape(-1, 2)
    spans = jnp.array([total_rows, width, total_depth], jnp.float32)
    rates = sorted_shifts.astype(jnp.float32) * (price / (spans * (H * softness)))[None, :]
    pos = jnp.stack([grid == 0, grid == grid_count - 1, scen == 0, scen == scen_count - 1]).astype(jnp.int32)
    row_heights = (grid * rows + 1 + jnp.arange(rows, dtype=jnp.int32)).astype(jnp.float32)
    heights = jnp.exp(rates[:, :1] * row_heights[None, :])[None]
    lands = (i1 - u1)[:, :, None] + jnp.arange(rows, dtype=jnp.int32)
    is_own = jnp.logical_and(jnp.logical_or(grid == 0, lands >= 0), jnp.logical_or(grid == grid_count - 1, lands < rows))
    outside = jnp.pad(jnp.where(is_own, 0.0, heights), extra).reshape(-1, rows)
    heights = jnp.pad(jnp.where(is_own, heights, 0.0), extra).reshape(-1, rows)
    listed = ((0, sizes.listed - releases), (0, 0), (0, 0))
    level = (scen * depth + 1 + jnp.arange(depth, dtype=jnp.int32)).astype(jnp.float32)
    depths = jnp.exp(jnp.broadcast_to(rates[:, 2][:, None, None] * level[None, :, None], (releases, depth, LANES)))
    place = sizes.place(jnp.arange(LANES, dtype=jnp.int32))
    level = (place[None, :] * sizes.planes + jnp.arange(sizes.planes, dtype=jnp.int32)[:, None] + 1).astype(jnp.float32)
    gains = jnp.exp(jnp.broadcast_to((rates[:, 1][:, None, None] * level[None])[:, :, None, :], (releases, sizes.planes, SUB, LANES)))
    factors = (
        jnp.pad(gains.reshape(releases, -1, LANES), listed).reshape(-1, LANES),
        jnp.pad(depths, listed).reshape(-1, LANES),
    )

    sums_shape = jax.ShapeDtypeStruct((sizes.scenarios, rows, sizes.planes, depth, LANES), jnp.float32)
    ext = pltpu.VMEM((max(rows, 2 * H) * sizes.row_size, LANES), jnp.float32)
    sums = call(functools.partial(own_kernel, sizes), (table, heights, below, inflows[:, 0], pos), (*factors, value_next), sums_shape, [ext])

    low, high, sums = lax.optimization_barrier((low, high, sums))

    if pair:
        low_before = high_before = from_below(low[rows - H :], "grid")
        low_after = high_after = from_above(low[:H], "grid")
    else:
        both = jnp.concatenate([low, high], axis=1)
        both_before, both_after = from_below(both[rows - H :], "grid"), from_above(both[:H], "grid")
        low_before, high_before = both_before[:, :LOW], both_before[:, LOW:]
        low_after, high_after = both_after[:, :LOW], both_after[:, LOW:]

    sums = call(
        functools.partial(edge_kernel, sizes, pair), (table, heights, outside, below, inflows[:, 0], pos), (*factors, low, high, before, after, sums), sums_shape, [ext],
        {12: 0},
    )

    scale = -softness / sizes.scenarios
    average, total = call(
        functools.partial(last_kernel, sizes, pair, scale), (table, outside, below, inflows[:, 0], pos), (*factors, low_before, high_before, low_after, high_after, sums),
        (jax.ShapeDtypeStruct(value_next.shape, jnp.float32), jax.ShapeDtypeStruct((1, LANES), jnp.float32)),
        [pltpu.VMEM(sums_shape.shape, jnp.float32), pltpu.VMEM((2 * H * sizes.row_size, LANES), jnp.float32)],
    )
    devices = grid_count * scen_count
    totals = lax.all_to_all(jnp.broadcast_to(total[None], (devices, 1, LANES)), ("scen", "grid"), 0, 0, tiled=True)
    return average - jnp.sum(totals) / float(total_rows * total_depth * width)


def solution(mesh):
    placed = (P("grid", "scen", None), P("scen"), P(), P(), P())
    return jax.shard_map(
        on_device, mesh=mesh, in_specs=placed, out_specs=P("grid", "scen", None), check_vma=False
    )
```

```python
import functools

import jax
import jax.numpy as jnp
from jax import lax
from jax.experimental import pallas as pl
from jax.experimental.pallas import tpu as pltpu
from jax.sharding import PartitionSpec as P

H = 8
LOW, HIGH = H, 2 * H
SUB, LANES = 8, 128
TILE = 1
UNROLL = 2
softness = 0.5

SHIFT_A, OFFSET, EDGE_OFFSET = range(3)


class Sizes:
    def __init__(self, rows, depth, width, scenarios, releases, grid_count, scen_count):
        self.rows, self.depth, self.width = rows, depth, width
        self.grid_count, self.scen_count = grid_count, scen_count
        self.scenarios, self.releases = scenarios, releases
        self.listed = releases + UNROLL - 1
        self.planes = width // LANES
        self.group = LANES // self.planes
        self.strips = depth // SUB
        self.planes_ext = LOW + self.planes + HIGH
        self.depth_ext = LOW + depth + HIGH
        self.row_size = self.planes_ext * self.depth_ext
        self.pair = scen_count == 2 and depth >= HIGH
        self.edge_strips = HIGH // SUB if self.pair else self.strips
        self.edge_ext = 2 * HIGH if self.pair else self.depth_ext
        self.edge_size = self.planes_ext * self.edge_ext

    def place(self, lane):
        return lane % self.planes * self.group + lane // self.planes

    def lane(self, place):
        return place % self.group * self.planes + place // self.group


def transpose(blocks):
    lane = lax.broadcasted_iota(jnp.int32, (SUB, LANES), 1)
    blocks = list(blocks)
    step = 1
    while step < len(blocks):
        odd = (lane // step) % 2 == 1
        for i in range(len(blocks)):
            if i // step % 2 == 0:
                first, second = blocks[i], blocks[i + step]
                blocks[i] = jnp.where(odd, pltpu.roll(second, step, 1), first)
                blocks[i + step] = jnp.where(odd, second, pltpu.roll(first, LANES - step, 1))
        step *= 2
    return blocks


def turns(sizes):
    return [*range(-(-(-LOW // sizes.planes)), 0), *range(1, -(-HIGH // sizes.planes) + 1)]


def fill_turns(matrix, sizes):
    shape = (2 * LANES, LANES)
    source = lax.broadcasted_iota(jnp.int32, shape, 0) % LANES
    place = sizes.place(lax.broadcasted_iota(jnp.int32, shape, 1))
    for i, turn in enumerate(turns(sizes)):
        there = jnp.clip(place + turn, 0, LANES - 1)
        matrix[:, i * LANES : i * LANES + LANES] = (sizes.lane(there) == source).astype(jnp.float32).astype(jnp.bfloat16)


def put(weights, sizes, matrix, row_bases, depth_ext, at, rows):
    place = sizes.place(lax.broadcasted_iota(jnp.int32, (SUB, LANES), 1))
    levels = rows[0].shape[1]
    both = jnp.concatenate([row.reshape(sizes.planes * levels, LANES) for row in rows], axis=0)
    upper = both.astype(jnp.bfloat16)
    lower = (both - upper.astype(jnp.float32)).astype(jnp.bfloat16)
    turned = jnp.dot(jnp.concatenate([upper, lower], axis=1), matrix[...], preferred_element_type=jnp.float32)
    for row, row_base in enumerate(row_bases):
        for strip in range(levels // SUB):
            base = row_base + at + strip * SUB

            def part(array, plane):
                first = (row * sizes.planes + plane) * levels + strip * SUB
                return array[first : first + SUB]

            for plane in range(sizes.planes):
                weights[pl.ds(base + (LOW + plane) * depth_ext, SUB), :] = part(both, plane)
            for i, turn in enumerate(turns(sizes)):
                moved = turned[:, i * LANES : i * LANES + LANES]
                end = part(moved, sizes.planes - 1 if turn > 0 else 0)
                past = place + turn > LANES - 1 if turn > 0 else place + turn < 0
                for plane in range(sizes.planes):
                    to = LOW + turn * sizes.planes + plane
                    if 0 <= to < sizes.planes_ext:
                        weights[pl.ds(base + to * depth_ext, SUB), :] = jnp.where(past, end, part(moved, plane))


def put_zeros(weights, sizes, row_base, depth_ext, at, count):
    zero = jnp.zeros((SUB, LANES), jnp.float32)
    for strip in range(count // SUB):
        for plane in range(sizes.planes_ext):
            weights[pl.ds(row_base + plane * depth_ext + at + strip * SUB, SUB), :] = zero


def repeat(weights, sizes, row_base, depth_ext, source, at, count):
    for plane in range(sizes.planes_ext):
        base = row_base + plane * depth_ext
        level = jnp.broadcast_to(weights[pl.ds(base + source, 1), :], (SUB, LANES))
        for strip in range(count // SUB):
            weights[pl.ds(base + at + strip * SUB, SUB), :] = level


class Plan:
    def __init__(self, sizes, release, inflow, price, ids, below, order, table, gains, depths, heights, matrix):
        self.sizes, self.matrix = sizes, matrix
        fill_turns(matrix, sizes)
        self.below, self.table, self.gains, self.depths, self.heights = below, table, gains, depths, heights
        self.grid, self.scen = lax.axis_index("grid"), lax.axis_index("scen")
        self.first_row, self.last_row = self.grid == 0, self.grid == sizes.grid_count - 1
        self.first_depth, self.last_depth = self.scen == 0, self.scen == sizes.scen_count - 1
        for value in range(H + 2):
            count = jnp.int32(0)
            for r in range(sizes.releases):
                count = count + (release[0, r] < value).astype(jnp.int32)
            below[value] = count
            below[H + 2 + value] = count
        for r in range(sizes.releases):
            value = release[0, r]
            to = below[H + 2 + value]
            below[H + 2 + value] = to + 1
            order[to] = r
        for extra in range(sizes.releases, sizes.listed):
            order[extra] = 0
        self.inflow_a = [inflow[0, ids[w][0]] for w in range(sizes.scenarios)]
        inflow_b = [inflow[1, ids[w][0]] for w in range(sizes.scenarios)]
        inflow_c = [inflow[2, ids[w][0]] for w in range(sizes.scenarios)]
        sublane = lax.broadcasted_iota(jnp.int32, (SUB, LANES), 0)
        place = sizes.place(lax.broadcasted_iota(jnp.int32, (SUB, LANES), 1))
        row0, depth0 = self.grid * sizes.rows, self.scen * sizes.depth
        spans = (sizes.rows * sizes.grid_count, sizes.width, sizes.depth * sizes.scen_count)
        prices = [price[i] * (1.0 / (spans[i] * H * softness)) for i in range(3)]

        def step(listed, _):
            r = order[listed]
            u1, u2, u3 = release[0, r], release[1, r], release[2, r]
            for w in range(sizes.scenarios):
                at = w * sizes.listed + listed
                plane = LOW + inflow_b[w] + u1 - u2
                shift = inflow_c[w] + u2 - u3
                table[at, SHIFT_A] = self.inflow_a[w] - u1
                table[at, OFFSET] = plane * sizes.depth_ext + LOW + shift
                if sizes.pair:
                    shift = jnp.where(self.first_depth, jnp.maximum(shift, 0), HIGH + jnp.minimum(shift, 0))
                    table[at, EDGE_OFFSET] = plane * sizes.edge_ext + shift
                else:
                    table[at, EDGE_OFFSET] = plane * sizes.edge_ext + LOW + shift
            rate = [prices[i] * u.astype(jnp.float32) for i, u in enumerate((u1, u2, u3))]
            for plane in range(sizes.planes):
                level = (place * sizes.planes + (plane + 1)).astype(jnp.float32)
                gains[pl.ds(pl.multiple_of((listed * sizes.planes + plane) * SUB, SUB), SUB), :] = jnp.exp(level * rate[1])
            listens = jnp.where(listed < sizes.releases, 1.0, 0.0)
            for refs, start, count, which in ((heights, row0, sizes.rows, 0), (depths, depth0, sizes.depth, 2)):
                for strip in range(count // SUB):
                    level = (sublane + (start + strip * SUB + 1)).astype(jnp.float32)
                    refs[pl.ds(pl.multiple_of(listed * count + strip * SUB, SUB), SUB), :] = jnp.exp(level * rate[which]) * listens
            return 0

        lax.fori_loop(0, sizes.listed, step, 0)

    def edge_first(self):
        if self.sizes.pair:
            return jnp.where(self.first_depth, self.sizes.strips - self.sizes.edge_strips, 0)
        return 0

    def put_rows(self, weights, rows, values):
        sizes = self.sizes
        ext = sizes.depth_ext
        bases = [row * sizes.row_size for row in rows]
        put(weights, sizes, self.matrix, bases, ext, LOW, values)
        for is_end, at, count, edge in (
            (self.first_depth, 0, LOW, LOW),
            (self.last_depth, LOW + sizes.depth, HIGH, LOW + sizes.depth - 1),
        ):

            @pl.when(is_end)
            def _():
                for base in bases:
                    repeat(weights, sizes, base, ext, edge, at, count)

            @pl.when(jnp.logical_not(is_end))
            def _():
                for base in bases:
                    put_zeros(weights, sizes, base, ext, at, count)

    def put_edges(self, weights, rows, beyond):
        sizes = self.sizes
        ext = sizes.edge_ext
        bases = [row * sizes.edge_size for row in rows]
        if sizes.pair:
            put(weights, sizes, self.matrix, bases, ext, jnp.where(self.first_depth, HIGH, 0), beyond)
            for base in bases:
                put_zeros(weights, sizes, base, ext, jnp.where(self.first_depth, 0, HIGH), HIGH)
            return
        for base in bases:
            put_zeros(weights, sizes, base, ext, 0, ext)

        @pl.when(jnp.logical_not(self.first_depth))
        def _():
            put(weights, sizes, self.matrix, bases, ext, 0, [row[:, :LOW] for row in beyond])

        @pl.when(jnp.logical_not(self.last_depth))
        def _():
            put(weights, sizes, self.matrix, bases, ext, LOW + sizes.depth, [row[:, LOW:] for row in beyond])

    def gain(self, listed, plane):
        return self.gains[pl.ds(pl.multiple_of((listed * self.sizes.planes + plane) * SUB, SUB), SUB), :]

    def factors(self, row, first, count, listed):
        height = self.heights[pl.ds(listed * self.sizes.rows + row, 1), :]
        return [
            self.depths[pl.ds(pl.multiple_of(listed * self.sizes.depth + (first + strip) * SUB, SUB), SUB), :] * height
            for strip in range(count)
        ]

    def base(self, edge, scenario, source, first, listed):
        at = scenario * self.sizes.listed + listed
        if edge:
            return source * self.sizes.edge_size + self.table[at, EDGE_OFFSET], self.sizes.edge_ext
        return source * self.sizes.row_size + self.table[at, OFFSET] + first * SUB, self.sizes.depth_ext

    def fill_beyond(self, weights, row_size):
        rows = self.sizes.rows
        unroll = 4

        def fill(index, _):
            for k in range(unroll):
                at = pl.multiple_of((index * unroll + k) * SUB, SUB)
                for is_end, to, source in ((self.first_row, 0, 1), (self.last_row, rows + 1, rows)):
                    end = weights[pl.ds(source * row_size + at, SUB), :]
                    weights[pl.ds(to * row_size + at, SUB), :] = end * is_end.astype(jnp.float32)
            return 0

        lax.fori_loop(0, row_size // (SUB * unroll), fill, 0)

    def own_terms(self, load, store, weights, edge, first, strips):
        sizes = self.sizes
        together = 2 if sizes.scenarios % 2 == 0 else 1

        def work(index, _):
            row = index % sizes.rows
            scenarios = [index // sizes.rows * together + i for i in range(together)]
            bases = []
            for listed in range(sizes.releases):
                bases.append([])
                for scenario in scenarios:
                    source = jnp.clip(row + 1 + self.table[scenario * sizes.listed + listed, SHIFT_A], 0, sizes.rows + 1)
                    bases[-1].append(self.base(edge, scenario, source, first, listed))
            for from_strip, count in strip_sets(strips, TILE):
                sums = [load(scenario, row, first + from_strip, count) for scenario in scenarios]
                for listed in range(sizes.releases):
                    factors = self.factors(row, first + from_strip, count, listed)
                    for plane in range(sizes.planes):
                        gain = self.gain(listed, plane)
                        for strip in range(count):
                            weight = gain * factors[strip]
                            at = plane * count + strip
                            for i, (base, ext) in enumerate(bases[listed]):
                                landed = weights[pl.ds(base + plane * ext + (from_strip + strip) * SUB, SUB), :]
                                sums[i][at] = sums[i][at] + landed * weight
                for i, scenario in enumerate(scenarios):
                    store(scenario, row, first + from_strip, count, sums[i], from_strip + count == strips)
            return 0

        lax.fori_loop(0, sizes.scenarios // together * sizes.rows, work, 0)

    def add_outside(self, sums, weights, edge, scenario, row, first, count, listed, shift):
        sizes = self.sizes
        source = jnp.clip(row + self.table[scenario * sizes.listed + listed, SHIFT_A] + shift, 0, 2 * H - 1)
        base, ext = self.base(edge, scenario, source, first, listed)
        factors = self.factors(row, first, count, listed)
        out = []
        for plane in range(sizes.planes):
            gain = self.gain(listed, plane)
            for strip in range(count):
                landed = weights[pl.ds(base + plane * ext + strip * SUB, SUB), :]
                out.append(sums[plane * count + strip] + landed * (gain * factors[strip]))
        return out

    def outside_terms(self, sums_ref, weights, edge, first, count, done=None):
        sizes = self.sizes

        def work(index, _):
            scenario, row = index // sizes.rows, index % sizes.rows
            top = row + self.inflow_a[0]
            for w in range(1, sizes.scenarios):
                top = jnp.where(scenario == w, row + self.inflow_a[w], top)
            start = jnp.where(self.last_row, 0, self.below[jnp.clip(top - sizes.rows + 1, 0, H + 1)])
            stop = jnp.where(self.first_row, sizes.releases, self.below[jnp.clip(top + 1, 0, H + 1)])

            def some(lo, hi, shift):
                @pl.when(lo < hi)
                def _():
                    def step(index, sums):
                        for k in range(UNROLL):
                            listed = lo + index * UNROLL + k
                            listed = jnp.where(listed < hi, listed, sizes.releases)
                            sums = self.add_outside(sums, weights, edge, scenario, row, first, count, listed, shift)
                        return tuple(sums)

                    sums = tuple(load_sums(sums_ref, sizes, scenario, row, first, count))
                    sums = lax.fori_loop(0, (hi - lo + UNROLL - 1) // UNROLL, step, sums)
                    store_sums(sums_ref, sizes, scenario, row, first, count, sums)

            some(0, start, H - sizes.rows)
            some(stop, sizes.releases, H)
            if done is not None:
                done(scenario, row)
            return 0

        lax.fori_loop(0, sizes.scenarios * sizes.rows, work, 0)


def load_sums(ref, sizes, scenario, row, first, count):
    return [
        ref[scenario, row, plane, pl.ds(pl.multiple_of((first + strip) * SUB, SUB), SUB), :]
        for plane in range(sizes.planes)
        for strip in range(count)
    ]


def store_sums(ref, sizes, scenario, row, first, count, sums):
    for plane in range(sizes.planes):
        for strip in range(count):
            ref[scenario, row, plane, pl.ds(pl.multiple_of((first + strip) * SUB, SUB), SUB), :] = sums[plane * count + strip]


def strip_sets(strips, most=4):
    return [(first, min(most, strips - first)) for first in range(0, strips, most)]


def fill_pairs(count, held, fill):
    def step(index, _):
        rows = [2 * index, 2 * index + 1]
        fill(rows, [held[row] for row in rows])
        return 0

    lax.fori_loop(0, count // 2, step, 0)


def planes_kernel(sizes, values, planes_out):
    def step(row, _):
        for strip in range(sizes.strips):
            levels = slice(strip * SUB, strip * SUB + SUB)
            blocks = (
                jnp.exp(values[row, levels, block * LANES : block * LANES + LANES] * (-1.0 / softness))
                for block in range(sizes.planes)
            )
            for plane, each in enumerate(transpose(blocks)):
                planes_out[row, plane, levels, :] = each
        return 0

    lax.fori_loop(0, sizes.rows, step, 0)


def own_kernel(sizes, own, sums_out, release, inflow, price, ids, plan, weights, sums, held, sems):
    copy = pltpu.make_async_copy(own, held, sems.at[0])
    copy.start()
    plan = Plan(sizes, release, inflow, price, ids, *plan)
    copy.wait()
    fill_pairs(sizes.rows, held, lambda rows, values: plan.put_rows(weights, [row + 1 for row in rows], values))
    plan.fill_beyond(weights, sizes.row_size)
    zero = jnp.zeros((SUB, LANES), jnp.float32)

    def store(scenario, row, first, count, values, is_last):
        store_sums(sums, sizes, scenario, row, first, count, values)
        if is_last:
            pltpu.make_async_copy(sums.at[scenario, row], sums_out.at[scenario, row], sems.at[1]).start()

    plan.own_terms(lambda scenario, row, first, count: [zero] * (sizes.planes * count), store, weights, False, 0, sizes.strips)
    pltpu.make_async_copy(sums, sums_out, sems.at[1]).wait()


def edge_kernel(sizes, beyond, before, after, sums_in, sums_out, release, inflow, price, ids, plan, weights, edges, sums, held, rows_held, sems):
    copies = [
        pltpu.make_async_copy(beyond, held, sems.at[0]),
        pltpu.make_async_copy(sums_in, sums, sems.at[1]),
        pltpu.make_async_copy(before, rows_held.at[pl.ds(0, H)], sems.at[2]),
        pltpu.make_async_copy(after, rows_held.at[pl.ds(H, H)], sems.at[3]),
    ]
    for copy in copies:
        copy.start()
    plan = Plan(sizes, release, inflow, price, ids, *plan)
    copies[0].wait()
    fill_pairs(sizes.rows, held, lambda rows, values: plan.put_edges(edges, [row + 1 for row in rows], values))
    plan.fill_beyond(edges, sizes.edge_size)
    copies[1].wait()

    def store(scenario, row, first, count, values, is_last):
        store_sums(sums, sizes, scenario, row, first, count, values)

    plan.own_terms(functools.partial(load_sums, sums, sizes), store, edges, True, plan.edge_first(), sizes.edge_strips)
    copies[2].wait()
    copies[3].wait()
    fill_pairs(2 * H, rows_held, functools.partial(plan.put_rows, weights))
    sets = strip_sets(sizes.strips)

    def done(scenario, row):
        pltpu.make_async_copy(sums.at[scenario, row], sums_out.at[scenario, row], sems.at[4]).start()

    for index, (first, count) in enumerate(sets):
        plan.outside_terms(sums, weights, False, first, count, done if index == len(sets) - 1 else None)
    pltpu.make_async_copy(sums, sums_out, sems.at[4]).wait()


def last_kernel(sizes, scale, before, after, sums_in, average_out, totals_out, release, inflow, price, ids, plan, edges, sums, held, average, sems):
    copies = [
        pltpu.make_async_copy(before, held.at[pl.ds(0, H)], sems.at[0]),
        pltpu.make_async_copy(after, held.at[pl.ds(H, H)], sems.at[1]),
        pltpu.make_async_copy(sums_in, sums, sems.at[2]),
    ]
    for copy in copies:
        copy.start()
    plan = Plan(sizes, release, inflow, price, ids, *plan)
    copies[0].wait()
    copies[1].wait()

    fill_pairs(2 * H, held, functools.partial(plan.put_edges, edges))
    copies[2].wait()
    for first, count in strip_sets(sizes.edge_strips):
        plan.outside_terms(sums, edges, True, plan.edge_first() + first, count)

    def finish(row, total):
        for strip in range(sizes.strips):
            levels = slice(strip * SUB, strip * SUB + SUB)
            averages = []
            for plane in range(sizes.planes):
                logs = None
                for scenario in range(0, sizes.scenarios, 2):
                    product = sums[scenario, row, plane, levels, :]
                    if scenario + 1 < sizes.scenarios:
                        product = product * sums[scenario + 1, row, plane, levels, :]
                    log = jnp.log(product)
                    logs = log if logs is None else logs + log
                averages.append(logs * scale)
                total = total + averages[-1]
            for block, values in enumerate(transpose(averages)):
                average[row, levels, block * LANES : block * LANES + LANES] = values
        pltpu.make_async_copy(average.at[row], average_out.at[row], sems.at[3]).start()
        return total

    total = lax.fori_loop(0, sizes.rows, finish, jnp.zeros((SUB, LANES), jnp.float32))
    total = jnp.sum(total, axis=0, keepdims=True)
    totals_out[...] = jnp.broadcast_to(total[None], totals_out.shape)
    pltpu.make_async_copy(average, average_out, sems.at[3]).wait()


def mean_kernel(sizes, cells, totals, average, out, held, sems):
    chunks = min(4, sizes.rows)
    step = sizes.rows // chunks
    copies = [
        pltpu.make_async_copy(average.at[pl.ds(i * step, step)], held.at[pl.ds(i * step, step)], sems.at[i]) for i in range(chunks)
    ]
    back = [
        pltpu.make_async_copy(held.at[pl.ds(i * step, step)], out.at[pl.ds(i * step, step)], sems.at[chunks + i]) for i in range(chunks)
    ]
    for copy in copies:
        copy.start()
    total = jnp.sum(totals[...], axis=0)
    mean = jnp.sum(total, axis=1, keepdims=True) * (1.0 / cells)
    mean = jnp.broadcast_to(mean, (sizes.depth, sizes.width))
    for i in range(chunks):
        copies[i].wait()
        for row in range(i * step, i * step + step):
            held[row] = held[row] - mean
        back[i].start()
    for copy in back:
        copy.wait()


def call(kernel, sizes, arrays, outs, in_hbm, out_hbm, scalars, scratch):
    smem, vmem, hbm = (pl.BlockSpec(memory_space=space) for space in (pltpu.SMEM, pltpu.VMEM, pl.ANY))
    release, inflow, price, ids = scalars
    count, listed = sizes.scenarios, sizes.listed
    plan = [
        pltpu.SMEM((2 * (H + 2),), jnp.int32),
        pltpu.SMEM((listed,), jnp.int32),
        pltpu.SMEM((count * listed, 3), jnp.int32),
        pltpu.VMEM((listed * sizes.planes * SUB, LANES), jnp.float32),
        pltpu.VMEM((listed * sizes.depth, LANES), jnp.float32),
        pltpu.VMEM((listed * sizes.rows, LANES), jnp.float32),
        pltpu.VMEM((2 * LANES, len(turns(sizes)) * LANES), jnp.bfloat16),
    ]

    def body(*refs):
        ins, refs = refs[: len(arrays)], refs[len(arrays) :]
        scalar_refs, refs = refs[: 3 + count], refs[3 + count :]
        out_refs, refs = refs[: len(outs)], refs[len(outs) :]
        kernel(*ins, *out_refs, *scalar_refs[:3], scalar_refs[3:], refs[: len(plan)], *refs[len(plan) :])

    return pl.pallas_call(
        body,
        out_shape=outs,
        in_specs=[hbm if is_hbm else vmem for is_hbm in in_hbm] + [smem] * (3 + count),
        out_specs=[hbm if is_hbm else vmem for is_hbm in out_hbm],
        scratch_shapes=plan + scratch,
        compiler_params=pltpu.CompilerParams(vmem_limit_bytes=48 * 2**20),
    )(*arrays, release, inflow, price, *ids)


def from_above(cells, axis, hops=1):
    count = lax.axis_size(axis)
    return lax.ppermute(cells, axis, [(i + hops, i) for i in range(count - hops)])


def from_below(cells, axis, hops=1):
    count = lax.axis_size(axis)
    return lax.ppermute(cells, axis, [(i, i + hops) for i in range(count - hops)])


def beyond_levels(own):
    depth = own.shape[2]
    scen_count, scen = lax.axis_size("scen"), lax.axis_index("scen")
    low, high = [], []
    for hop in range(-(-LOW // depth), 0, -1):
        low.append(from_below(own, "scen", hop) if hop < scen_count else jnp.zeros_like(own))
    for hop in range(1, -(-HIGH // depth) + 1):
        high.append(from_above(own, "scen", hop) if hop < scen_count else jnp.zeros_like(own))
    low = jnp.concatenate(low, axis=2)[:, :, -LOW:]
    high = jnp.concatenate(high, axis=2)[:, :, :HIGH]
    for hop in range(1, -(-HIGH // depth)):
        fill = high[:, :, hop * depth - 1 : hop * depth]
        keep = lax.broadcasted_iota(jnp.int32, high.shape, 2) < hop * depth
        high = jnp.where(jnp.logical_or(scen + hop != scen_count - 1, keep), high, fill)
    return jnp.concatenate([low, high], axis=2)


def on_device(value_next, scenario_ids, inflow_table, release_shifts, price):
    rows, depth, width = value_next.shape
    grid_count, scen_count = lax.axis_size("grid"), lax.axis_size("scen")
    scen = lax.axis_index("scen")
    scenarios = scenario_ids.shape[0] * scen_count
    sizes = Sizes(rows, depth, width, scenarios, release_shifts.shape[0], grid_count, scen_count)

    ids = [scenario_ids]
    for hop in range(1, scen_count):
        ids.append(lax.ppermute(scenario_ids, "scen", [(i, (i + hop) % scen_count) for i in range(scen_count)]))
    ids = [each[i : i + 1] for each in ids for i in range(scenario_ids.shape[0])]

    own = pl.pallas_call(
        functools.partial(planes_kernel, sizes),
        out_shape=jax.ShapeDtypeStruct((rows, sizes.planes, depth, LANES), jnp.float32),
        in_specs=[pl.BlockSpec(memory_space=pltpu.VMEM)],
        out_specs=pl.BlockSpec(memory_space=pltpu.VMEM),
    )(value_next)
    own, ids = lax.optimization_barrier((own, ids))
    scalars = (release_shifts.T, inflow_table.T, price, ids)
    if sizes.pair:
        sent = jnp.where(scen == 0, own[:, :, depth - HIGH :], own[:, :, :HIGH])
        beyond = lax.ppermute(sent, "scen", [(0, 1), (1, 0)])
    else:
        beyond = beyond_levels(own)
    before = from_below(own[rows - H :], "grid")
    after = from_above(own[:H], "grid")

    shape = (scenarios, rows, sizes.planes, depth, LANES)
    sums_shape = jax.ShapeDtypeStruct(shape, jnp.float32)
    sums_held = pltpu.VMEM(shape, jnp.float32)
    inside, outside = rows + 2, 2 * H
    (sums,) = call(
        functools.partial(own_kernel, sizes), sizes, (own,), [sums_shape], [True], [True], scalars,
        [
            pltpu.VMEM((inside * sizes.row_size, LANES), jnp.float32), sums_held, pltpu.VMEM(own.shape, jnp.float32),
            pltpu.SemaphoreType.DMA((2,)),
        ],
    )
    beyond, sums = lax.optimization_barrier((beyond, sums))
    corner_before = from_below(beyond[rows - H :], "grid")
    corner_after = from_above(beyond[:H], "grid")
    (sums,) = call(
        functools.partial(edge_kernel, sizes), sizes, (beyond, before, after, sums), [sums_shape], [True] * 4, [True], scalars,
        [
            pltpu.VMEM((outside * sizes.row_size, LANES), jnp.float32), pltpu.VMEM((inside * sizes.edge_size, LANES), jnp.float32),
            sums_held, pltpu.VMEM(beyond.shape, jnp.float32), pltpu.VMEM((2 * H, *own.shape[1:]), jnp.float32),
            pltpu.SemaphoreType.DMA((5,)),
        ],
    )
    scale = -softness / scenarios
    devices = grid_count * scen_count
    average, totals = call(
        functools.partial(last_kernel, sizes, scale), sizes, (corner_before, corner_after, sums),
        [jax.ShapeDtypeStruct(value_next.shape, jnp.float32), jax.ShapeDtypeStruct((devices, 1, LANES), jnp.float32)],
        [True] * 3, [True, False], scalars,
        [
            pltpu.VMEM((outside * sizes.edge_size, LANES), jnp.float32), sums_held, pltpu.VMEM((2 * H, *beyond.shape[1:]), jnp.float32), pltpu.VMEM(value_next.shape, jnp.float32),
            pltpu.SemaphoreType.DMA((4,)),
        ],
    )
    totals = lax.all_to_all(totals, ("scen", "grid"), 0, 0, tiled=True)
    cells = rows * grid_count * depth * scen_count * width
    return pl.pallas_call(
        functools.partial(mean_kernel, sizes, cells),
        out_shape=jax.ShapeDtypeStruct(value_next.shape, jnp.float32),
        in_specs=[pl.BlockSpec(memory_space=pltpu.VMEM), pl.BlockSpec(memory_space=pl.ANY)],
        out_specs=pl.BlockSpec(memory_space=pl.ANY),
        scratch_shapes=[pltpu.VMEM(value_next.shape, jnp.float32), pltpu.SemaphoreType.DMA((8,))],
    )(totals, average)


def solution(mesh):
    placed = (P("grid", "scen", None), P("scen"), P(), P(), P())
    return jax.shard_map(
        on_device, mesh=mesh, in_specs=placed, out_specs=P("grid", "scen", None), check_vma=False
    )
```

```python
import functools

import jax
import jax.numpy as jnp
from jax import lax
from jax.experimental import pallas as pl
from jax.experimental.pallas import tpu as pltpu
from jax.sharding import PartitionSpec as P

H = 8
LOW, HIGH = H, 2 * H
SUB, LANES = 8, 128
TILE = 2
CHUNK = 4
UNROLL = 2
softness = 0.5

ORDER = 0
SHIFT_A, OFFSET, EDGE_OFFSET = range(3)


class Sizes:
    def __init__(self, rows, depth, width, scenarios, releases, grid_count, scen_count):
        self.rows, self.depth, self.width = rows, depth, width
        self.grid_count, self.scen_count = grid_count, scen_count
        self.scenarios, self.releases = scenarios, releases
        self.listed = releases + UNROLL - 1
        self.columns = 1 + 3 * scenarios
        self.far_size = releases + 1 + UNROLL
        self.pieces = [(0, H), (H, rows - 2 * H), (rows - H, H)] if rows > 2 * H else [(0, H), (H, H)] if rows == 2 * H else [(0, rows)]
        self.planes = width // LANES
        self.group = LANES // self.planes
        self.strips = depth // SUB
        self.planes_ext = LOW + self.planes + HIGH
        self.depth_ext = LOW + depth + HIGH
        self.row_size = self.planes_ext * self.depth_ext
        self.pair = scen_count == 2 and depth >= HIGH
        self.edge_strips = HIGH // SUB if self.pair else self.strips
        self.edge_ext = 2 * HIGH if self.pair else self.depth_ext
        self.edge_size = self.planes_ext * self.edge_ext

    def place(self, lane):
        return lane % self.planes * self.group + lane // self.planes

    def lane(self, place):
        return place % self.group * self.planes + place // self.group


def transpose(blocks):
    lane = lax.broadcasted_iota(jnp.int32, (SUB, LANES), 1)
    blocks = [pltpu.roll(block, k, 1) if k else block for k, block in enumerate(blocks)]
    count = len(blocks)
    step = 1
    while step < count:
        odd = (lane // step) % 2 == 1
        blocks = [jnp.where(odd, blocks[(i + step) % count], blocks[i]) for i in range(count)]
        step *= 2
    return [pltpu.roll(blocks[-j % count], LANES - j, 1) if j else blocks[0] for j in range(count)]


def turns(sizes):
    return [*range(-(-(-LOW // sizes.planes)), 0), *range(1, -(-HIGH // sizes.planes) + 1)]


def fill_turns(matrix, sizes):
    shape = (2 * LANES, LANES)
    source = lax.broadcasted_iota(jnp.int32, shape, 0) % LANES
    place = sizes.place(lax.broadcasted_iota(jnp.int32, shape, 1))
    for i, turn in enumerate(turns(sizes)):
        there = jnp.clip(place + turn, 0, LANES - 1)
        matrix[:, i * LANES : i * LANES + LANES] = (sizes.lane(there) == source).astype(jnp.float32).astype(jnp.bfloat16)


def put(weights, sizes, matrix, row_bases, depth_ext, at, rows):
    place = sizes.place(lax.broadcasted_iota(jnp.int32, (SUB, LANES), 1))
    levels = rows[0].shape[1]
    both = jnp.concatenate([row.reshape(sizes.planes * levels, LANES) for row in rows], axis=0)
    upper = both.astype(jnp.bfloat16)
    lower = (both - upper.astype(jnp.float32)).astype(jnp.bfloat16)
    turned = jnp.dot(jnp.concatenate([upper, lower], axis=1), matrix[...], preferred_element_type=jnp.float32)
    for row, row_base in enumerate(row_bases):
        for strip in range(levels // SUB):
            base = row_base + at + strip * SUB

            def part(array, plane):
                first = (row * sizes.planes + plane) * levels + strip * SUB
                return array[first : first + SUB]

            for plane in range(sizes.planes):
                weights[pl.ds(base + (LOW + plane) * depth_ext, SUB), :] = part(both, plane)
            for i, turn in enumerate(turns(sizes)):
                moved = turned[:, i * LANES : i * LANES + LANES]
                end = part(moved, sizes.planes - 1 if turn > 0 else 0)
                past = place + turn > LANES - 1 if turn > 0 else place + turn < 0
                for plane in range(sizes.planes):
                    to = LOW + turn * sizes.planes + plane
                    if 0 <= to < sizes.planes_ext:
                        weights[pl.ds(base + to * depth_ext, SUB), :] = jnp.where(past, end, part(moved, plane))


def put_zeros(weights, sizes, row_base, depth_ext, at, count):
    zero = jnp.zeros((SUB, LANES), jnp.float32)
    for strip in range(count // SUB):
        for plane in range(sizes.planes_ext):
            weights[pl.ds(row_base + plane * depth_ext + at + strip * SUB, SUB), :] = zero


def repeat(weights, sizes, row_base, depth_ext, source, at, count):
    for plane in range(sizes.planes_ext):
        base = row_base + plane * depth_ext
        level = jnp.broadcast_to(weights[pl.ds(base + source, 1), :], (SUB, LANES))
        for strip in range(count // SUB):
            weights[pl.ds(base + at + strip * SUB, SUB), :] = level


def make_lists(sizes, release, inflow, ids, below, table, far):
    first_depth = lax.axis_index("scen") == 0
    inflow_a, inflow_b, inflow_c = ([inflow[i, ids[w][0]] for w in range(sizes.scenarios)] for i in range(3))
    for value in range(H + 2):
        count = jnp.int32(0)
        for r in range(sizes.releases):
            count = count + (release[0, r] < value).astype(jnp.int32)
        below[value] = count
        below[H + 2 + value] = count
    for w in range(sizes.scenarios):
        below[2 * (H + 2) + w] = inflow_a[w]
    for r in range(sizes.releases):
        value = release[0, r]
        to = below[H + 2 + value]
        below[H + 2 + value] = to + 1
        table[sizes.columns * to + ORDER] = r
    for extra in range(sizes.releases, sizes.listed):
        table[sizes.columns * extra + ORDER] = 0

    def step(listed, counts):
        r = table[sizes.columns * listed + ORDER]
        u1, u2, u3 = release[0, r], release[1, r], release[2, r]
        out = []
        for w in range(sizes.scenarios):
            at = sizes.columns * listed + 1 + 3 * w
            plane = LOW + inflow_b[w] + u1 - u2
            shift = inflow_c[w] + u2 - u3
            table[at + SHIFT_A] = inflow_a[w] - u1
            table[at + OFFSET] = plane * sizes.depth_ext + LOW + shift
            far[w * sizes.far_size + 1 + counts[w]] = listed
            reaches = jnp.logical_and(jnp.logical_and(first_depth, shift > SUB), listed < sizes.releases)
            out.append(counts[w] + reaches.astype(jnp.int32))
            if sizes.pair:
                shift = jnp.where(first_depth, jnp.maximum(shift, 0), HIGH + jnp.minimum(shift, 0))
                table[at + EDGE_OFFSET] = plane * sizes.edge_ext + shift
            else:
                table[at + EDGE_OFFSET] = plane * sizes.edge_ext + LOW + shift
        return tuple(out)

    counts = lax.fori_loop(0, sizes.listed, step, tuple(jnp.int32(0) for _ in range(sizes.scenarios)))
    for w in range(sizes.scenarios):
        far[w * sizes.far_size] = counts[w]
        far[w * sizes.far_size + 1 + counts[w]] = sizes.releases


def make_factors(sizes, release, price, table, gains, depths, heights):
    sublane = lax.broadcasted_iota(jnp.int32, (SUB, LANES), 0)
    place = sizes.place(lax.broadcasted_iota(jnp.int32, (SUB, LANES), 1))
    row0, depth0 = lax.axis_index("grid") * sizes.rows, lax.axis_index("scen") * sizes.depth
    spans = (sizes.rows * sizes.grid_count, sizes.width, sizes.depth * sizes.scen_count)
    prices = [price[i] * (1.0 / (spans[i] * H * softness)) for i in range(3)]

    def step(listed, _):
        r = table[sizes.columns * listed + ORDER]
        rate = [prices[i] * release[i, r].astype(jnp.float32) for i in range(3)]
        for plane in range(sizes.planes):
            level = (place * sizes.planes + (plane + 1)).astype(jnp.float32)
            gains[pl.ds(pl.multiple_of((listed * sizes.planes + plane) * SUB, SUB), SUB), :] = jnp.exp(level * rate[1])
        listens = jnp.where(listed < sizes.releases, 1.0, 0.0)
        for refs, start, count, which in ((heights, row0, sizes.rows, 0), (depths, depth0, sizes.depth, 2)):
            for strip in range(count // SUB):
                level = (sublane + (start + strip * SUB + 1)).astype(jnp.float32)
                refs[pl.ds(pl.multiple_of(listed * count + strip * SUB, SUB), SUB), :] = jnp.exp(level * rate[which]) * listens
        return 0

    lax.fori_loop(0, sizes.listed, step, 0)


class Plan:
    def __init__(self, sizes, below, table, far, factors, matrix):
        self.sizes, self.below, self.table, self.far, self.matrix = sizes, below, table, far, matrix
        self.gains, self.depths, self.heights = factors
        grid, scen = lax.axis_index("grid"), lax.axis_index("scen")
        self.first_row, self.last_row = grid == 0, grid == sizes.grid_count - 1
        self.first_depth, self.last_depth = scen == 0, scen == sizes.scen_count - 1
        fill_turns(matrix, sizes)

    def entry(self, scenario, listed, column):
        return self.table[self.sizes.columns * listed + 1 + 3 * scenario + column]

    def edge_first(self):
        if self.sizes.pair:
            return jnp.where(self.first_depth, self.sizes.strips - self.sizes.edge_strips, 0)
        return 0

    def put_rows(self, weights, rows, values):
        sizes = self.sizes
        ext = sizes.depth_ext
        bases = [row * sizes.row_size for row in rows]
        put(weights, sizes, self.matrix, bases, ext, LOW, values)
        for is_end, at, count, edge in (
            (self.first_depth, 0, LOW, LOW),
            (self.last_depth, LOW + sizes.depth, HIGH, LOW + sizes.depth - 1),
        ):

            @pl.when(is_end)
            def _():
                for base in bases:
                    repeat(weights, sizes, base, ext, edge, at, count)

            @pl.when(jnp.logical_not(is_end))
            def _():
                for base in bases:
                    put_zeros(weights, sizes, base, ext, at, count)

    def put_edges(self, weights, rows, beyond):
        sizes = self.sizes
        ext = sizes.edge_ext
        bases = [row * sizes.edge_size for row in rows]
        if sizes.pair:
            put(weights, sizes, self.matrix, bases, ext, jnp.where(self.first_depth, HIGH, 0), beyond)
            for base in bases:
                put_zeros(weights, sizes, base, ext, jnp.where(self.first_depth, 0, HIGH), HIGH)
            return
        for base in bases:
            put_zeros(weights, sizes, base, ext, 0, ext)

        @pl.when(jnp.logical_not(self.first_depth))
        def _():
            put(weights, sizes, self.matrix, bases, ext, 0, [row[:, :LOW] for row in beyond])

        @pl.when(jnp.logical_not(self.last_depth))
        def _():
            put(weights, sizes, self.matrix, bases, ext, LOW + sizes.depth, [row[:, LOW:] for row in beyond])

    def gain(self, listed, plane):
        return self.gains[pl.ds(pl.multiple_of((listed * self.sizes.planes + plane) * SUB, SUB), SUB), :]

    def factors(self, row, first, count, listed):
        height = self.heights[pl.ds(listed * self.sizes.rows + row, 1), :]
        return [
            self.depths[pl.ds(pl.multiple_of(listed * self.sizes.depth + (first + strip) * SUB, SUB), SUB), :] * height
            for strip in range(count)
        ]

    def base(self, edge, scenario, source, first, listed):
        if edge:
            return source * self.sizes.edge_size + self.entry(scenario, listed, EDGE_OFFSET), self.sizes.edge_ext
        return source * self.sizes.row_size + self.entry(scenario, listed, OFFSET) + first * SUB, self.sizes.depth_ext

    def fill_beyond(self, weights, row_size):
        rows = self.sizes.rows
        unroll = 4

        def fill(index, _):
            for k in range(unroll):
                at = pl.multiple_of((index * unroll + k) * SUB, SUB)
                for is_end, to, source in ((self.first_row, 0, 1), (self.last_row, rows + 1, rows)):
                    end = weights[pl.ds(source * row_size + at, SUB), :]
                    weights[pl.ds(to * row_size + at, SUB), :] = end * is_end.astype(jnp.float32)
            return 0

        lax.fori_loop(0, row_size // (SUB * unroll), fill, 0)

    def far_terms(self, sums_ref, edges):
        sizes = self.sizes
        strip = sizes.strips - 2
        together = 2 if sizes.rows % 2 == 0 else 1

        def scenario_terms(scenario, _):
            count = self.far[scenario * sizes.far_size]

            def work(index, _):
                rows = [index * together + i for i in range(together)]

                def step(index, sums):
                    sums = [list(each) for each in sums]
                    for k in range(UNROLL):
                        listed = self.far[scenario * sizes.far_size + 1 + index * UNROLL + k]
                        lands = self.entry(scenario, listed, SHIFT_A) + 1
                        for i, row in enumerate(rows):
                            source = jnp.clip(row + lands, 0, sizes.rows + 1)
                            sums[i] = self.add_release(sums[i], edges, True, scenario, row, strip, 1, listed, source)
                    return tuple(tuple(each) for each in sums)

                sums = tuple(tuple(load_sums(sums_ref, sizes, scenario, row, strip, 1)) for row in rows)
                sums = lax.fori_loop(0, (count + UNROLL - 1) // UNROLL, step, sums)
                for row, each in zip(rows, sums, strict=True):
                    store_sums(sums_ref, sizes, scenario, row, strip, 1, each)
                return 0

            @pl.when(count > 0)
            def _():
                lax.fori_loop(0, sizes.rows // together, work, 0)

            return 0

        lax.fori_loop(0, sizes.scenarios, scenario_terms, 0)

    def own_terms(self, load, store, weights, edge, first, strips, shift=0, chunk=None):
        sizes = self.sizes
        together = 2 if sizes.scenarios % 2 == 0 else 1

        def work(index, _):
            row = index % sizes.rows
            scenarios = [index // sizes.rows * together + i for i in range(together)]

            def find(listed):
                found = []
                for scenario in scenarios:
                    source = jnp.clip(row + 1 + self.entry(scenario, listed, SHIFT_A), 0, sizes.rows + 1)
                    base, ext = self.base(edge, scenario, source, first, listed)
                    found.append((base + shift, ext))
                return found

            def add(sums, from_strip, count, listed, bases):
                factors = self.factors(row, first + from_strip, count, listed)
                for plane in range(sizes.planes):
                    gain = self.gain(listed, plane)
                    for strip in range(count):
                        weight = gain * factors[strip]
                        at = plane * count + strip
                        for i, (base, ext) in enumerate(bases):
                            landed = weights[pl.ds(base + plane * ext + (from_strip + strip) * SUB, SUB), :]
                            sums[i][at] = sums[i][at] + landed * weight

            bases = None if chunk else [find(listed) for listed in range(sizes.releases)]
            for from_strip, count in strip_sets(strips, TILE):
                sums = [load(scenario, row, first + from_strip, count) for scenario in scenarios]
                if chunk:

                    def step(index, sums):
                        sums = [list(each) for each in sums]
                        for k in range(chunk):
                            add(sums, from_strip, count, index * chunk + k, find(index * chunk + k))
                        return tuple(tuple(each) for each in sums)

                    sums = lax.fori_loop(0, sizes.releases // chunk, step, tuple(tuple(each) for each in sums))
                else:
                    for listed in range(sizes.releases):
                        add(sums, from_strip, count, listed, bases[listed])
                for i, scenario in enumerate(scenarios):
                    store(scenario, row, first + from_strip, count, sums[i], from_strip + count == strips)
            return 0

        lax.fori_loop(0, sizes.scenarios // together * sizes.rows, work, 0)

    def add_release(self, sums, weights, edge, scenario, row, first, count, listed, source):
        sizes = self.sizes
        base, ext = self.base(edge, scenario, source, first, listed)
        factors = self.factors(row, first, count, listed)
        out = []
        for plane in range(sizes.planes):
            gain = self.gain(listed, plane)
            for strip in range(count):
                landed = weights[pl.ds(base + plane * ext + strip * SUB, SUB), :]
                out.append(sums[plane * count + strip] + landed * (gain * factors[strip]))
        return out

    def outside_terms(self, sums_ref, weights, edge, first, count, done=None):
        sizes = self.sizes

        def work(index, _):
            scenario, row = index // sizes.rows, index % sizes.rows
            top = row + self.below[2 * (H + 2) + scenario]
            start = jnp.where(self.last_row, 0, self.below[jnp.clip(top - sizes.rows + 1, 0, H + 1)])
            stop = jnp.where(self.first_row, sizes.releases, self.below[jnp.clip(top + 1, 0, H + 1)])

            def some(lo, hi, shift):
                @pl.when(lo < hi)
                def _():
                    def step(index, sums):
                        for k in range(UNROLL):
                            listed = lo + index * UNROLL + k
                            listed = jnp.where(listed < hi, listed, sizes.releases)
                            source = row + self.entry(scenario, listed, SHIFT_A) + shift
                            source = jnp.clip(source, 0, 2 * H - 1)
                            sums = self.add_release(sums, weights, edge, scenario, row, first, count, listed, source)
                        return tuple(sums)

                    sums = tuple(load_sums(sums_ref, sizes, scenario, row, first, count))
                    sums = lax.fori_loop(0, (hi - lo + UNROLL - 1) // UNROLL, step, sums)
                    store_sums(sums_ref, sizes, scenario, row, first, count, sums)

            if sizes.rows >= 2 * H:
                low = row < H
                some(jnp.where(low, stop, 0), jnp.where(low, sizes.releases, start), jnp.where(low, H, H - sizes.rows))
            else:
                some(0, start, H - sizes.rows)
                some(stop, sizes.releases, H)
            if done is not None:
                done(scenario, row)
            return 0

        lax.fori_loop(0, sizes.scenarios * sizes.rows, work, 0)


def load_sums(ref, sizes, scenario, row, first, count):
    return [
        ref[scenario, row, plane, pl.ds(pl.multiple_of((first + strip) * SUB, SUB), SUB), :]
        for plane in range(sizes.planes)
        for strip in range(count)
    ]


def store_sums(ref, sizes, scenario, row, first, count, sums):
    for plane in range(sizes.planes):
        for strip in range(count):
            ref[scenario, row, plane, pl.ds(pl.multiple_of((first + strip) * SUB, SUB), SUB), :] = sums[plane * count + strip]


def strip_sets(strips, most=4):
    return [(first, min(most, strips - first)) for first in range(0, strips, most)]


def fill_pairs(count, held, fill):
    def step(index, _):
        rows = [2 * index, 2 * index + 1]
        fill(rows, [held[row] for row in rows])
        return 0

    lax.fori_loop(0, count // 2, step, 0)


def planes_kernel(sizes, values, *refs):
    outs, (held, planes_held, sems) = refs[:-3], refs[-3:]
    size = 4 if all(count % 4 == 0 for _, count in sizes.pieces) else 1
    copies = [
        pltpu.make_async_copy(values.at[pl.ds(row, size)], held.at[pl.ds(row, size)], sems.at[i])
        for i, row in enumerate(range(0, sizes.rows, size))
    ]
    for copy in copies:
        copy.start()
    start = pl.multiple_of(jnp.where(lax.axis_index("scen") == 0, sizes.depth - HIGH, 0), SUB) if sizes.pair else None
    sent_sem, first_sem = sems.at[len(copies)], len(copies) + 1

    def step(row, _):
        for strip in range(sizes.strips):
            levels = slice(strip * SUB, strip * SUB + SUB)
            blocks = (
                jnp.exp(held[row, levels, block * LANES : block * LANES + LANES] * (-1.0 / softness))
                for block in range(sizes.planes)
            )
            for plane, each in enumerate(transpose(blocks)):
                planes_held[row, plane, levels, :] = each
        if sizes.pair:
            pltpu.make_async_copy(planes_held.at[row, :, pl.ds(start, HIGH)], outs[-1].at[row], sent_sem).start()
        return 0

    pieces = []
    for i, (first, count) in enumerate(sizes.pieces):
        for row in range(first, first + count, size):
            copies[row // size].wait()
            lax.fori_loop(row, row + size, step, 0)
        pieces.append(pltpu.make_async_copy(planes_held.at[pl.ds(first, count)], outs[i], sems.at[first_sem + i]))
        pieces[-1].start()
    if sizes.pair:
        pltpu.make_async_copy(planes_held.at[:, :, pl.ds(start, HIGH)], outs[-1], sent_sem).wait()
    for piece in pieces:
        piece.wait()


def own_kernel(sizes, *refs):
    own, refs = refs[: len(sizes.pieces)], refs[len(sizes.pieces) :]
    release, inflow, price, ids, sums_out, gains_out, depths_out, heights_out, below, table, far, factors, matrix, *refs = refs
    weights, sums, held, sems = refs
    copies = [
        pltpu.make_async_copy(piece, held.at[pl.ds(first, count)], sems.at[5 + i])
        for i, (piece, (first, count)) in enumerate(zip(own, sizes.pieces, strict=True))
    ]
    for copy in copies:
        copy.start()
    make_lists(sizes, release, inflow, ids, below, table, far)
    make_factors(sizes, release, price, table, *factors)
    backs = [
        pltpu.make_async_copy(ref, out, sems.at[2 + i])
        for i, (ref, out) in enumerate(zip(factors, (gains_out, depths_out, heights_out), strict=True))
    ]
    for back in backs:
        back.start()
    plan = Plan(sizes, below, table, far, factors, matrix)
    for copy in copies:
        copy.wait()
    fill_pairs(sizes.rows, held, lambda rows, values: plan.put_rows(weights, [row + 1 for row in rows], values))
    plan.fill_beyond(weights, sizes.row_size)
    zero = jnp.zeros((SUB, LANES), jnp.float32)

    def store(scenario, row, first, count, values, is_last):
        store_sums(sums, sizes, scenario, row, first, count, values)
        if is_last:
            pltpu.make_async_copy(sums.at[scenario, row], sums_out.at[scenario, row], sems.at[1]).start()

    chunk = CHUNK if sizes.releases % CHUNK == 0 else None
    plan.own_terms(lambda scenario, row, first, count: [zero] * (sizes.planes * count), store, weights, False, 0, sizes.strips, 0, chunk)
    for back in backs:
        back.wait()
    pltpu.make_async_copy(sums, sums_out, sems.at[1]).wait()


def start_copies(refs, held, sems):
    copies = [pltpu.make_async_copy(ref, to, sems.at[i]) for i, (ref, to) in enumerate(zip(refs, held, strict=True))]
    for copy in copies:
        copy.start()
    return copies


def edge_kernel(
    sizes, beyond, before, after, sums_in, gains, depths, heights, below, table, far, sums_out, factors, matrix, weights, edges, sums, held,
    rows_held, sems,
):
    copies = [
        pltpu.make_async_copy(beyond, held, sems.at[0]),
        pltpu.make_async_copy(sums_in, sums, sems.at[1]),
        pltpu.make_async_copy(before, rows_held.at[pl.ds(0, H)], sems.at[2]),
        pltpu.make_async_copy(after, rows_held.at[pl.ds(H, H)], sems.at[3]),
    ]
    for copy in copies:
        copy.start()
    copies += start_copies((gains, depths, heights), factors, sems.at[pl.ds(5, 3)])
    plan = Plan(sizes, below, table, far, factors, matrix)
    copies[0].wait()
    fill_pairs(sizes.rows, held, lambda rows, values: plan.put_edges(edges, [row + 1 for row in rows], values))
    plan.fill_beyond(edges, sizes.edge_size)
    for copy in (copies[1], *copies[4:]):
        copy.wait()

    def store(scenario, row, first, count, values, is_last):
        store_sums(sums, sizes, scenario, row, first, count, values)

    load = functools.partial(load_sums, sums, sizes)
    if sizes.pair:
        near = jnp.where(plan.first_depth, sizes.strips - 1, 0)
        shift = jnp.where(plan.first_depth, HIGH - SUB, 0)
        plan.own_terms(load, store, edges, True, near, 1, shift, CHUNK if sizes.releases % CHUNK == 0 else None)
        plan.far_terms(sums, edges)
    else:
        plan.own_terms(load, store, edges, True, 0, sizes.edge_strips)
    copies[2].wait()
    copies[3].wait()
    fill_pairs(2 * H, rows_held, functools.partial(plan.put_rows, weights))
    sets = strip_sets(sizes.strips)

    def done(scenario, row):
        pltpu.make_async_copy(sums.at[scenario, row], sums_out.at[scenario, row], sems.at[4]).start()

    for index, (first, count) in enumerate(sets):
        plan.outside_terms(sums, weights, False, first, count, done if index == len(sets) - 1 else None)
    pltpu.make_async_copy(sums, sums_out, sems.at[4]).wait()


def last_kernel(
    sizes, scale, before, after, sums_in, gains, depths, heights, below, table, far, average_out, totals_out, factors, matrix, edges, sums,
    held, average, sems,
):
    copies = [
        pltpu.make_async_copy(before, held.at[pl.ds(0, H)], sems.at[0]),
        pltpu.make_async_copy(after, held.at[pl.ds(H, H)], sems.at[1]),
        pltpu.make_async_copy(sums_in, sums, sems.at[2]),
    ]
    for copy in copies:
        copy.start()
    copies += start_copies((gains, depths, heights), factors, sems.at[pl.ds(4, 3)])
    plan = Plan(sizes, below, table, far, factors, matrix)
    copies[0].wait()
    copies[1].wait()

    fill_pairs(2 * H, held, functools.partial(plan.put_edges, edges))
    for copy in copies[2:]:
        copy.wait()
    for first, count in strip_sets(sizes.edge_strips):
        plan.outside_terms(sums, edges, True, plan.edge_first() + first, count)

    def finish(index, total):
        for row in (2 * index, 2 * index + 1):
            for strip in range(sizes.strips):
                levels = slice(strip * SUB, strip * SUB + SUB)
                averages = []
                for plane in range(sizes.planes):
                    logs = None
                    for scenario in range(0, sizes.scenarios, 2):
                        product = sums[scenario, row, plane, levels, :]
                        if scenario + 1 < sizes.scenarios:
                            product = product * sums[scenario + 1, row, plane, levels, :]
                        log = jnp.log(product)
                        logs = log if logs is None else logs + log
                    averages.append(logs * scale)
                    total = total + averages[-1]
                for block, values in enumerate(transpose(averages)):
                    average[row, levels, block * LANES : block * LANES + LANES] = values
            pltpu.make_async_copy(average.at[row], average_out.at[row], sems.at[3]).start()
        return total

    total = lax.fori_loop(0, sizes.rows // 2, finish, jnp.zeros((SUB, LANES), jnp.float32))
    total = jnp.sum(total, axis=0, keepdims=True)
    totals_out[...] = jnp.broadcast_to(total[None], totals_out.shape)
    pltpu.make_async_copy(average, average_out, sems.at[3]).wait()


def mean_kernel(sizes, cells, totals, average, out, held, sems):
    chunks = min(8, sizes.rows)
    step = sizes.rows // chunks
    copies = [
        pltpu.make_async_copy(average.at[pl.ds(i * step, step)], held.at[pl.ds(i * step, step)], sems.at[i]) for i in range(chunks)
    ]
    back = [
        pltpu.make_async_copy(held.at[pl.ds(i * step, step)], out.at[pl.ds(i * step, step)], sems.at[chunks + i]) for i in range(chunks)
    ]
    for copy in copies:
        copy.start()
    total = jnp.sum(totals[...], axis=0)
    mean = jnp.sum(total, axis=1, keepdims=True) * (1.0 / cells)
    mean = jnp.broadcast_to(mean, (sizes.depth, sizes.width))
    for i in range(chunks):
        copies[i].wait()
        for row in range(i * step, i * step + step):
            held[row] = held[row] - mean
        back[i].start()
    for copy in back:
        copy.wait()


SMEM, VMEM, HBM, ANY = (pl.BlockSpec(memory_space=space) for space in (pltpu.SMEM, pltpu.VMEM, pltpu.HBM, pl.ANY))


def call(kernel, sizes, arrays, scalars, outs, out_specs, scratch):
    listed = sizes.listed
    factors = [(listed * sizes.planes * SUB, LANES), (listed * sizes.depth, LANES), (listed * sizes.rows, LANES)]
    factors = [pltpu.VMEM(shape, jnp.float32) for shape in factors]
    matrix = pltpu.VMEM((2 * LANES, len(turns(sizes)) * LANES), jnp.bfloat16)
    flat, tree = jax.tree.flatten(scalars)

    def body(*refs):
        ins, refs = refs[: len(arrays)], refs[len(arrays) :]
        scalar_refs, refs = jax.tree.unflatten(tree, refs[: len(flat)]), refs[len(flat) :]
        out_refs, refs = refs[: len(outs)], refs[len(outs) :]
        kernel(*ins, *scalar_refs, *out_refs, refs[: len(factors)], *refs[len(factors) :])

    return pl.pallas_call(
        body,
        out_shape=outs,
        in_specs=[ANY] * len(arrays) + [SMEM] * len(flat),
        out_specs=out_specs,
        scratch_shapes=[*factors, matrix, *scratch],
        compiler_params=pltpu.CompilerParams(vmem_limit_bytes=61 * 2**20),
    )(*arrays, *flat)


def from_above(cells, axis, hops=1):
    count = lax.axis_size(axis)
    return lax.ppermute(cells, axis, [(i + hops, i) for i in range(count - hops)])


def from_below(cells, axis, hops=1):
    count = lax.axis_size(axis)
    return lax.ppermute(cells, axis, [(i, i + hops) for i in range(count - hops)])


def beyond_levels(own):
    depth = own.shape[2]
    scen_count, scen = lax.axis_size("scen"), lax.axis_index("scen")
    low, high = [], []
    for hop in range(-(-LOW // depth), 0, -1):
        low.append(from_below(own, "scen", hop) if hop < scen_count else jnp.zeros_like(own))
    for hop in range(1, -(-HIGH // depth) + 1):
        high.append(from_above(own, "scen", hop) if hop < scen_count else jnp.zeros_like(own))
    low = jnp.concatenate(low, axis=2)[:, :, -LOW:]
    high = jnp.concatenate(high, axis=2)[:, :, :HIGH]
    for hop in range(1, -(-HIGH // depth)):
        fill = high[:, :, hop * depth - 1 : hop * depth]
        keep = lax.broadcasted_iota(jnp.int32, high.shape, 2) < hop * depth
        high = jnp.where(jnp.logical_or(scen + hop != scen_count - 1, keep), high, fill)
    return jnp.concatenate([low, high], axis=2)


def on_device(value_next, scenario_ids, inflow_table, release_shifts, price):
    rows, depth, width = value_next.shape
    grid_count, scen_count = lax.axis_size("grid"), lax.axis_size("scen")
    scenarios = scenario_ids.shape[0] * scen_count
    sizes = Sizes(rows, depth, width, scenarios, release_shifts.shape[0], grid_count, scen_count)

    ids = [scenario_ids]
    for hop in range(1, scen_count):
        ids.append(lax.ppermute(scenario_ids, "scen", [(i, (i + hop) % scen_count) for i in range(scen_count)]))
    ids = [each[i : i + 1] for each in ids for i in range(scenario_ids.shape[0])]

    def like(*shape, kind=jnp.float32):
        return jax.ShapeDtypeStruct(shape, kind)

    planes = sizes.planes
    made = [like(count, planes, depth, LANES) for _, count in sizes.pieces]
    if sizes.pair:
        made.append(like(rows, planes, HIGH, LANES))
    made = pl.pallas_call(
        functools.partial(planes_kernel, sizes),
        out_shape=made,
        in_specs=[HBM],
        out_specs=[HBM] * len(made),
        scratch_shapes=[
            pltpu.VMEM(value_next.shape, jnp.float32), pltpu.VMEM((rows, planes, depth, LANES), jnp.float32),
            pltpu.SemaphoreType.DMA((rows + 4,)),
        ],
        compiler_params=pltpu.CompilerParams(vmem_limit_bytes=61 * 2**20),
    )(value_next)
    made, ids = lax.optimization_barrier((made, ids))
    pieces = made[: len(sizes.pieces)]
    scalars = (release_shifts.T, inflow_table.T, price, ids)
    if sizes.pair:
        beyond = lax.ppermute(made[-1], "scen", [(0, 1), (1, 0)])
    else:
        beyond = beyond_levels(jnp.concatenate(pieces, axis=0))
    before = from_below(pieces[-1][-H:], "grid")
    after = from_above(pieces[0][:H], "grid")

    shape = (scenarios, rows, sizes.planes, depth, LANES)
    sums_shape = jax.ShapeDtypeStruct(shape, jnp.float32)
    sums_held = pltpu.VMEM(shape, jnp.float32)
    inside, outside = rows + 2, 2 * H
    listed = sizes.listed
    factors = [like(listed * planes * SUB, LANES), like(listed * depth, LANES), like(listed * rows, LANES)]
    lists = [2 * (H + 2) + scenarios, listed * sizes.columns, scenarios * sizes.far_size]
    lists = [like(size, kind=jnp.int32) for size in lists]
    sums, *factors = call(
        functools.partial(own_kernel, sizes), sizes, pieces, scalars, [sums_shape, *factors, *lists], [HBM] * 4 + [SMEM] * 3,
        [
            pltpu.VMEM((inside * sizes.row_size, LANES), jnp.float32), sums_held,
            pltpu.VMEM((rows, planes, depth, LANES), jnp.float32), pltpu.SemaphoreType.DMA((8,)),
        ],
    )
    factors, lists = factors[:3], factors[3:]
    beyond, sums = lax.optimization_barrier((beyond, sums))
    corner_before = from_below(beyond[rows - H :], "grid")
    corner_after = from_above(beyond[:H], "grid")
    (sums,) = call(
        functools.partial(edge_kernel, sizes), sizes, (beyond, before, after, sums, *factors), lists, [sums_shape], [HBM],
        [
            pltpu.VMEM((outside * sizes.row_size, LANES), jnp.float32), pltpu.VMEM((inside * sizes.edge_size, LANES), jnp.float32),
            sums_held, pltpu.VMEM(beyond.shape, jnp.float32), pltpu.VMEM((2 * H, planes, depth, LANES), jnp.float32),
            pltpu.SemaphoreType.DMA((8,)),
        ],
    )
    scale = -softness / scenarios
    devices = grid_count * scen_count
    average, totals = call(
        functools.partial(last_kernel, sizes, scale), sizes, (corner_before, corner_after, sums, *factors), lists,
        [jax.ShapeDtypeStruct(value_next.shape, jnp.float32), jax.ShapeDtypeStruct((devices, 1, LANES), jnp.float32)],
        [HBM, VMEM],
        [
            pltpu.VMEM((outside * sizes.edge_size, LANES), jnp.float32), sums_held, pltpu.VMEM((2 * H, *beyond.shape[1:]), jnp.float32), pltpu.VMEM(value_next.shape, jnp.float32),
            pltpu.SemaphoreType.DMA((7,)),
        ],
    )
    totals = lax.all_to_all(totals, ("scen", "grid"), 0, 0, tiled=True)
    cells = rows * grid_count * depth * scen_count * width
    return pl.pallas_call(
        functools.partial(mean_kernel, sizes, cells),
        out_shape=jax.ShapeDtypeStruct(value_next.shape, jnp.float32),
        in_specs=[VMEM, HBM],
        out_specs=HBM,
        scratch_shapes=[pltpu.VMEM(value_next.shape, jnp.float32), pltpu.SemaphoreType.DMA((16,))],
        compiler_params=pltpu.CompilerParams(vmem_limit_bytes=61 * 2**20),
    )(totals, average)


def solution(mesh):
    placed = (P("grid", "scen", None), P("scen"), P(), P(), P())
    return jax.shard_map(
        on_device, mesh=mesh, in_specs=placed, out_specs=P("grid", "scen", None), check_vma=False
    )
```

```python
import functools

import jax
import jax.numpy as jnp
from jax import lax
from jax.experimental import pallas as pl
from jax.experimental.pallas import tpu as pltpu
from jax.sharding import PartitionSpec as P

H = 8
LOW, HIGH = H, 2 * H
SUB, LANES = 8, 128
TILE = 2
CHUNK = 4
FILL = 8
UNROLL = 2
softness = 0.5

ORDER = 0
SHIFT_A, OFFSET, EDGE_OFFSET = range(3)


class Sizes:
    def __init__(self, rows, depth, width, scenarios, releases, grid_count, scen_count):
        self.rows, self.depth, self.width = rows, depth, width
        self.grid_count, self.scen_count = grid_count, scen_count
        self.scenarios, self.releases = scenarios, releases
        self.listed = releases + UNROLL - 1
        self.columns = 1 + 3 * scenarios
        self.far_size = releases + 1 + UNROLL
        self.pieces = [(0, H), (H, rows - 2 * H), (rows - H, H)] if rows > 2 * H else [(0, H), (H, H)] if rows == 2 * H else [(0, rows)]
        self.planes = width // LANES
        self.group = LANES // self.planes
        self.strips = depth // SUB
        self.planes_ext = LOW + self.planes + HIGH
        self.depth_ext = LOW + depth + HIGH
        self.row_size = self.planes_ext * self.depth_ext
        self.pair = scen_count == 2 and depth >= HIGH
        self.edge_strips = HIGH // SUB if self.pair else self.strips
        self.edge_ext = 2 * HIGH if self.pair else self.depth_ext
        self.edge_size = self.planes_ext * self.edge_ext

    def place(self, lane):
        return lane % self.planes * self.group + lane // self.planes

    def lane(self, place):
        return place % self.group * self.planes + place // self.group


def transpose(blocks):
    lane = lax.broadcasted_iota(jnp.int32, (SUB, LANES), 1)
    blocks = [pltpu.roll(block, k, 1) if k else block for k, block in enumerate(blocks)]
    count = len(blocks)
    step = 1
    while step < count:
        odd = (lane // step) % 2 == 1
        blocks = [jnp.where(odd, blocks[(i + step) % count], blocks[i]) for i in range(count)]
        step *= 2
    return [pltpu.roll(blocks[-j % count], LANES - j, 1) if j else blocks[0] for j in range(count)]


def turns(sizes):
    return [*range(-(-(-LOW // sizes.planes)), 0), *range(1, -(-HIGH // sizes.planes) + 1)]


def fill_turns(matrix, sizes):
    shape = (2 * LANES, LANES)
    source = lax.broadcasted_iota(jnp.int32, shape, 0) % LANES
    place = sizes.place(lax.broadcasted_iota(jnp.int32, shape, 1))
    for i, turn in enumerate(turns(sizes)):
        there = jnp.clip(place + turn, 0, LANES - 1)
        matrix[:, i * LANES : i * LANES + LANES] = (sizes.lane(there) == source).astype(jnp.float32).astype(jnp.bfloat16)


def put(weights, sizes, matrix, row_bases, depth_ext, at, rows):
    place = sizes.place(lax.broadcasted_iota(jnp.int32, (SUB, LANES), 1))
    levels = rows[0].shape[1]
    both = jnp.concatenate([row.reshape(sizes.planes * levels, LANES) for row in rows], axis=0)
    upper = both.astype(jnp.bfloat16)
    lower = (both - upper.astype(jnp.float32)).astype(jnp.bfloat16)
    turned = jnp.dot(jnp.concatenate([upper, lower], axis=1), matrix[...], preferred_element_type=jnp.float32)
    for row, row_base in enumerate(row_bases):
        for strip in range(levels // SUB):
            base = row_base + at + strip * SUB

            def part(array, plane):
                first = (row * sizes.planes + plane) * levels + strip * SUB
                return array[first : first + SUB]

            for plane in range(sizes.planes):
                weights[pl.ds(base + (LOW + plane) * depth_ext, SUB), :] = part(both, plane)
            for i, turn in enumerate(turns(sizes)):
                moved = turned[:, i * LANES : i * LANES + LANES]
                end = part(moved, sizes.planes - 1 if turn > 0 else 0)
                past = place + turn > LANES - 1 if turn > 0 else place + turn < 0
                for plane in range(sizes.planes):
                    to = LOW + turn * sizes.planes + plane
                    if 0 <= to < sizes.planes_ext:
                        weights[pl.ds(base + to * depth_ext, SUB), :] = jnp.where(past, end, part(moved, plane))


def put_zeros(weights, sizes, row_base, depth_ext, at, count):
    zero = jnp.zeros((SUB, LANES), jnp.float32)
    for strip in range(count // SUB):
        for plane in range(sizes.planes_ext):
            weights[pl.ds(row_base + plane * depth_ext + at + strip * SUB, SUB), :] = zero


def repeat(weights, sizes, row_base, depth_ext, source, at, count):
    for plane in range(sizes.planes_ext):
        base = row_base + plane * depth_ext
        level = jnp.broadcast_to(weights[pl.ds(base + source, 1), :], (SUB, LANES))
        for strip in range(count // SUB):
            weights[pl.ds(base + at + strip * SUB, SUB), :] = level


def make_lists(sizes, release, inflow, ids, below, table, far):
    first_depth = lax.axis_index("scen") == 0
    inflow_a, inflow_b, inflow_c = ([inflow[i, ids[w][0]] for w in range(sizes.scenarios)] for i in range(3))
    for value in range(H + 2):
        count = jnp.int32(0)
        for r in range(sizes.releases):
            count = count + (release[0, r] < value).astype(jnp.int32)
        below[value] = count
        below[H + 2 + value] = count
    for w in range(sizes.scenarios):
        below[2 * (H + 2) + w] = inflow_a[w]
    for r in range(sizes.releases):
        value = release[0, r]
        to = below[H + 2 + value]
        below[H + 2 + value] = to + 1
        table[sizes.columns * to + ORDER] = r
    for extra in range(sizes.releases, sizes.listed):
        table[sizes.columns * extra + ORDER] = 0

    def step(listed, counts):
        r = table[sizes.columns * listed + ORDER]
        u1, u2, u3 = release[0, r], release[1, r], release[2, r]
        out = []
        for w in range(sizes.scenarios):
            at = sizes.columns * listed + 1 + 3 * w
            plane = LOW + inflow_b[w] + u1 - u2
            shift = inflow_c[w] + u2 - u3
            table[at + SHIFT_A] = inflow_a[w] - u1
            table[at + OFFSET] = plane * sizes.depth_ext + LOW + shift
            far[w * sizes.far_size + 1 + counts[w]] = listed
            reaches = jnp.logical_and(jnp.logical_and(first_depth, shift > SUB), listed < sizes.releases)
            out.append(counts[w] + reaches.astype(jnp.int32))
            if sizes.pair:
                shift = jnp.where(first_depth, jnp.maximum(shift, 0), HIGH + jnp.minimum(shift, 0))
                table[at + EDGE_OFFSET] = plane * sizes.edge_ext + shift
            else:
                table[at + EDGE_OFFSET] = plane * sizes.edge_ext + LOW + shift
        return tuple(out)

    counts = lax.fori_loop(0, sizes.listed, step, tuple(jnp.int32(0) for _ in range(sizes.scenarios)))
    for w in range(sizes.scenarios):
        far[w * sizes.far_size] = counts[w]
        far[w * sizes.far_size + 1 + counts[w]] = sizes.releases


def make_factors(sizes, release, price, table, gains, depths, heights):
    sublane = lax.broadcasted_iota(jnp.int32, (SUB, LANES), 0)
    place = sizes.place(lax.broadcasted_iota(jnp.int32, (SUB, LANES), 1))
    row0, depth0 = lax.axis_index("grid") * sizes.rows, lax.axis_index("scen") * sizes.depth
    spans = (sizes.rows * sizes.grid_count, sizes.width, sizes.depth * sizes.scen_count)
    prices = [price[i] * (1.0 / (spans[i] * H * softness)) for i in range(3)]

    def step(listed, _):
        r = table[sizes.columns * listed + ORDER]
        rate = [prices[i] * release[i, r].astype(jnp.float32) for i in range(3)]
        for plane in range(sizes.planes):
            level = (place * sizes.planes + (plane + 1)).astype(jnp.float32)
            gains[pl.ds(pl.multiple_of((listed * sizes.planes + plane) * SUB, SUB), SUB), :] = jnp.exp(level * rate[1])
        listens = jnp.where(listed < sizes.releases, 1.0, 0.0)
        for refs, start, count, which in ((heights, row0, sizes.rows, 0), (depths, depth0, sizes.depth, 2)):
            for strip in range(count // SUB):
                level = (sublane + (start + strip * SUB + 1)).astype(jnp.float32)
                refs[pl.ds(pl.multiple_of(listed * count + strip * SUB, SUB), SUB), :] = jnp.exp(level * rate[which]) * listens
        return 0

    lax.fori_loop(0, sizes.listed, step, 0)


class Plan:
    def __init__(self, sizes, below, table, far, factors, matrix):
        self.sizes, self.below, self.table, self.far, self.matrix = sizes, below, table, far, matrix
        self.gains, self.depths, self.heights = factors
        grid, scen = lax.axis_index("grid"), lax.axis_index("scen")
        self.first_row, self.last_row = grid == 0, grid == sizes.grid_count - 1
        self.first_depth, self.last_depth = scen == 0, scen == sizes.scen_count - 1
        fill_turns(matrix, sizes)

    def entry(self, scenario, listed, column):
        return self.table[self.sizes.columns * listed + 1 + 3 * scenario + column]

    def edge_first(self):
        if self.sizes.pair:
            return jnp.where(self.first_depth, self.sizes.strips - self.sizes.edge_strips, 0)
        return 0

    def put_rows(self, weights, rows, values):
        sizes = self.sizes
        ext = sizes.depth_ext
        bases = [row * sizes.row_size for row in rows]
        put(weights, sizes, self.matrix, bases, ext, LOW, values)
        for is_end, at, count, edge in (
            (self.first_depth, 0, LOW, LOW),
            (self.last_depth, LOW + sizes.depth, HIGH, LOW + sizes.depth - 1),
        ):

            @pl.when(is_end)
            def _():
                for base in bases:
                    repeat(weights, sizes, base, ext, edge, at, count)

            @pl.when(jnp.logical_not(is_end))
            def _():
                for base in bases:
                    put_zeros(weights, sizes, base, ext, at, count)

    def put_edges(self, weights, rows, beyond):
        sizes = self.sizes
        ext = sizes.edge_ext
        bases = [row * sizes.edge_size for row in rows]
        if sizes.pair:
            put(weights, sizes, self.matrix, bases, ext, jnp.where(self.first_depth, HIGH, 0), beyond)
            for base in bases:
                put_zeros(weights, sizes, base, ext, jnp.where(self.first_depth, 0, HIGH), HIGH)
            return
        for base in bases:
            put_zeros(weights, sizes, base, ext, 0, ext)

        @pl.when(jnp.logical_not(self.first_depth))
        def _():
            put(weights, sizes, self.matrix, bases, ext, 0, [row[:, :LOW] for row in beyond])

        @pl.when(jnp.logical_not(self.last_depth))
        def _():
            put(weights, sizes, self.matrix, bases, ext, LOW + sizes.depth, [row[:, LOW:] for row in beyond])

    def gain(self, listed, plane):
        return self.gains[pl.ds(pl.multiple_of((listed * self.sizes.planes + plane) * SUB, SUB), SUB), :]

    def factors(self, row, first, count, listed):
        height = self.heights[pl.ds(listed * self.sizes.rows + row, 1), :]
        return [
            self.depths[pl.ds(pl.multiple_of(listed * self.sizes.depth + (first + strip) * SUB, SUB), SUB), :] * height
            for strip in range(count)
        ]

    def base(self, edge, scenario, source, first, listed):
        if edge:
            return source * self.sizes.edge_size + self.entry(scenario, listed, EDGE_OFFSET), self.sizes.edge_ext
        return source * self.sizes.row_size + self.entry(scenario, listed, OFFSET) + first * SUB, self.sizes.depth_ext

    def fill_beyond(self, weights, row_size):
        rows = self.sizes.rows
        unroll = 4

        def fill(index, _):
            for k in range(unroll):
                at = pl.multiple_of((index * unroll + k) * SUB, SUB)
                for is_end, to, source in ((self.first_row, 0, 1), (self.last_row, rows + 1, rows)):
                    end = weights[pl.ds(source * row_size + at, SUB), :]
                    weights[pl.ds(to * row_size + at, SUB), :] = end * is_end.astype(jnp.float32)
            return 0

        lax.fori_loop(0, row_size // (SUB * unroll), fill, 0)

    def far_terms(self, sums_ref, edges):
        sizes = self.sizes
        strip = sizes.strips - 2
        together = 2 if sizes.rows % 2 == 0 else 1

        def scenario_terms(scenario, _):
            count = self.far[scenario * sizes.far_size]

            def work(index, _):
                rows = [index * together + i for i in range(together)]

                def step(index, sums):
                    sums = [list(each) for each in sums]
                    for k in range(UNROLL):
                        listed = self.far[scenario * sizes.far_size + 1 + index * UNROLL + k]
                        lands = self.entry(scenario, listed, SHIFT_A) + 1
                        for i, row in enumerate(rows):
                            source = jnp.clip(row + lands, 0, sizes.rows + 1)
                            sums[i] = self.add_release(sums[i], edges, True, scenario, row, strip, 1, listed, source)
                    return tuple(tuple(each) for each in sums)

                sums = tuple(tuple(load_sums(sums_ref, sizes, scenario, row, strip, 1)) for row in rows)
                sums = lax.fori_loop(0, (count + UNROLL - 1) // UNROLL, step, sums)
                for row, each in zip(rows, sums, strict=True):
                    store_sums(sums_ref, sizes, scenario, row, strip, 1, each)
                return 0

            @pl.when(count > 0)
            def _():
                lax.fori_loop(0, sizes.rows // together, work, 0)

            return 0

        lax.fori_loop(0, sizes.scenarios, scenario_terms, 0)

    def own_terms(self, load, store, weights, edge, first, strips, shift=0, chunk=None):
        sizes = self.sizes
        together = 2 if sizes.scenarios % 2 == 0 else 1

        def work(index, _):
            row = index % sizes.rows
            scenarios = [index // sizes.rows * together + i for i in range(together)]

            def find(listed):
                found = []
                for scenario in scenarios:
                    source = jnp.clip(row + 1 + self.entry(scenario, listed, SHIFT_A), 0, sizes.rows + 1)
                    base, ext = self.base(edge, scenario, source, first, listed)
                    found.append((base + shift, ext))
                return found

            def add(sums, from_strip, count, listed, bases):
                factors = self.factors(row, first + from_strip, count, listed)
                for plane in range(sizes.planes):
                    gain = self.gain(listed, plane)
                    for strip in range(count):
                        weight = gain * factors[strip]
                        at = plane * count + strip
                        for i, (base, ext) in enumerate(bases):
                            landed = weights[pl.ds(base + plane * ext + (from_strip + strip) * SUB, SUB), :]
                            sums[i][at] = sums[i][at] + landed * weight

            bases = None if chunk else [find(listed) for listed in range(sizes.releases)]
            for from_strip, count in strip_sets(strips, TILE):
                sums = [load(scenario, row, first + from_strip, count) for scenario in scenarios]
                if chunk:

                    def step(index, sums):
                        sums = [list(each) for each in sums]
                        for k in range(chunk):
                            add(sums, from_strip, count, index * chunk + k, find(index * chunk + k))
                        return tuple(tuple(each) for each in sums)

                    sums = lax.fori_loop(0, sizes.releases // chunk, step, tuple(tuple(each) for each in sums))
                else:
                    for listed in range(sizes.releases):
                        add(sums, from_strip, count, listed, bases[listed])
                for i, scenario in enumerate(scenarios):
                    store(scenario, row, first + from_strip, count, sums[i], from_strip + count == strips)
            return 0

        lax.fori_loop(0, sizes.scenarios // together * sizes.rows, work, 0)

    def add_release(self, sums, weights, edge, scenario, row, first, count, listed, source):
        sizes = self.sizes
        base, ext = self.base(edge, scenario, source, first, listed)
        factors = self.factors(row, first, count, listed)
        out = []
        for plane in range(sizes.planes):
            gain = self.gain(listed, plane)
            for strip in range(count):
                landed = weights[pl.ds(base + plane * ext + strip * SUB, SUB), :]
                out.append(sums[plane * count + strip] + landed * (gain * factors[strip]))
        return out

    def outside_terms(self, sums_ref, weights, edge, first, count, done=None):
        sizes = self.sizes

        def work(index, _):
            scenario, row = index // sizes.rows, index % sizes.rows
            top = row + self.below[2 * (H + 2) + scenario]
            start = jnp.where(self.last_row, 0, self.below[jnp.clip(top - sizes.rows + 1, 0, H + 1)])
            stop = jnp.where(self.first_row, sizes.releases, self.below[jnp.clip(top + 1, 0, H + 1)])

            def some(lo, hi, shift):
                @pl.when(lo < hi)
                def _():
                    def step(index, sums):
                        for k in range(UNROLL):
                            listed = lo + index * UNROLL + k
                            listed = jnp.where(listed < hi, listed, sizes.releases)
                            source = row + self.entry(scenario, listed, SHIFT_A) + shift
                            source = jnp.clip(source, 0, 2 * H - 1)
                            sums = self.add_release(sums, weights, edge, scenario, row, first, count, listed, source)
                        return tuple(sums)

                    sums = tuple(load_sums(sums_ref, sizes, scenario, row, first, count))
                    sums = lax.fori_loop(0, (hi - lo + UNROLL - 1) // UNROLL, step, sums)
                    store_sums(sums_ref, sizes, scenario, row, first, count, sums)

            if sizes.rows >= 2 * H:
                low = row < H
                some(jnp.where(low, stop, 0), jnp.where(low, sizes.releases, start), jnp.where(low, H, H - sizes.rows))
            else:
                some(0, start, H - sizes.rows)
                some(stop, sizes.releases, H)
            if done is not None:
                done(scenario, row)
            return 0

        lax.fori_loop(0, sizes.scenarios * sizes.rows, work, 0)


def load_sums(ref, sizes, scenario, row, first, count):
    return [
        ref[scenario, row, plane, pl.ds(pl.multiple_of((first + strip) * SUB, SUB), SUB), :]
        for plane in range(sizes.planes)
        for strip in range(count)
    ]


def store_sums(ref, sizes, scenario, row, first, count, sums):
    for plane in range(sizes.planes):
        for strip in range(count):
            ref[scenario, row, plane, pl.ds(pl.multiple_of((first + strip) * SUB, SUB), SUB), :] = sums[plane * count + strip]


def strip_sets(strips, most=4):
    return [(first, min(most, strips - first)) for first in range(0, strips, most)]


def fill_rows(count, held, fill):
    together = FILL if count % FILL == 0 else 1

    def step(index, _):
        rows = [together * index + i for i in range(together)]
        fill(rows, [held[row] for row in rows])
        return 0

    lax.fori_loop(0, count // together, step, 0)


def planes_kernel(sizes, values, *refs):
    outs, (held, planes_held, sems) = refs[:-3], refs[-3:]
    size = 4 if all(count % 4 == 0 for _, count in sizes.pieces) else 1
    copies = [
        pltpu.make_async_copy(values.at[pl.ds(row, size)], held.at[pl.ds(row, size)], sems.at[i])
        for i, row in enumerate(range(0, sizes.rows, size))
    ]
    for copy in copies:
        copy.start()
    start = pl.multiple_of(jnp.where(lax.axis_index("scen") == 0, sizes.depth - HIGH, 0), SUB) if sizes.pair else None
    sent_sem, first_sem = sems.at[len(copies)], len(copies) + 1

    def step(row, _):
        for strip in range(sizes.strips):
            levels = slice(strip * SUB, strip * SUB + SUB)
            blocks = (
                jnp.exp(held[row, levels, block * LANES : block * LANES + LANES] * (-1.0 / softness))
                for block in range(sizes.planes)
            )
            for plane, each in enumerate(transpose(blocks)):
                planes_held[row, plane, levels, :] = each
        if sizes.pair:
            pltpu.make_async_copy(planes_held.at[row, :, pl.ds(start, HIGH)], outs[-1].at[row], sent_sem).start()
        return 0

    pieces = []
    for i, (first, count) in enumerate(sizes.pieces):
        for row in range(first, first + count, size):
            copies[row // size].wait()
            lax.fori_loop(row, row + size, step, 0)
        pieces.append(pltpu.make_async_copy(planes_held.at[pl.ds(first, count)], outs[i], sems.at[first_sem + i]))
        pieces[-1].start()
    if sizes.pair:
        pltpu.make_async_copy(planes_held.at[:, :, pl.ds(start, HIGH)], outs[-1], sent_sem).wait()
    for piece in pieces:
        piece.wait()


def own_kernel(sizes, *refs):
    own, refs = refs[: len(sizes.pieces)], refs[len(sizes.pieces) :]
    release, inflow, price, ids, sums_out, gains_out, depths_out, heights_out, below, table, far, factors, matrix, *refs = refs
    weights, sums, held, sems = refs
    copies = [
        pltpu.make_async_copy(piece, held.at[pl.ds(first, count)], sems.at[5 + i])
        for i, (piece, (first, count)) in enumerate(zip(own, sizes.pieces, strict=True))
    ]
    for copy in copies:
        copy.start()
    make_lists(sizes, release, inflow, ids, below, table, far)
    make_factors(sizes, release, price, table, *factors)
    backs = [
        pltpu.make_async_copy(ref, out, sems.at[2 + i])
        for i, (ref, out) in enumerate(zip(factors, (gains_out, depths_out, heights_out), strict=True))
    ]
    for back in backs:
        back.start()
    plan = Plan(sizes, below, table, far, factors, matrix)
    for copy in copies:
        copy.wait()
    fill_rows(sizes.rows, held, lambda rows, values: plan.put_rows(weights, [row + 1 for row in rows], values))
    plan.fill_beyond(weights, sizes.row_size)
    zero = jnp.zeros((SUB, LANES), jnp.float32)

    def store(scenario, row, first, count, values, is_last):
        store_sums(sums, sizes, scenario, row, first, count, values)
        if is_last:
            pltpu.make_async_copy(sums.at[scenario, row], sums_out.at[scenario, row], sems.at[1]).start()

    chunk = CHUNK if sizes.releases % CHUNK == 0 else None
    plan.own_terms(lambda scenario, row, first, count: [zero] * (sizes.planes * count), store, weights, False, 0, sizes.strips, 0, chunk)
    for back in backs:
        back.wait()
    pltpu.make_async_copy(sums, sums_out, sems.at[1]).wait()


def start_copies(refs, held, sems):
    copies = [pltpu.make_async_copy(ref, to, sems.at[i]) for i, (ref, to) in enumerate(zip(refs, held, strict=True))]
    for copy in copies:
        copy.start()
    return copies


def edge_kernel(
    sizes, beyond, before, after, sums_in, gains, depths, heights, below, table, far, sums, factors, matrix, weights, edges, held,
    rows_held, sems,
):
    copies = [
        pltpu.make_async_copy(beyond, held, sems.at[0]),
        pltpu.make_async_copy(sums_in, sums, sems.at[1]),
        pltpu.make_async_copy(before, rows_held.at[pl.ds(0, H)], sems.at[2]),
        pltpu.make_async_copy(after, rows_held.at[pl.ds(H, H)], sems.at[3]),
    ]
    for copy in copies:
        copy.start()
    copies += start_copies((gains, depths, heights), factors, sems.at[pl.ds(5, 3)])
    plan = Plan(sizes, below, table, far, factors, matrix)
    copies[0].wait()
    fill_rows(sizes.rows, held, lambda rows, values: plan.put_edges(edges, [row + 1 for row in rows], values))
    plan.fill_beyond(edges, sizes.edge_size)
    for copy in (copies[1], *copies[4:]):
        copy.wait()

    def store(scenario, row, first, count, values, is_last):
        store_sums(sums, sizes, scenario, row, first, count, values)

    load = functools.partial(load_sums, sums, sizes)
    if sizes.pair:
        near = jnp.where(plan.first_depth, sizes.strips - 1, 0)
        shift = jnp.where(plan.first_depth, HIGH - SUB, 0)
        plan.own_terms(load, store, edges, True, near, 1, shift, CHUNK if sizes.releases % CHUNK == 0 else None)
        plan.far_terms(sums, edges)
    else:
        plan.own_terms(load, store, edges, True, 0, sizes.edge_strips)
    copies[2].wait()
    copies[3].wait()
    fill_rows(2 * H, rows_held, functools.partial(plan.put_rows, weights))
    sets = strip_sets(sizes.strips)

    for first, count in sets:
        plan.outside_terms(sums, weights, False, first, count)


def last_kernel(
    sizes, scale, before, after, sums_in, gains, depths, heights, below, table, far, average, totals_out, factors, matrix, edges, sums,
    held, sems,
):
    copies = [
        pltpu.make_async_copy(before, held.at[pl.ds(0, H)], sems.at[0]),
        pltpu.make_async_copy(after, held.at[pl.ds(H, H)], sems.at[1]),
        pltpu.make_async_copy(sums_in, sums, sems.at[2]),
    ]
    for copy in copies:
        copy.start()
    copies += start_copies((gains, depths, heights), factors, sems.at[pl.ds(4, 3)])
    plan = Plan(sizes, below, table, far, factors, matrix)
    copies[0].wait()
    copies[1].wait()

    fill_rows(2 * H, held, functools.partial(plan.put_edges, edges))
    for copy in copies[2:]:
        copy.wait()
    for first, count in strip_sets(sizes.edge_strips):
        plan.outside_terms(sums, edges, True, plan.edge_first() + first, count)

    def finish(index, total):
        for row in (2 * index, 2 * index + 1):
            for strip in range(sizes.strips):
                levels = slice(strip * SUB, strip * SUB + SUB)
                averages = []
                for plane in range(sizes.planes):
                    logs = None
                    for scenario in range(0, sizes.scenarios, 2):
                        product = sums[scenario, row, plane, levels, :]
                        if scenario + 1 < sizes.scenarios:
                            product = product * sums[scenario + 1, row, plane, levels, :]
                        log = jnp.log(product)
                        logs = log if logs is None else logs + log
                    averages.append(logs * scale)
                    total = total + averages[-1]
                for block, values in enumerate(transpose(averages)):
                    average[row, levels, block * LANES : block * LANES + LANES] = values
        return total

    total = lax.fori_loop(0, sizes.rows // 2, finish, jnp.zeros((SUB, LANES), jnp.float32))
    total = jnp.sum(total, axis=0, keepdims=True)
    totals_out[...] = jnp.broadcast_to(total[None], totals_out.shape)


def mean_kernel(sizes, cells, totals, average, out, held, sems):
    chunks = min(8, sizes.rows)
    step = sizes.rows // chunks
    back = [
        pltpu.make_async_copy(held.at[pl.ds(i * step, step)], out.at[pl.ds(i * step, step)], sems.at[chunks + i]) for i in range(chunks)
    ]
    total = jnp.sum(totals[...], axis=0)
    mean = jnp.sum(total, axis=1, keepdims=True) * (1.0 / cells)
    mean = jnp.broadcast_to(mean, (sizes.depth, sizes.width))
    for i in range(chunks):
        for row in range(i * step, i * step + step):
            held[row] = average[row] - mean
        back[i].start()
    for copy in back:
        copy.wait()


SMEM, VMEM, HBM, ANY = (pl.BlockSpec(memory_space=space) for space in (pltpu.SMEM, pltpu.VMEM, pltpu.HBM, pl.ANY))


def call(kernel, sizes, arrays, scalars, outs, out_specs, scratch, limit=61):
    listed = sizes.listed
    factors = [(listed * sizes.planes * SUB, LANES), (listed * sizes.depth, LANES), (listed * sizes.rows, LANES)]
    factors = [pltpu.VMEM(shape, jnp.float32) for shape in factors]
    matrix = pltpu.VMEM((2 * LANES, len(turns(sizes)) * LANES), jnp.bfloat16)
    flat, tree = jax.tree.flatten(scalars)

    def body(*refs):
        ins, refs = refs[: len(arrays)], refs[len(arrays) :]
        scalar_refs, refs = jax.tree.unflatten(tree, refs[: len(flat)]), refs[len(flat) :]
        out_refs, refs = refs[: len(outs)], refs[len(outs) :]
        kernel(*ins, *scalar_refs, *out_refs, refs[: len(factors)], *refs[len(factors) :])

    return pl.pallas_call(
        body,
        out_shape=outs,
        in_specs=[ANY] * len(arrays) + [SMEM] * len(flat),
        out_specs=out_specs,
        scratch_shapes=[*factors, matrix, *scratch],
        compiler_params=pltpu.CompilerParams(vmem_limit_bytes=limit * 2**20),
    )(*arrays, *flat)


def from_above(cells, axis, hops=1):
    count = lax.axis_size(axis)
    return lax.ppermute(cells, axis, [(i + hops, i) for i in range(count - hops)])


def from_below(cells, axis, hops=1):
    count = lax.axis_size(axis)
    return lax.ppermute(cells, axis, [(i, i + hops) for i in range(count - hops)])


def beyond_levels(own):
    depth = own.shape[2]
    scen_count, scen = lax.axis_size("scen"), lax.axis_index("scen")
    low, high = [], []
    for hop in range(-(-LOW // depth), 0, -1):
        low.append(from_below(own, "scen", hop) if hop < scen_count else jnp.zeros_like(own))
    for hop in range(1, -(-HIGH // depth) + 1):
        high.append(from_above(own, "scen", hop) if hop < scen_count else jnp.zeros_like(own))
    low = jnp.concatenate(low, axis=2)[:, :, -LOW:]
    high = jnp.concatenate(high, axis=2)[:, :, :HIGH]
    for hop in range(1, -(-HIGH // depth)):
        fill = high[:, :, hop * depth - 1 : hop * depth]
        keep = lax.broadcasted_iota(jnp.int32, high.shape, 2) < hop * depth
        high = jnp.where(jnp.logical_or(scen + hop != scen_count - 1, keep), high, fill)
    return jnp.concatenate([low, high], axis=2)


def on_device(value_next, scenario_ids, inflow_table, release_shifts, price):
    rows, depth, width = value_next.shape
    grid_count, scen_count = lax.axis_size("grid"), lax.axis_size("scen")
    scenarios = scenario_ids.shape[0] * scen_count
    sizes = Sizes(rows, depth, width, scenarios, release_shifts.shape[0], grid_count, scen_count)

    ids = [scenario_ids]
    for hop in range(1, scen_count):
        ids.append(lax.ppermute(scenario_ids, "scen", [(i, (i + hop) % scen_count) for i in range(scen_count)]))
    ids = [each[i : i + 1] for each in ids for i in range(scenario_ids.shape[0])]

    def like(*shape, kind=jnp.float32):
        return jax.ShapeDtypeStruct(shape, kind)

    planes = sizes.planes
    made = [like(count, planes, depth, LANES) for _, count in sizes.pieces]
    if sizes.pair:
        made.append(like(rows, planes, HIGH, LANES))
    made = pl.pallas_call(
        functools.partial(planes_kernel, sizes),
        out_shape=made,
        in_specs=[HBM],
        out_specs=[HBM] * len(made),
        scratch_shapes=[
            pltpu.VMEM(value_next.shape, jnp.float32), pltpu.VMEM((rows, planes, depth, LANES), jnp.float32),
            pltpu.SemaphoreType.DMA((rows + 4,)),
        ],
        compiler_params=pltpu.CompilerParams(vmem_limit_bytes=61 * 2**20),
    )(value_next)
    made, ids = lax.optimization_barrier((made, ids))
    pieces = made[: len(sizes.pieces)]
    scalars = (release_shifts.T, inflow_table.T, price, ids)
    if sizes.pair:
        beyond = lax.ppermute(made[-1], "scen", [(0, 1), (1, 0)])
    else:
        beyond = beyond_levels(jnp.concatenate(pieces, axis=0))
    before = from_below(pieces[-1][-H:], "grid")
    after = from_above(pieces[0][:H], "grid")

    shape = (scenarios, rows, sizes.planes, depth, LANES)
    sums_shape = jax.ShapeDtypeStruct(shape, jnp.float32)
    sums_held = pltpu.VMEM(shape, jnp.float32)
    inside, outside = rows + 2, 2 * H
    listed = sizes.listed
    factors = [like(listed * planes * SUB, LANES), like(listed * depth, LANES), like(listed * rows, LANES)]
    lists = [2 * (H + 2) + scenarios, listed * sizes.columns, scenarios * sizes.far_size]
    lists = [like(size, kind=jnp.int32) for size in lists]
    sums, *factors = call(
        functools.partial(own_kernel, sizes), sizes, pieces, scalars, [sums_shape, *factors, *lists], [HBM] * 4 + [SMEM] * 3,
        [
            pltpu.VMEM((inside * sizes.row_size, LANES), jnp.float32), sums_held,
            pltpu.VMEM((rows, planes, depth, LANES), jnp.float32), pltpu.SemaphoreType.DMA((8,)),
        ],
    )
    factors, lists = factors[:3], factors[3:]
    beyond, sums = lax.optimization_barrier((beyond, sums))
    corner_before = from_below(beyond[rows - H :], "grid")
    corner_after = from_above(beyond[:H], "grid")
    (sums,) = call(
        functools.partial(edge_kernel, sizes), sizes, (beyond, before, after, sums, *factors), lists, [sums_shape], [VMEM],
        [
            pltpu.VMEM((outside * sizes.row_size, LANES), jnp.float32), pltpu.VMEM((inside * sizes.edge_size, LANES), jnp.float32),
            pltpu.VMEM(beyond.shape, jnp.float32), pltpu.VMEM((2 * H, planes, depth, LANES), jnp.float32),
            pltpu.SemaphoreType.DMA((8,)),
        ],
        44,
    )
    scale = -softness / scenarios
    devices = grid_count * scen_count
    average, totals = call(
        functools.partial(last_kernel, sizes, scale), sizes, (corner_before, corner_after, sums, *factors), lists,
        [jax.ShapeDtypeStruct(value_next.shape, jnp.float32), jax.ShapeDtypeStruct((devices, 1, LANES), jnp.float32)],
        [VMEM, VMEM],
        [
            pltpu.VMEM((outside * sizes.edge_size, LANES), jnp.float32), sums_held, pltpu.VMEM((2 * H, *beyond.shape[1:]), jnp.float32),
            pltpu.SemaphoreType.DMA((7,)),
        ],
        24,
    )
    totals = lax.all_to_all(totals, ("scen", "grid"), 0, 0, tiled=True)
    cells = rows * grid_count * depth * scen_count * width
    return pl.pallas_call(
        functools.partial(mean_kernel, sizes, cells),
        out_shape=jax.ShapeDtypeStruct(value_next.shape, jnp.float32),
        in_specs=[VMEM, VMEM],
        out_specs=HBM,
        scratch_shapes=[pltpu.VMEM(value_next.shape, jnp.float32), pltpu.SemaphoreType.DMA((16,))],
        compiler_params=pltpu.CompilerParams(vmem_limit_bytes=8 * 2**20),
    )(totals, average)


def solution(mesh):
    placed = (P("grid", "scen", None), P("scen"), P(), P(), P())
    return jax.shard_map(
        on_device, mesh=mesh, in_specs=placed, out_specs=P("grid", "scen", None), check_vma=False
    )
```

```python
import functools

import jax
import jax.numpy as jnp
from jax import lax
from jax.experimental import pallas as pl
from jax.experimental.pallas import tpu as pltpu
from jax.sharding import PartitionSpec as P

H = 8
LOW, HIGH = H, 2 * H
SUB, LANES = 8, 128
TILE = 2
CHUNK = 4
FILL = 8
UNROLL = 2
softness = 0.5

ORDER = 0
SHIFT_A, OFFSET, EDGE_OFFSET = range(3)


class Sizes:
    def __init__(self, rows, depth, width, scenarios, releases, grid_count, scen_count):
        self.rows, self.depth, self.width = rows, depth, width
        self.grid_count, self.scen_count = grid_count, scen_count
        self.scenarios, self.releases = scenarios, releases
        self.listed = releases + UNROLL - 1
        self.columns = 1 + 3 * scenarios
        self.far_size = releases + 1 + UNROLL
        self.pieces = [(0, H), (H, rows - 2 * H), (rows - H, H)] if rows > 2 * H else [(0, H), (H, H)] if rows == 2 * H else [(0, rows)]
        self.planes = width // LANES
        self.group = LANES // self.planes
        self.strips = depth // SUB
        self.planes_ext = LOW + self.planes + HIGH
        self.depth_ext = LOW + depth + HIGH
        self.row_size = self.planes_ext * self.depth_ext
        self.pair = scen_count == 2 and depth >= HIGH
        self.edge_strips = HIGH // SUB if self.pair else self.strips
        self.edge_ext = 2 * HIGH if self.pair else self.depth_ext
        self.edge_size = self.planes_ext * self.edge_ext

    def place(self, lane):
        return lane % self.planes * self.group + lane // self.planes

    def lane(self, place):
        return place % self.group * self.planes + place // self.group


def transpose(blocks):
    lane = lax.broadcasted_iota(jnp.int32, (SUB, LANES), 1)
    blocks = [pltpu.roll(block, k, 1) if k else block for k, block in enumerate(blocks)]
    count = len(blocks)
    step = 1
    while step < count:
        odd = (lane // step) % 2 == 1
        blocks = [jnp.where(odd, blocks[(i + step) % count], blocks[i]) for i in range(count)]
        step *= 2
    return [pltpu.roll(blocks[-j % count], LANES - j, 1) if j else blocks[0] for j in range(count)]


def turns(sizes):
    return [*range(-(-(-LOW // sizes.planes)), 0), *range(1, -(-HIGH // sizes.planes) + 1)]


def fill_turns(matrix, sizes):
    shape = (2 * LANES, LANES)
    source = lax.broadcasted_iota(jnp.int32, shape, 0) % LANES
    place = sizes.place(lax.broadcasted_iota(jnp.int32, shape, 1))
    for i, turn in enumerate(turns(sizes)):
        there = jnp.clip(place + turn, 0, LANES - 1)
        matrix[:, i * LANES : i * LANES + LANES] = (sizes.lane(there) == source).astype(jnp.float32).astype(jnp.bfloat16)


def put(weights, sizes, matrix, row_bases, depth_ext, at, rows):
    place = sizes.place(lax.broadcasted_iota(jnp.int32, (SUB, LANES), 1))
    levels = rows[0].shape[1]
    both = jnp.concatenate([row.reshape(sizes.planes * levels, LANES) for row in rows], axis=0)
    upper = both.astype(jnp.bfloat16)
    lower = (both - upper.astype(jnp.float32)).astype(jnp.bfloat16)
    turned = jnp.dot(jnp.concatenate([upper, lower], axis=1), matrix[...], preferred_element_type=jnp.float32)
    for row, row_base in enumerate(row_bases):
        for strip in range(levels // SUB):
            base = row_base + at + strip * SUB

            def part(array, plane):
                first = (row * sizes.planes + plane) * levels + strip * SUB
                return array[first : first + SUB]

            for plane in range(sizes.planes):
                weights[pl.ds(base + (LOW + plane) * depth_ext, SUB), :] = part(both, plane)
            for i, turn in enumerate(turns(sizes)):
                moved = turned[:, i * LANES : i * LANES + LANES]
                end = part(moved, sizes.planes - 1 if turn > 0 else 0)
                past = place + turn > LANES - 1 if turn > 0 else place + turn < 0
                for plane in range(sizes.planes):
                    to = LOW + turn * sizes.planes + plane
                    if 0 <= to < sizes.planes_ext:
                        weights[pl.ds(base + to * depth_ext, SUB), :] = jnp.where(past, end, part(moved, plane))


def put_zeros(weights, sizes, row_base, depth_ext, at, count):
    zero = jnp.zeros((SUB, LANES), jnp.float32)
    for strip in range(count // SUB):
        for plane in range(sizes.planes_ext):
            weights[pl.ds(row_base + plane * depth_ext + at + strip * SUB, SUB), :] = zero


def repeat(weights, sizes, row_base, depth_ext, source, at, count):
    for plane in range(sizes.planes_ext):
        base = row_base + plane * depth_ext
        level = jnp.broadcast_to(weights[pl.ds(base + source, 1), :], (SUB, LANES))
        for strip in range(count // SUB):
            weights[pl.ds(base + at + strip * SUB, SUB), :] = level


def make_lists(sizes, release, inflow, ids, below, table, far):
    first_depth = lax.axis_index("scen") == 0
    inflow_a, inflow_b, inflow_c = ([inflow[i, ids[w][0]] for w in range(sizes.scenarios)] for i in range(3))
    for value in range(H + 2):
        count = jnp.int32(0)
        for r in range(sizes.releases):
            count = count + (release[0, r] < value).astype(jnp.int32)
        below[value] = count
        below[H + 2 + value] = count
    for w in range(sizes.scenarios):
        below[2 * (H + 2) + w] = inflow_a[w]
    for r in range(sizes.releases):
        value = release[0, r]
        to = below[H + 2 + value]
        below[H + 2 + value] = to + 1
        table[sizes.columns * to + ORDER] = r
    for extra in range(sizes.releases, sizes.listed):
        table[sizes.columns * extra + ORDER] = 0

    def step(listed, counts):
        r = table[sizes.columns * listed + ORDER]
        u1, u2, u3 = release[0, r], release[1, r], release[2, r]
        out = []
        for w in range(sizes.scenarios):
            at = sizes.columns * listed + 1 + 3 * w
            plane = LOW + inflow_b[w] + u1 - u2
            shift = inflow_c[w] + u2 - u3
            table[at + SHIFT_A] = inflow_a[w] - u1
            table[at + OFFSET] = plane * sizes.depth_ext + LOW + shift
            far[w * sizes.far_size + 1 + counts[w]] = listed
            reaches = jnp.logical_and(jnp.logical_and(first_depth, shift > SUB), listed < sizes.releases)
            out.append(counts[w] + reaches.astype(jnp.int32))
            if sizes.pair:
                shift = jnp.where(first_depth, jnp.maximum(shift, 0), HIGH + jnp.minimum(shift, 0))
                table[at + EDGE_OFFSET] = plane * sizes.edge_ext + shift
            else:
                table[at + EDGE_OFFSET] = plane * sizes.edge_ext + LOW + shift
        return tuple(out)

    counts = lax.fori_loop(0, sizes.listed, step, tuple(jnp.int32(0) for _ in range(sizes.scenarios)))
    for w in range(sizes.scenarios):
        far[w * sizes.far_size] = counts[w]
        far[w * sizes.far_size + 1 + counts[w]] = sizes.releases


def make_factors(sizes, release, price, table, gains, depths, heights):
    sublane = lax.broadcasted_iota(jnp.int32, (SUB, LANES), 0)
    place = sizes.place(lax.broadcasted_iota(jnp.int32, (SUB, LANES), 1))
    row0, depth0 = lax.axis_index("grid") * sizes.rows, lax.axis_index("scen") * sizes.depth
    spans = (sizes.rows * sizes.grid_count, sizes.width, sizes.depth * sizes.scen_count)
    prices = [price[i] * (1.0 / (spans[i] * H * softness)) for i in range(3)]

    def step(listed, _):
        r = table[sizes.columns * listed + ORDER]
        rate = [prices[i] * release[i, r].astype(jnp.float32) for i in range(3)]
        for plane in range(sizes.planes):
            level = (place * sizes.planes + (plane + 1)).astype(jnp.float32)
            gains[pl.ds(pl.multiple_of((listed * sizes.planes + plane) * SUB, SUB), SUB), :] = jnp.exp(level * rate[1])
        listens = jnp.where(listed < sizes.releases, 1.0, 0.0)
        for refs, start, count, which in ((heights, row0, sizes.rows, 0), (depths, depth0, sizes.depth, 2)):
            for strip in range(count // SUB):
                level = (sublane + (start + strip * SUB + 1)).astype(jnp.float32)
                refs[pl.ds(pl.multiple_of(listed * count + strip * SUB, SUB), SUB), :] = jnp.exp(level * rate[which]) * listens
        return 0

    lax.fori_loop(0, sizes.listed, step, 0)


class Plan:
    def __init__(self, sizes, below, table, far, factors, matrix):
        self.sizes, self.below, self.table, self.far, self.matrix = sizes, below, table, far, matrix
        self.gains, self.depths, self.heights = factors
        grid, scen = lax.axis_index("grid"), lax.axis_index("scen")
        self.first_row, self.last_row = grid == 0, grid == sizes.grid_count - 1
        self.first_depth, self.last_depth = scen == 0, scen == sizes.scen_count - 1
        fill_turns(matrix, sizes)

    def entry(self, scenario, listed, column):
        return self.table[self.sizes.columns * listed + 1 + 3 * scenario + column]

    def edge_first(self):
        if self.sizes.pair:
            return jnp.where(self.first_depth, self.sizes.strips - self.sizes.edge_strips, 0)
        return 0

    def put_rows(self, weights, rows, values):
        sizes = self.sizes
        ext = sizes.depth_ext
        bases = [row * sizes.row_size for row in rows]
        put(weights, sizes, self.matrix, bases, ext, LOW, values)
        for is_end, at, count, edge in (
            (self.first_depth, 0, LOW, LOW),
            (self.last_depth, LOW + sizes.depth, HIGH, LOW + sizes.depth - 1),
        ):

            @pl.when(is_end)
            def _():
                for base in bases:
                    repeat(weights, sizes, base, ext, edge, at, count)

            @pl.when(jnp.logical_not(is_end))
            def _():
                for base in bases:
                    put_zeros(weights, sizes, base, ext, at, count)

    def put_edges(self, weights, rows, beyond):
        sizes = self.sizes
        ext = sizes.edge_ext
        bases = [row * sizes.edge_size for row in rows]
        if sizes.pair:
            put(weights, sizes, self.matrix, bases, ext, jnp.where(self.first_depth, HIGH, 0), beyond)
            for base in bases:
                put_zeros(weights, sizes, base, ext, jnp.where(self.first_depth, 0, HIGH), HIGH)
            return
        for base in bases:
            put_zeros(weights, sizes, base, ext, 0, ext)

        @pl.when(jnp.logical_not(self.first_depth))
        def _():
            put(weights, sizes, self.matrix, bases, ext, 0, [row[:, :LOW] for row in beyond])

        @pl.when(jnp.logical_not(self.last_depth))
        def _():
            put(weights, sizes, self.matrix, bases, ext, LOW + sizes.depth, [row[:, LOW:] for row in beyond])

    def gain(self, listed, plane):
        return self.gains[pl.ds(pl.multiple_of((listed * self.sizes.planes + plane) * SUB, SUB), SUB), :]

    def factors(self, row, first, count, listed):
        height = self.heights[pl.ds(listed * self.sizes.rows + row, 1), :]
        return [
            self.depths[pl.ds(pl.multiple_of(listed * self.sizes.depth + (first + strip) * SUB, SUB), SUB), :] * height
            for strip in range(count)
        ]

    def base(self, edge, scenario, source, first, listed):
        if edge:
            return source * self.sizes.edge_size + self.entry(scenario, listed, EDGE_OFFSET), self.sizes.edge_ext
        return source * self.sizes.row_size + self.entry(scenario, listed, OFFSET) + first * SUB, self.sizes.depth_ext

    def fill_beyond(self, weights, row_size):
        rows = self.sizes.rows
        unroll = 4

        def fill(index, _):
            for k in range(unroll):
                at = pl.multiple_of((index * unroll + k) * SUB, SUB)
                for is_end, to, source in ((self.first_row, 0, 1), (self.last_row, rows + 1, rows)):
                    end = weights[pl.ds(source * row_size + at, SUB), :]
                    weights[pl.ds(to * row_size + at, SUB), :] = end * is_end.astype(jnp.float32)
            return 0

        lax.fori_loop(0, row_size // (SUB * unroll), fill, 0)

    def far_terms(self, sums_ref, edges):
        sizes = self.sizes
        strip = sizes.strips - 2
        together = 2 if sizes.rows % 2 == 0 else 1

        def scenario_terms(scenario, _):
            count = self.far[scenario * sizes.far_size]

            def work(index, _):
                rows = [index * together + i for i in range(together)]

                def step(index, sums):
                    sums = [list(each) for each in sums]
                    for k in range(UNROLL):
                        listed = self.far[scenario * sizes.far_size + 1 + index * UNROLL + k]
                        lands = self.entry(scenario, listed, SHIFT_A) + 1
                        for i, row in enumerate(rows):
                            source = jnp.clip(row + lands, 0, sizes.rows + 1)
                            sums[i] = self.add_release(sums[i], edges, True, scenario, row, strip, 1, listed, source)
                    return tuple(tuple(each) for each in sums)

                sums = tuple(tuple(load_sums(sums_ref, sizes, scenario, row, strip, 1)) for row in rows)
                sums = lax.fori_loop(0, (count + UNROLL - 1) // UNROLL, step, sums)
                for row, each in zip(rows, sums, strict=True):
                    store_sums(sums_ref, sizes, scenario, row, strip, 1, each)
                return 0

            @pl.when(count > 0)
            def _():
                lax.fori_loop(0, sizes.rows // together, work, 0)

            return 0

        lax.fori_loop(0, sizes.scenarios, scenario_terms, 0)

    def own_terms(self, load, store, weights, edge, first, strips, shift=0, chunk=None):
        sizes = self.sizes
        together = 2 if sizes.scenarios % 2 == 0 else 1

        def work(index, _):
            row = index % sizes.rows
            scenarios = [index // sizes.rows * together + i for i in range(together)]

            def find(listed):
                found = []
                for scenario in scenarios:
                    source = jnp.clip(row + 1 + self.entry(scenario, listed, SHIFT_A), 0, sizes.rows + 1)
                    base, ext = self.base(edge, scenario, source, first, listed)
                    found.append((base + shift, ext))
                return found

            def add(sums, from_strip, count, listed, bases):
                factors = self.factors(row, first + from_strip, count, listed)
                for plane in range(sizes.planes):
                    gain = self.gain(listed, plane)
                    for strip in range(count):
                        weight = gain * factors[strip]
                        at = plane * count + strip
                        for i, (base, ext) in enumerate(bases):
                            landed = weights[pl.ds(base + plane * ext + (from_strip + strip) * SUB, SUB), :]
                            sums[i][at] = sums[i][at] + landed * weight

            bases = None if chunk else [find(listed) for listed in range(sizes.releases)]
            for from_strip, count in strip_sets(strips, TILE):
                sums = [load(scenario, row, first + from_strip, count) for scenario in scenarios]
                if chunk:

                    def step(index, sums):
                        sums = [list(each) for each in sums]
                        for k in range(chunk):
                            add(sums, from_strip, count, index * chunk + k, find(index * chunk + k))
                        return tuple(tuple(each) for each in sums)

                    sums = lax.fori_loop(0, sizes.releases // chunk, step, tuple(tuple(each) for each in sums))
                else:
                    for listed in range(sizes.releases):
                        add(sums, from_strip, count, listed, bases[listed])
                for i, scenario in enumerate(scenarios):
                    store(scenario, row, first + from_strip, count, sums[i], from_strip + count == strips)
            return 0

        lax.fori_loop(0, sizes.scenarios // together * sizes.rows, work, 0)

    def add_release(self, sums, weights, edge, scenario, row, first, count, listed, source):
        sizes = self.sizes
        base, ext = self.base(edge, scenario, source, first, listed)
        factors = self.factors(row, first, count, listed)
        out = []
        for plane in range(sizes.planes):
            gain = self.gain(listed, plane)
            for strip in range(count):
                landed = weights[pl.ds(base + plane * ext + strip * SUB, SUB), :]
                out.append(sums[plane * count + strip] + landed * (gain * factors[strip]))
        return out

    def outside_terms(self, sums_ref, weights, edge, first, count, done=None):
        sizes = self.sizes

        def work(index, _):
            scenario, row = index // sizes.rows, index % sizes.rows
            top = row + self.below[2 * (H + 2) + scenario]
            start = jnp.where(self.last_row, 0, self.below[jnp.clip(top - sizes.rows + 1, 0, H + 1)])
            stop = jnp.where(self.first_row, sizes.releases, self.below[jnp.clip(top + 1, 0, H + 1)])

            def some(lo, hi, shift):
                @pl.when(lo < hi)
                def _():
                    def step(index, sums):
                        for k in range(UNROLL):
                            listed = lo + index * UNROLL + k
                            listed = jnp.where(listed < hi, listed, sizes.releases)
                            source = row + self.entry(scenario, listed, SHIFT_A) + shift
                            source = jnp.clip(source, 0, 2 * H - 1)
                            sums = self.add_release(sums, weights, edge, scenario, row, first, count, listed, source)
                        return tuple(sums)

                    sums = tuple(load_sums(sums_ref, sizes, scenario, row, first, count))
                    sums = lax.fori_loop(0, (hi - lo + UNROLL - 1) // UNROLL, step, sums)
                    store_sums(sums_ref, sizes, scenario, row, first, count, sums)

            if sizes.rows >= 2 * H:
                low = row < H
                some(jnp.where(low, stop, 0), jnp.where(low, sizes.releases, start), jnp.where(low, H, H - sizes.rows))
            else:
                some(0, start, H - sizes.rows)
                some(stop, sizes.releases, H)
            if done is not None:
                done(scenario, row)
            return 0

        lax.fori_loop(0, sizes.scenarios * sizes.rows, work, 0)


def load_sums(ref, sizes, scenario, row, first, count):
    return [
        ref[scenario, row, plane, pl.ds(pl.multiple_of((first + strip) * SUB, SUB), SUB), :]
        for plane in range(sizes.planes)
        for strip in range(count)
    ]


def store_sums(ref, sizes, scenario, row, first, count, sums):
    for plane in range(sizes.planes):
        for strip in range(count):
            ref[scenario, row, plane, pl.ds(pl.multiple_of((first + strip) * SUB, SUB), SUB), :] = sums[plane * count + strip]


def strip_sets(strips, most=4):
    return [(first, min(most, strips - first)) for first in range(0, strips, most)]


def fill_rows(count, held, fill):
    together = FILL if count % FILL == 0 else 1

    def step(index, _):
        rows = [together * index + i for i in range(together)]
        fill(rows, [held[row] for row in rows])
        return 0

    lax.fori_loop(0, count // together, step, 0)


def planes_kernel(sizes, values, *refs):
    *outs, sent_sem = refs
    start = pl.multiple_of(jnp.where(lax.axis_index("scen") == 0, sizes.depth - HIGH, 0), SUB) if sizes.pair else None

    def step(out, first, row, _):
        for strip in range(sizes.strips):
            levels = slice(strip * SUB, strip * SUB + SUB)
            blocks = (
                jnp.exp(values[row, levels, block * LANES : block * LANES + LANES] * (-1.0 / softness))
                for block in range(sizes.planes)
            )
            for plane, each in enumerate(transpose(blocks)):
                out[row - first, plane, levels, :] = each
        if sizes.pair:
            pltpu.make_async_copy(out.at[row - first, :, pl.ds(start, HIGH)], outs[-1].at[row], sent_sem).start()
        return 0

    for out, (first, count) in zip(outs, sizes.pieces):
        lax.fori_loop(first, first + count, functools.partial(step, out, first), 0)
    if sizes.pair:
        for out, (first, count) in zip(outs, sizes.pieces):
            pltpu.make_async_copy(out.at[:, :, pl.ds(start, HIGH)], outs[-1].at[pl.ds(first, count)], sent_sem).wait()


def own_kernel(sizes, *refs):
    own, refs = refs[: len(sizes.pieces)], refs[len(sizes.pieces) :]
    release, inflow, price, ids, sums, gains, depths, heights, below, table, far, matrix, *refs = refs
    weights, held, sems = refs
    copies = [
        pltpu.make_async_copy(piece, held.at[pl.ds(first, count)], sems.at[5 + i])
        for i, (piece, (first, count)) in enumerate(zip(own, sizes.pieces, strict=True))
    ]
    for copy in copies:
        copy.start()
    make_lists(sizes, release, inflow, ids, below, table, far)
    factors = gains, depths, heights
    make_factors(sizes, release, price, table, *factors)
    plan = Plan(sizes, below, table, far, factors, matrix)
    for copy in copies:
        copy.wait()
    fill_rows(sizes.rows, held, lambda rows, values: plan.put_rows(weights, [row + 1 for row in rows], values))
    plan.fill_beyond(weights, sizes.row_size)
    zero = jnp.zeros((SUB, LANES), jnp.float32)

    def store(scenario, row, first, count, values, is_last):
        store_sums(sums, sizes, scenario, row, first, count, values)

    chunk = CHUNK if sizes.releases % CHUNK == 0 else None
    plan.own_terms(lambda scenario, row, first, count: [zero] * (sizes.planes * count), store, weights, False, 0, sizes.strips, 0, chunk)


def edge_kernel(
    sizes, beyond, before, after, sums_in, gains, depths, heights, below, table, far, sums, matrix, weights, edges, held,
    rows_held, sems,
):
    copies = [
        pltpu.make_async_copy(beyond, held, sems.at[0]),
        pltpu.make_async_copy(sums_in, sums, sems.at[1]),
        pltpu.make_async_copy(before, rows_held.at[pl.ds(0, H)], sems.at[2]),
        pltpu.make_async_copy(after, rows_held.at[pl.ds(H, H)], sems.at[3]),
    ]
    for copy in copies:
        copy.start()
    plan = Plan(sizes, below, table, far, (gains, depths, heights), matrix)
    copies[0].wait()
    fill_rows(sizes.rows, held, lambda rows, values: plan.put_edges(edges, [row + 1 for row in rows], values))
    plan.fill_beyond(edges, sizes.edge_size)
    copies[1].wait()

    def store(scenario, row, first, count, values, is_last):
        store_sums(sums, sizes, scenario, row, first, count, values)

    load = functools.partial(load_sums, sums, sizes)
    if sizes.pair:
        near = jnp.where(plan.first_depth, sizes.strips - 1, 0)
        shift = jnp.where(plan.first_depth, HIGH - SUB, 0)
        plan.own_terms(load, store, edges, True, near, 1, shift, CHUNK if sizes.releases % CHUNK == 0 else None)
        plan.far_terms(sums, edges)
    else:
        plan.own_terms(load, store, edges, True, 0, sizes.edge_strips)
    copies[2].wait()
    copies[3].wait()
    fill_rows(2 * H, rows_held, functools.partial(plan.put_rows, weights))
    sets = strip_sets(sizes.strips)

    for first, count in sets:
        plan.outside_terms(sums, weights, False, first, count)


def last_kernel(
    sizes, scale, before, after, sums_in, gains, depths, heights, below, table, far, average, totals_out, matrix, edges, sums,
    held, sems,
):
    copies = [
        pltpu.make_async_copy(before, held.at[pl.ds(0, H)], sems.at[0]),
        pltpu.make_async_copy(after, held.at[pl.ds(H, H)], sems.at[1]),
        pltpu.make_async_copy(sums_in, sums, sems.at[2]),
    ]
    for copy in copies:
        copy.start()
    plan = Plan(sizes, below, table, far, (gains, depths, heights), matrix)
    copies[0].wait()
    copies[1].wait()

    fill_rows(2 * H, held, functools.partial(plan.put_edges, edges))
    for copy in copies[2:]:
        copy.wait()
    for first, count in strip_sets(sizes.edge_strips):
        plan.outside_terms(sums, edges, True, plan.edge_first() + first, count)

    def finish(index, total):
        for row in (2 * index, 2 * index + 1):
            for strip in range(sizes.strips):
                levels = slice(strip * SUB, strip * SUB + SUB)
                averages = []
                for plane in range(sizes.planes):
                    logs = None
                    for scenario in range(0, sizes.scenarios, 2):
                        product = sums[scenario, row, plane, levels, :]
                        if scenario + 1 < sizes.scenarios:
                            product = product * sums[scenario + 1, row, plane, levels, :]
                        log = jnp.log(product)
                        logs = log if logs is None else logs + log
                    averages.append(logs * scale)
                    total = total + averages[-1]
                for block, values in enumerate(transpose(averages)):
                    average[row, levels, block * LANES : block * LANES + LANES] = values
        return total

    total = lax.fori_loop(0, sizes.rows // 2, finish, jnp.zeros((SUB, LANES), jnp.float32))
    total = jnp.sum(total, axis=0, keepdims=True)
    totals_out[...] = jnp.broadcast_to(total[None], totals_out.shape)


def mean_kernel(sizes, cells, totals, average, out, held, sems):
    chunks = min(8, sizes.rows)
    step = sizes.rows // chunks
    back = [
        pltpu.make_async_copy(held.at[pl.ds(i * step, step)], out.at[pl.ds(i * step, step)], sems.at[chunks + i]) for i in range(chunks)
    ]
    total = jnp.sum(totals[...], axis=0)
    mean = jnp.sum(total, axis=1, keepdims=True) * (1.0 / cells)
    mean = jnp.broadcast_to(mean, (sizes.depth, sizes.width))
    for i in range(chunks):
        for row in range(i * step, i * step + step):
            held[row] = average[row] - mean
        back[i].start()
    for copy in back:
        copy.wait()


SMEM, VMEM, HBM, ANY = (pl.BlockSpec(memory_space=space) for space in (pltpu.SMEM, pltpu.VMEM, pltpu.HBM, pl.ANY))


def call(kernel, sizes, arrays, scalars, outs, out_specs, scratch, limit=61):
    matrix = pltpu.VMEM((2 * LANES, len(turns(sizes)) * LANES), jnp.bfloat16)
    flat, tree = jax.tree.flatten(scalars)

    def body(*refs):
        ins, refs = refs[: len(arrays)], refs[len(arrays) :]
        scalar_refs, refs = jax.tree.unflatten(tree, refs[: len(flat)]), refs[len(flat) :]
        out_refs, refs = refs[: len(outs)], refs[len(outs) :]
        kernel(*ins, *scalar_refs, *out_refs, *refs)

    return pl.pallas_call(
        body,
        out_shape=outs,
        in_specs=[VMEM if array.ndim == 2 else ANY for array in arrays] + [SMEM] * len(flat),
        out_specs=out_specs,
        scratch_shapes=[matrix, *scratch],
        compiler_params=pltpu.CompilerParams(vmem_limit_bytes=limit * 2**20),
    )(*arrays, *flat)


def from_above(cells, axis, hops=1):
    count = lax.axis_size(axis)
    return lax.ppermute(cells, axis, [(i + hops, i) for i in range(count - hops)])


def from_below(cells, axis, hops=1):
    count = lax.axis_size(axis)
    return lax.ppermute(cells, axis, [(i, i + hops) for i in range(count - hops)])


def beyond_levels(own):
    depth = own.shape[2]
    scen_count, scen = lax.axis_size("scen"), lax.axis_index("scen")
    low, high = [], []
    for hop in range(-(-LOW // depth), 0, -1):
        low.append(from_below(own, "scen", hop) if hop < scen_count else jnp.zeros_like(own))
    for hop in range(1, -(-HIGH // depth) + 1):
        high.append(from_above(own, "scen", hop) if hop < scen_count else jnp.zeros_like(own))
    low = jnp.concatenate(low, axis=2)[:, :, -LOW:]
    high = jnp.concatenate(high, axis=2)[:, :, :HIGH]
    for hop in range(1, -(-HIGH // depth)):
        fill = high[:, :, hop * depth - 1 : hop * depth]
        keep = lax.broadcasted_iota(jnp.int32, high.shape, 2) < hop * depth
        high = jnp.where(jnp.logical_or(scen + hop != scen_count - 1, keep), high, fill)
    return jnp.concatenate([low, high], axis=2)


def on_device(value_next, scenario_ids, inflow_table, release_shifts, price):
    rows, depth, width = value_next.shape
    grid_count, scen_count = lax.axis_size("grid"), lax.axis_size("scen")
    scenarios = scenario_ids.shape[0] * scen_count
    sizes = Sizes(rows, depth, width, scenarios, release_shifts.shape[0], grid_count, scen_count)

    ids = [scenario_ids]
    for hop in range(1, scen_count):
        ids.append(lax.ppermute(scenario_ids, "scen", [(i, (i + hop) % scen_count) for i in range(scen_count)]))
    ids = [each[i : i + 1] for each in ids for i in range(scenario_ids.shape[0])]

    def like(*shape, kind=jnp.float32):
        return jax.ShapeDtypeStruct(shape, kind)

    planes = sizes.planes
    made = [like(count, planes, depth, LANES) for _, count in sizes.pieces]
    if sizes.pair:
        made.append(like(rows, planes, HIGH, LANES))
    made = pl.pallas_call(
        functools.partial(planes_kernel, sizes),
        out_shape=made,
        in_specs=[VMEM],
        out_specs=[VMEM] * len(made),
        scratch_shapes=[pltpu.SemaphoreType.DMA],
        compiler_params=pltpu.CompilerParams(vmem_limit_bytes=12 * 2**20),
    )(value_next)
    made, ids = lax.optimization_barrier((made, ids))
    pieces = made[: len(sizes.pieces)]
    scalars = (release_shifts.T, inflow_table.T, price, ids)
    if sizes.pair:
        beyond = lax.ppermute(made[-1], "scen", [(0, 1), (1, 0)])
    else:
        beyond = beyond_levels(jnp.concatenate(pieces, axis=0))
    before = from_below(pieces[-1][-H:], "grid")
    after = from_above(pieces[0][:H], "grid")

    shape = (scenarios, rows, sizes.planes, depth, LANES)
    sums_shape = jax.ShapeDtypeStruct(shape, jnp.float32)
    sums_held = pltpu.VMEM(shape, jnp.float32)
    inside, outside = rows + 2, 2 * H
    listed = sizes.listed
    factors = [like(listed * planes * SUB, LANES), like(listed * depth, LANES), like(listed * rows, LANES)]
    lists = [2 * (H + 2) + scenarios, listed * sizes.columns, scenarios * sizes.far_size]
    lists = [like(size, kind=jnp.int32) for size in lists]
    sums, *factors = call(
        functools.partial(own_kernel, sizes), sizes, pieces, scalars, [sums_shape, *factors, *lists], [VMEM] * 4 + [SMEM] * 3,
        [
            pltpu.VMEM((inside * sizes.row_size, LANES), jnp.float32), pltpu.VMEM((rows, planes, depth, LANES), jnp.float32),
            pltpu.SemaphoreType.DMA((8,)),
        ],
        28,
    )
    factors, lists = factors[:3], factors[3:]
    beyond, sums = lax.optimization_barrier((beyond, sums))
    corner_before = from_below(beyond[rows - H :], "grid")
    corner_after = from_above(beyond[:H], "grid")
    (sums,) = call(
        functools.partial(edge_kernel, sizes), sizes, (beyond, before, after, sums, *factors), lists, [sums_shape], [VMEM],
        [
            pltpu.VMEM((outside * sizes.row_size, LANES), jnp.float32), pltpu.VMEM((inside * sizes.edge_size, LANES), jnp.float32),
            pltpu.VMEM(beyond.shape, jnp.float32), pltpu.VMEM((2 * H, planes, depth, LANES), jnp.float32),
            pltpu.SemaphoreType.DMA((8,)),
        ],
        44,
    )
    scale = -softness / scenarios
    devices = grid_count * scen_count
    average, totals = call(
        functools.partial(last_kernel, sizes, scale), sizes, (corner_before, corner_after, sums, *factors), lists,
        [jax.ShapeDtypeStruct(value_next.shape, jnp.float32), jax.ShapeDtypeStruct((devices, 1, LANES), jnp.float32)],
        [VMEM, VMEM],
        [
            pltpu.VMEM((outside * sizes.edge_size, LANES), jnp.float32), sums_held, pltpu.VMEM((2 * H, *beyond.shape[1:]), jnp.float32),
            pltpu.SemaphoreType.DMA((7,)),
        ],
        24,
    )
    totals = lax.all_to_all(totals, ("scen", "grid"), 0, 0, tiled=True)
    cells = rows * grid_count * depth * scen_count * width
    return pl.pallas_call(
        functools.partial(mean_kernel, sizes, cells),
        out_shape=jax.ShapeDtypeStruct(value_next.shape, jnp.float32),
        in_specs=[VMEM, VMEM],
        out_specs=HBM,
        scratch_shapes=[pltpu.VMEM(value_next.shape, jnp.float32), pltpu.SemaphoreType.DMA((16,))],
        compiler_params=pltpu.CompilerParams(vmem_limit_bytes=8 * 2**20),
    )(totals, average)


def solution(mesh):
    placed = (P("grid", "scen", None), P("scen"), P(), P(), P())
    return jax.shard_map(
        on_device, mesh=mesh, in_specs=placed, out_specs=P("grid", "scen", None), check_vma=False
    )
```

```python
import functools

import jax
import jax.numpy as jnp
from jax import lax
from jax.experimental import pallas as pl
from jax.experimental.pallas import tpu as pltpu
from jax.sharding import PartitionSpec as P

H = 8
LOW, HIGH = H, 2 * H
SUB, LANES = 8, 128
TILE = 2
CHUNK = 4
FILL = 16
UNROLL = 2
softness = 0.5

ORDER = 0
SHIFT_A, OFFSET, EDGE_OFFSET = range(3)


class Sizes:
    def __init__(self, rows, depth, width, scenarios, releases, grid_count, scen_count):
        self.rows, self.depth, self.width = rows, depth, width
        self.grid_count, self.scen_count = grid_count, scen_count
        self.scenarios, self.releases = scenarios, releases
        self.listed = releases + UNROLL - 1
        self.columns = 1 + 3 * scenarios
        self.far_size = releases + 1 + UNROLL
        self.pieces = [(0, H), (H, rows - 2 * H), (rows - H, H)] if rows > 2 * H else [(0, H), (H, H)] if rows == 2 * H else [(0, rows)]
        self.planes = width // LANES
        self.group = LANES // self.planes
        self.strips = depth // SUB
        self.planes_ext = LOW + self.planes + HIGH
        self.depth_ext = LOW + depth + HIGH
        self.row_size = self.planes_ext * self.depth_ext
        self.pair = scen_count == 2 and depth >= HIGH
        self.edge_strips = HIGH // SUB if self.pair else self.strips
        self.edge_ext = 2 * HIGH if self.pair else self.depth_ext
        self.edge_size = self.planes_ext * self.edge_ext

    def place(self, lane):
        return lane % self.planes * self.group + lane // self.planes

    def lane(self, place):
        return place % self.group * self.planes + place // self.group


def transpose(blocks):
    lane = lax.broadcasted_iota(jnp.int32, (SUB, LANES), 1)
    blocks = [pltpu.roll(block, k, 1) if k else block for k, block in enumerate(blocks)]
    count = len(blocks)
    step = 1
    while step < count:
        odd = (lane // step) % 2 == 1
        blocks = [jnp.where(odd, blocks[(i + step) % count], blocks[i]) for i in range(count)]
        step *= 2
    return [pltpu.roll(blocks[-j % count], LANES - j, 1) if j else blocks[0] for j in range(count)]


def turns(sizes):
    return [*range(-(-(-LOW // sizes.planes)), 0), *range(1, -(-HIGH // sizes.planes) + 1)]


def fill_turns(matrix, sizes):
    shape = (2 * LANES, LANES)
    source = lax.broadcasted_iota(jnp.int32, shape, 0) % LANES
    place = sizes.place(lax.broadcasted_iota(jnp.int32, shape, 1))
    for i, turn in enumerate(turns(sizes)):
        there = jnp.clip(place + turn, 0, LANES - 1)
        matrix[:, i * LANES : i * LANES + LANES] = (sizes.lane(there) == source).astype(jnp.float32).astype(jnp.bfloat16)


def put(weights, sizes, matrix, row_bases, depth_ext, at, rows):
    place = sizes.place(lax.broadcasted_iota(jnp.int32, (SUB, LANES), 1))
    levels = rows[0].shape[1]
    both = jnp.concatenate([row.reshape(sizes.planes * levels, LANES) for row in rows], axis=0)
    upper = both.astype(jnp.bfloat16)
    lower = (both - upper.astype(jnp.float32)).astype(jnp.bfloat16)
    turned = jnp.dot(jnp.concatenate([upper, lower], axis=1), matrix[...], preferred_element_type=jnp.float32)
    for row, row_base in enumerate(row_bases):
        for strip in range(levels // SUB):
            base = row_base + at + strip * SUB

            def part(array, plane):
                first = (row * sizes.planes + plane) * levels + strip * SUB
                return array[first : first + SUB]

            for plane in range(sizes.planes):
                weights[pl.ds(base + (LOW + plane) * depth_ext, SUB), :] = part(both, plane)
            for i, turn in enumerate(turns(sizes)):
                moved = turned[:, i * LANES : i * LANES + LANES]
                end = part(moved, sizes.planes - 1 if turn > 0 else 0)
                past = place + turn > LANES - 1 if turn > 0 else place + turn < 0
                for plane in range(sizes.planes):
                    to = LOW + turn * sizes.planes + plane
                    if 0 <= to < sizes.planes_ext:
                        weights[pl.ds(base + to * depth_ext, SUB), :] = jnp.where(past, end, part(moved, plane))


def put_zeros(weights, sizes, row_base, depth_ext, at, count):
    zero = jnp.zeros((SUB, LANES), jnp.float32)
    for strip in range(count // SUB):
        for plane in range(sizes.planes_ext):
            weights[pl.ds(row_base + plane * depth_ext + at + strip * SUB, SUB), :] = zero


def repeat(weights, sizes, row_base, depth_ext, source, at, count):
    for plane in range(sizes.planes_ext):
        base = row_base + plane * depth_ext
        level = jnp.broadcast_to(weights[pl.ds(base + source, 1), :], (SUB, LANES))
        for strip in range(count // SUB):
            weights[pl.ds(base + at + strip * SUB, SUB), :] = level


def make_lists(sizes, release, inflow, ids, below, table, far):
    first_depth = lax.axis_index("scen") == 0
    inflow_a, inflow_b, inflow_c = ([inflow[i, ids[w][0]] for w in range(sizes.scenarios)] for i in range(3))
    for value in range(H + 2):
        count = jnp.int32(0)
        for r in range(sizes.releases):
            count = count + (release[0, r] < value).astype(jnp.int32)
        below[value] = count
        below[H + 2 + value] = count
    for w in range(sizes.scenarios):
        below[2 * (H + 2) + w] = inflow_a[w]
    for r in range(sizes.releases):
        value = release[0, r]
        to = below[H + 2 + value]
        below[H + 2 + value] = to + 1
        table[sizes.columns * to + ORDER] = r
    for extra in range(sizes.releases, sizes.listed):
        table[sizes.columns * extra + ORDER] = 0

    def step(listed, counts):
        r = table[sizes.columns * listed + ORDER]
        u1, u2, u3 = release[0, r], release[1, r], release[2, r]
        out = []
        for w in range(sizes.scenarios):
            at = sizes.columns * listed + 1 + 3 * w
            plane = LOW + inflow_b[w] + u1 - u2
            shift = inflow_c[w] + u2 - u3
            table[at + SHIFT_A] = inflow_a[w] - u1
            table[at + OFFSET] = plane * sizes.depth_ext + LOW + shift
            far[w * sizes.far_size + 1 + counts[w]] = listed
            reaches = jnp.logical_and(jnp.logical_and(first_depth, shift > SUB), listed < sizes.releases)
            out.append(counts[w] + reaches.astype(jnp.int32))
            if sizes.pair:
                shift = jnp.where(first_depth, jnp.maximum(shift, 0), HIGH + jnp.minimum(shift, 0))
                table[at + EDGE_OFFSET] = plane * sizes.edge_ext + shift
            else:
                table[at + EDGE_OFFSET] = plane * sizes.edge_ext + LOW + shift
        return tuple(out)

    counts = lax.fori_loop(0, sizes.listed, step, tuple(jnp.int32(0) for _ in range(sizes.scenarios)))
    for w in range(sizes.scenarios):
        far[w * sizes.far_size] = counts[w]
        far[w * sizes.far_size + 1 + counts[w]] = sizes.releases


def make_factors(sizes, release, price, table, gains, depths, heights):
    sublane = lax.broadcasted_iota(jnp.int32, (SUB, LANES), 0)
    place = sizes.place(lax.broadcasted_iota(jnp.int32, (SUB, LANES), 1))
    row0, depth0 = lax.axis_index("grid") * sizes.rows, lax.axis_index("scen") * sizes.depth
    spans = (sizes.rows * sizes.grid_count, sizes.width, sizes.depth * sizes.scen_count)
    prices = [price[i] * (1.0 / (spans[i] * H * softness)) for i in range(3)]

    def step(listed, _):
        r = table[sizes.columns * listed + ORDER]
        rate = [prices[i] * release[i, r].astype(jnp.float32) for i in range(3)]
        for plane in range(sizes.planes):
            level = (place * sizes.planes + (plane + 1)).astype(jnp.float32)
            gains[pl.ds(pl.multiple_of((listed * sizes.planes + plane) * SUB, SUB), SUB), :] = jnp.exp(level * rate[1])
        listens = jnp.where(listed < sizes.releases, 1.0, 0.0)
        for refs, start, count, which in ((heights, row0, sizes.rows, 0), (depths, depth0, sizes.depth, 2)):
            for strip in range(count // SUB):
                level = (sublane + (start + strip * SUB + 1)).astype(jnp.float32)
                refs[pl.ds(pl.multiple_of(listed * count + strip * SUB, SUB), SUB), :] = jnp.exp(level * rate[which]) * listens
        return 0

    lax.fori_loop(0, sizes.listed, step, 0)


class Plan:
    def __init__(self, sizes, below, table, far, factors, matrix):
        self.sizes, self.below, self.table, self.far, self.matrix = sizes, below, table, far, matrix
        self.gains, self.depths, self.heights = factors
        grid, scen = lax.axis_index("grid"), lax.axis_index("scen")
        self.first_row, self.last_row = grid == 0, grid == sizes.grid_count - 1
        self.first_depth, self.last_depth = scen == 0, scen == sizes.scen_count - 1
        fill_turns(matrix, sizes)

    def entry(self, scenario, listed, column):
        return self.table[self.sizes.columns * listed + 1 + 3 * scenario + column]

    def edge_first(self):
        if self.sizes.pair:
            return jnp.where(self.first_depth, self.sizes.strips - self.sizes.edge_strips, 0)
        return 0

    def put_rows(self, weights, rows, values):
        sizes = self.sizes
        ext = sizes.depth_ext
        bases = [row * sizes.row_size for row in rows]
        put(weights, sizes, self.matrix, bases, ext, LOW, values)
        for is_end, at, count, edge in (
            (self.first_depth, 0, LOW, LOW),
            (self.last_depth, LOW + sizes.depth, HIGH, LOW + sizes.depth - 1),
        ):

            @pl.when(is_end)
            def _():
                for base in bases:
                    repeat(weights, sizes, base, ext, edge, at, count)

            @pl.when(jnp.logical_not(is_end))
            def _():
                for base in bases:
                    put_zeros(weights, sizes, base, ext, at, count)

    def put_edges(self, weights, rows, beyond):
        sizes = self.sizes
        ext = sizes.edge_ext
        bases = [row * sizes.edge_size for row in rows]
        if sizes.pair:
            put(weights, sizes, self.matrix, bases, ext, jnp.where(self.first_depth, HIGH, 0), beyond)
            for base in bases:
                put_zeros(weights, sizes, base, ext, jnp.where(self.first_depth, 0, HIGH), HIGH)
            return
        for base in bases:
            put_zeros(weights, sizes, base, ext, 0, ext)

        @pl.when(jnp.logical_not(self.first_depth))
        def _():
            put(weights, sizes, self.matrix, bases, ext, 0, [row[:, :LOW] for row in beyond])

        @pl.when(jnp.logical_not(self.last_depth))
        def _():
            put(weights, sizes, self.matrix, bases, ext, LOW + sizes.depth, [row[:, LOW:] for row in beyond])

    def gain(self, listed, plane):
        return self.gains[pl.ds(pl.multiple_of((listed * self.sizes.planes + plane) * SUB, SUB), SUB), :]

    def factors(self, row, first, count, listed):
        height = self.heights[pl.ds(listed * self.sizes.rows + row, 1), :]
        return [
            self.depths[pl.ds(pl.multiple_of(listed * self.sizes.depth + (first + strip) * SUB, SUB), SUB), :] * height
            for strip in range(count)
        ]

    def base(self, edge, scenario, source, first, listed):
        if edge:
            return source * self.sizes.edge_size + self.entry(scenario, listed, EDGE_OFFSET), self.sizes.edge_ext
        return source * self.sizes.row_size + self.entry(scenario, listed, OFFSET) + first * SUB, self.sizes.depth_ext

    def fill_beyond(self, weights, row_size):
        rows = self.sizes.rows
        unroll = 4

        def fill(index, _):
            for k in range(unroll):
                at = pl.multiple_of((index * unroll + k) * SUB, SUB)
                for is_end, to, source in ((self.first_row, 0, 1), (self.last_row, rows + 1, rows)):
                    end = weights[pl.ds(source * row_size + at, SUB), :]
                    weights[pl.ds(to * row_size + at, SUB), :] = end * is_end.astype(jnp.float32)
            return 0

        lax.fori_loop(0, row_size // (SUB * unroll), fill, 0)

    def far_terms(self, sums_ref, edges):
        sizes = self.sizes
        strip = sizes.strips - 2
        together = 2 if sizes.rows % 2 == 0 else 1

        def scenario_terms(scenario, _):
            count = self.far[scenario * sizes.far_size]

            def work(index, _):
                rows = [index * together + i for i in range(together)]

                def step(index, sums):
                    sums = [list(each) for each in sums]
                    for k in range(UNROLL):
                        listed = self.far[scenario * sizes.far_size + 1 + index * UNROLL + k]
                        lands = self.entry(scenario, listed, SHIFT_A) + 1
                        for i, row in enumerate(rows):
                            source = jnp.clip(row + lands, 0, sizes.rows + 1)
                            sums[i] = self.add_release(sums[i], edges, True, scenario, row, strip, 1, listed, source)
                    return tuple(tuple(each) for each in sums)

                sums = tuple(tuple(load_sums(sums_ref, sizes, scenario, row, strip, 1)) for row in rows)
                sums = lax.fori_loop(0, (count + UNROLL - 1) // UNROLL, step, sums)
                for row, each in zip(rows, sums, strict=True):
                    store_sums(sums_ref, sizes, scenario, row, strip, 1, each)
                return 0

            @pl.when(count > 0)
            def _():
                lax.fori_loop(0, sizes.rows // together, work, 0)

            return 0

        lax.fori_loop(0, sizes.scenarios, scenario_terms, 0)

    def own_terms(self, load, store, weights, edge, first, strips, shift=0, chunk=None):
        sizes = self.sizes
        together = 2 if sizes.scenarios % 2 == 0 else 1

        def work(index, _):
            row = index % sizes.rows
            scenarios = [index // sizes.rows * together + i for i in range(together)]

            def find(listed):
                found = []
                for scenario in scenarios:
                    source = jnp.clip(row + 1 + self.entry(scenario, listed, SHIFT_A), 0, sizes.rows + 1)
                    base, ext = self.base(edge, scenario, source, first, listed)
                    found.append((base + shift, ext))
                return found

            def add(sums, from_strip, count, listed, bases):
                factors = self.factors(row, first + from_strip, count, listed)
                for plane in range(sizes.planes):
                    gain = self.gain(listed, plane)
                    for strip in range(count):
                        weight = gain * factors[strip]
                        at = plane * count + strip
                        for i, (base, ext) in enumerate(bases):
                            landed = weights[pl.ds(base + plane * ext + (from_strip + strip) * SUB, SUB), :]
                            sums[i][at] = sums[i][at] + landed * weight

            bases = None if chunk else [find(listed) for listed in range(sizes.releases)]
            for from_strip, count in strip_sets(strips, TILE):
                sums = [load(scenario, row, first + from_strip, count) for scenario in scenarios]
                if chunk:

                    def step(index, sums):
                        sums = [list(each) for each in sums]
                        for k in range(chunk):
                            add(sums, from_strip, count, index * chunk + k, find(index * chunk + k))
                        return tuple(tuple(each) for each in sums)

                    sums = lax.fori_loop(0, sizes.releases // chunk, step, tuple(tuple(each) for each in sums))
                else:
                    for listed in range(sizes.releases):
                        add(sums, from_strip, count, listed, bases[listed])
                for i, scenario in enumerate(scenarios):
                    store(scenario, row, first + from_strip, count, sums[i], from_strip + count == strips)
            return 0

        lax.fori_loop(0, sizes.scenarios // together * sizes.rows, work, 0)

    def add_release(self, sums, weights, edge, scenario, row, first, count, listed, source):
        sizes = self.sizes
        base, ext = self.base(edge, scenario, source, first, listed)
        factors = self.factors(row, first, count, listed)
        out = []
        for plane in range(sizes.planes):
            gain = self.gain(listed, plane)
            for strip in range(count):
                landed = weights[pl.ds(base + plane * ext + strip * SUB, SUB), :]
                out.append(sums[plane * count + strip] + landed * (gain * factors[strip]))
        return out

    def outside_terms(self, sums_ref, weights, edge, first, count, done=None):
        sizes = self.sizes

        def work(index, _):
            scenario, row = index // sizes.rows, index % sizes.rows
            top = row + self.below[2 * (H + 2) + scenario]
            start = jnp.where(self.last_row, 0, self.below[jnp.clip(top - sizes.rows + 1, 0, H + 1)])
            stop = jnp.where(self.first_row, sizes.releases, self.below[jnp.clip(top + 1, 0, H + 1)])

            def some(lo, hi, shift):
                @pl.when(lo < hi)
                def _():
                    def step(index, sums):
                        for k in range(UNROLL):
                            listed = lo + index * UNROLL + k
                            listed = jnp.where(listed < hi, listed, sizes.releases)
                            source = row + self.entry(scenario, listed, SHIFT_A) + shift
                            source = jnp.clip(source, 0, 2 * H - 1)
                            sums = self.add_release(sums, weights, edge, scenario, row, first, count, listed, source)
                        return tuple(sums)

                    sums = tuple(load_sums(sums_ref, sizes, scenario, row, first, count))
                    sums = lax.fori_loop(0, (hi - lo + UNROLL - 1) // UNROLL, step, sums)
                    store_sums(sums_ref, sizes, scenario, row, first, count, sums)

            if sizes.rows >= 2 * H:
                low = row < H
                some(jnp.where(low, stop, 0), jnp.where(low, sizes.releases, start), jnp.where(low, H, H - sizes.rows))
            else:
                some(0, start, H - sizes.rows)
                some(stop, sizes.releases, H)
            if done is not None:
                done(scenario, row)
            return 0

        lax.fori_loop(0, sizes.scenarios * sizes.rows, work, 0)


def load_sums(ref, sizes, scenario, row, first, count):
    return [
        ref[scenario, row, plane, pl.ds(pl.multiple_of((first + strip) * SUB, SUB), SUB), :]
        for plane in range(sizes.planes)
        for strip in range(count)
    ]


def store_sums(ref, sizes, scenario, row, first, count, sums):
    for plane in range(sizes.planes):
        for strip in range(count):
            ref[scenario, row, plane, pl.ds(pl.multiple_of((first + strip) * SUB, SUB), SUB), :] = sums[plane * count + strip]


def strip_sets(strips, most=4):
    return [(first, min(most, strips - first)) for first in range(0, strips, most)]


def fill_rows(count, held, fill):
    together = FILL if count % FILL == 0 else 1

    def step(index, _):
        rows = [together * index + i for i in range(together)]
        fill(rows, [held[row] for row in rows])
        return 0

    lax.fori_loop(0, count // together, step, 0)


def planes_kernel(sizes, values, *refs):
    *outs, sent_sem = refs
    start = pl.multiple_of(jnp.where(lax.axis_index("scen") == 0, sizes.depth - HIGH, 0), SUB) if sizes.pair else None

    def step(out, first, row, _):
        for strip in range(sizes.strips):
            levels = slice(strip * SUB, strip * SUB + SUB)
            blocks = (
                jnp.exp(values[row, levels, block * LANES : block * LANES + LANES] * (-1.0 / softness))
                for block in range(sizes.planes)
            )
            for plane, each in enumerate(transpose(blocks)):
                out[row - first, plane, levels, :] = each
        if sizes.pair:
            pltpu.make_async_copy(out.at[row - first, :, pl.ds(start, HIGH)], outs[-1].at[row], sent_sem).start()
        return 0

    for out, (first, count) in zip(outs, sizes.pieces):
        lax.fori_loop(first, first + count, functools.partial(step, out, first), 0)
    if sizes.pair:
        for out, (first, count) in zip(outs, sizes.pieces):
            pltpu.make_async_copy(out.at[:, :, pl.ds(start, HIGH)], outs[-1].at[pl.ds(first, count)], sent_sem).wait()


def own_kernel(sizes, *refs):
    own, refs = refs[: len(sizes.pieces)], refs[len(sizes.pieces) :]
    release, inflow, price, ids, sums, gains, depths, heights, below, table, far, matrix, *refs = refs
    weights, held, sems = refs
    copies = [
        pltpu.make_async_copy(piece, held.at[pl.ds(first, count)], sems.at[5 + i])
        for i, (piece, (first, count)) in enumerate(zip(own, sizes.pieces, strict=True))
    ]
    for copy in copies:
        copy.start()
    make_lists(sizes, release, inflow, ids, below, table, far)
    factors = gains, depths, heights
    make_factors(sizes, release, price, table, *factors)
    plan = Plan(sizes, below, table, far, factors, matrix)
    for copy in copies:
        copy.wait()
    fill_rows(sizes.rows, held, lambda rows, values: plan.put_rows(weights, [row + 1 for row in rows], values))
    plan.fill_beyond(weights, sizes.row_size)
    zero = jnp.zeros((SUB, LANES), jnp.float32)

    def store(scenario, row, first, count, values, is_last):
        store_sums(sums, sizes, scenario, row, first, count, values)

    chunk = CHUNK if sizes.releases % CHUNK == 0 else None
    plan.own_terms(lambda scenario, row, first, count: [zero] * (sizes.planes * count), store, weights, False, 0, sizes.strips, 0, chunk)


def edge_kernel(
    sizes, beyond, before, after, sums_in, gains, depths, heights, below, table, far, sums, matrix, weights, edges, held,
    rows_held, sems,
):
    copies = [
        pltpu.make_async_copy(beyond, held, sems.at[0]),
        pltpu.make_async_copy(sums_in, sums, sems.at[1]),
        pltpu.make_async_copy(before, rows_held.at[pl.ds(0, H)], sems.at[2]),
        pltpu.make_async_copy(after, rows_held.at[pl.ds(H, H)], sems.at[3]),
    ]
    for copy in copies:
        copy.start()
    plan = Plan(sizes, below, table, far, (gains, depths, heights), matrix)
    copies[0].wait()
    fill_rows(sizes.rows, held, lambda rows, values: plan.put_edges(edges, [row + 1 for row in rows], values))
    plan.fill_beyond(edges, sizes.edge_size)
    copies[1].wait()

    def store(scenario, row, first, count, values, is_last):
        store_sums(sums, sizes, scenario, row, first, count, values)

    load = functools.partial(load_sums, sums, sizes)
    if sizes.pair:
        near = jnp.where(plan.first_depth, sizes.strips - 1, 0)
        shift = jnp.where(plan.first_depth, HIGH - SUB, 0)
        plan.own_terms(load, store, edges, True, near, 1, shift, CHUNK if sizes.releases % CHUNK == 0 else None)
        plan.far_terms(sums, edges)
    else:
        plan.own_terms(load, store, edges, True, 0, sizes.edge_strips)
    copies[2].wait()
    copies[3].wait()
    fill_rows(2 * H, rows_held, functools.partial(plan.put_rows, weights))
    sets = strip_sets(sizes.strips)

    for first, count in sets:
        plan.outside_terms(sums, weights, False, first, count)


def last_kernel(
    sizes, scale, before, after, sums_in, gains, depths, heights, below, table, far, average, totals_out, matrix, edges, sums,
    held, sems,
):
    copies = [
        pltpu.make_async_copy(before, held.at[pl.ds(0, H)], sems.at[0]),
        pltpu.make_async_copy(after, held.at[pl.ds(H, H)], sems.at[1]),
        pltpu.make_async_copy(sums_in, sums, sems.at[2]),
    ]
    for copy in copies:
        copy.start()
    plan = Plan(sizes, below, table, far, (gains, depths, heights), matrix)
    copies[0].wait()
    copies[1].wait()

    fill_rows(2 * H, held, functools.partial(plan.put_edges, edges))
    for copy in copies[2:]:
        copy.wait()
    for first, count in strip_sets(sizes.edge_strips):
        plan.outside_terms(sums, edges, True, plan.edge_first() + first, count)

    def finish(index, total):
        for row in (2 * index, 2 * index + 1):
            for strip in range(sizes.strips):
                levels = slice(strip * SUB, strip * SUB + SUB)
                averages = []
                for plane in range(sizes.planes):
                    logs = None
                    for scenario in range(0, sizes.scenarios, 2):
                        product = sums[scenario, row, plane, levels, :]
                        if scenario + 1 < sizes.scenarios:
                            product = product * sums[scenario + 1, row, plane, levels, :]
                        log = jnp.log(product)
                        logs = log if logs is None else logs + log
                    averages.append(logs * scale)
                    total = total + averages[-1]
                for block, values in enumerate(transpose(averages)):
                    average[row, levels, block * LANES : block * LANES + LANES] = values
        return total

    total = lax.fori_loop(0, sizes.rows // 2, finish, jnp.zeros((SUB, LANES), jnp.float32))
    total = jnp.sum(total, axis=0, keepdims=True)
    totals_out[...] = jnp.broadcast_to(total[None], totals_out.shape)


def mean_kernel(sizes, cells, totals, average, out, held, sems):
    chunks = min(8, sizes.rows)
    step = sizes.rows // chunks
    back = [
        pltpu.make_async_copy(held.at[pl.ds(i * step, step)], out.at[pl.ds(i * step, step)], sems.at[chunks + i]) for i in range(chunks)
    ]
    total = jnp.sum(totals[...], axis=0)
    mean = jnp.sum(total, axis=1, keepdims=True) * (1.0 / cells)
    mean = jnp.broadcast_to(mean, (sizes.depth, sizes.width))
    for i in range(chunks):
        for row in range(i * step, i * step + step):
            held[row] = average[row] - mean
        back[i].start()
    for copy in back:
        copy.wait()


SMEM, VMEM, HBM, ANY = (pl.BlockSpec(memory_space=space) for space in (pltpu.SMEM, pltpu.VMEM, pltpu.HBM, pl.ANY))


def call(kernel, sizes, arrays, scalars, outs, out_specs, scratch, limit=61):
    matrix = pltpu.VMEM((2 * LANES, len(turns(sizes)) * LANES), jnp.bfloat16)
    flat, tree = jax.tree.flatten(scalars)

    def body(*refs):
        ins, refs = refs[: len(arrays)], refs[len(arrays) :]
        scalar_refs, refs = jax.tree.unflatten(tree, refs[: len(flat)]), refs[len(flat) :]
        out_refs, refs = refs[: len(outs)], refs[len(outs) :]
        kernel(*ins, *scalar_refs, *out_refs, *refs)

    return pl.pallas_call(
        body,
        out_shape=outs,
        in_specs=[VMEM if array.ndim == 2 else ANY for array in arrays] + [SMEM] * len(flat),
        out_specs=out_specs,
        scratch_shapes=[matrix, *scratch],
        compiler_params=pltpu.CompilerParams(vmem_limit_bytes=limit * 2**20),
    )(*arrays, *flat)


def from_above(cells, axis, hops=1):
    count = lax.axis_size(axis)
    return lax.ppermute(cells, axis, [(i + hops, i) for i in range(count - hops)])


def from_below(cells, axis, hops=1):
    count = lax.axis_size(axis)
    return lax.ppermute(cells, axis, [(i, i + hops) for i in range(count - hops)])


def beyond_levels(own):
    depth = own.shape[2]
    scen_count, scen = lax.axis_size("scen"), lax.axis_index("scen")
    low, high = [], []
    for hop in range(-(-LOW // depth), 0, -1):
        low.append(from_below(own, "scen", hop) if hop < scen_count else jnp.zeros_like(own))
    for hop in range(1, -(-HIGH // depth) + 1):
        high.append(from_above(own, "scen", hop) if hop < scen_count else jnp.zeros_like(own))
    low = jnp.concatenate(low, axis=2)[:, :, -LOW:]
    high = jnp.concatenate(high, axis=2)[:, :, :HIGH]
    for hop in range(1, -(-HIGH // depth)):
        fill = high[:, :, hop * depth - 1 : hop * depth]
        keep = lax.broadcasted_iota(jnp.int32, high.shape, 2) < hop * depth
        high = jnp.where(jnp.logical_or(scen + hop != scen_count - 1, keep), high, fill)
    return jnp.concatenate([low, high], axis=2)


def on_device(value_next, scenario_ids, inflow_table, release_shifts, price):
    rows, depth, width = value_next.shape
    grid_count, scen_count = lax.axis_size("grid"), lax.axis_size("scen")
    scenarios = scenario_ids.shape[0] * scen_count
    sizes = Sizes(rows, depth, width, scenarios, release_shifts.shape[0], grid_count, scen_count)

    ids = [scenario_ids]
    for hop in range(1, scen_count):
        ids.append(lax.ppermute(scenario_ids, "scen", [(i, (i + hop) % scen_count) for i in range(scen_count)]))
    ids = [each[i : i + 1] for each in ids for i in range(scenario_ids.shape[0])]

    def like(*shape, kind=jnp.float32):
        return jax.ShapeDtypeStruct(shape, kind)

    planes = sizes.planes
    made = [like(count, planes, depth, LANES) for _, count in sizes.pieces]
    if sizes.pair:
        made.append(like(rows, planes, HIGH, LANES))
    made = pl.pallas_call(
        functools.partial(planes_kernel, sizes),
        out_shape=made,
        in_specs=[VMEM],
        out_specs=[VMEM] * len(made),
        scratch_shapes=[pltpu.SemaphoreType.DMA],
        compiler_params=pltpu.CompilerParams(vmem_limit_bytes=12 * 2**20),
    )(value_next)
    made, ids = lax.optimization_barrier((made, ids))
    pieces = made[: len(sizes.pieces)]
    scalars = (release_shifts.T, inflow_table.T, price, ids)
    if sizes.pair:
        beyond = lax.ppermute(made[-1], "scen", [(0, 1), (1, 0)])
    else:
        beyond = beyond_levels(jnp.concatenate(pieces, axis=0))
    before = from_below(pieces[-1][-H:], "grid")
    after = from_above(pieces[0][:H], "grid")

    shape = (scenarios, rows, sizes.planes, depth, LANES)
    sums_shape = jax.ShapeDtypeStruct(shape, jnp.float32)
    sums_held = pltpu.VMEM(shape, jnp.float32)
    inside, outside = rows + 2, 2 * H
    listed = sizes.listed
    factors = [like(listed * planes * SUB, LANES), like(listed * depth, LANES), like(listed * rows, LANES)]
    lists = [2 * (H + 2) + scenarios, listed * sizes.columns, scenarios * sizes.far_size]
    lists = [like(size, kind=jnp.int32) for size in lists]
    sums, *factors = call(
        functools.partial(own_kernel, sizes), sizes, pieces, scalars, [sums_shape, *factors, *lists], [VMEM] * 4 + [SMEM] * 3,
        [
            pltpu.VMEM((inside * sizes.row_size, LANES), jnp.float32), pltpu.VMEM((rows, planes, depth, LANES), jnp.float32),
            pltpu.SemaphoreType.DMA((8,)),
        ],
        28,
    )
    factors, lists = factors[:3], factors[3:]
    beyond, sums = lax.optimization_barrier((beyond, sums))
    corner_before = from_below(beyond[rows - H :], "grid")
    corner_after = from_above(beyond[:H], "grid")
    (sums,) = call(
        functools.partial(edge_kernel, sizes), sizes, (beyond, before, after, sums, *factors), lists, [sums_shape], [VMEM],
        [
            pltpu.VMEM((outside * sizes.row_size, LANES), jnp.float32), pltpu.VMEM((inside * sizes.edge_size, LANES), jnp.float32),
            pltpu.VMEM(beyond.shape, jnp.float32), pltpu.VMEM((2 * H, planes, depth, LANES), jnp.float32),
            pltpu.SemaphoreType.DMA((8,)),
        ],
        44,
    )
    scale = -softness / scenarios
    devices = grid_count * scen_count
    average, totals = call(
        functools.partial(last_kernel, sizes, scale), sizes, (corner_before, corner_after, sums, *factors), lists,
        [jax.ShapeDtypeStruct(value_next.shape, jnp.float32), jax.ShapeDtypeStruct((devices, 1, LANES), jnp.float32)],
        [VMEM, VMEM],
        [
            pltpu.VMEM((outside * sizes.edge_size, LANES), jnp.float32), sums_held, pltpu.VMEM((2 * H, *beyond.shape[1:]), jnp.float32),
            pltpu.SemaphoreType.DMA((7,)),
        ],
        24,
    )
    totals = lax.all_to_all(totals, ("scen", "grid"), 0, 0, tiled=True)
    cells = rows * grid_count * depth * scen_count * width
    return pl.pallas_call(
        functools.partial(mean_kernel, sizes, cells),
        out_shape=jax.ShapeDtypeStruct(value_next.shape, jnp.float32),
        in_specs=[VMEM, VMEM],
        out_specs=HBM,
        scratch_shapes=[pltpu.VMEM(value_next.shape, jnp.float32), pltpu.SemaphoreType.DMA((16,))],
        compiler_params=pltpu.CompilerParams(vmem_limit_bytes=8 * 2**20),
    )(totals, average)


def solution(mesh):
    placed = (P("grid", "scen", None), P("scen"), P(), P(), P())
    return jax.shard_map(
        on_device, mesh=mesh, in_specs=placed, out_specs=P("grid", "scen", None), check_vma=False
    )
```
